32 devices in a mesh: seq: 8 (over z, y), sub: 4 (over x, core).
Axes of the slice: x: 2, y: 2, z: 4, core: 2. Of those that a mesh axis runs over, the one named last changes fastest.
Arguments:
- normed: bfloat16 [4096, 2048], P(('seq', 'sub')), as said below
- w_query: bfloat16 [2048, 2048], P(None, 'sub'), as said below
- w_key: bfloat16 [2048, 2048], P(None, 'sub'), as said below
- w_value: bfloat16 [2048, 2048], P(None, 'sub'), may hold values from -0.125 to 0.125
- w_out: bfloat16 [2048, 2048], P('sub'), may hold values from -0.25 to 0.25
- pattern: int32 [16, 128], P('sub'), may hold values from 0 to 127, each once within a row
- slide_lengths: int32 [8], replicated, may hold values from 1 to 20, 32 in all
Outputs:
- mixed: bfloat16 [4096, 2048], P(('seq', 'sub'))
The draws below stay inside these ranges and needn't reach their ends.
Inputs may be any that keep to these rules, and one draw needn't show every extreme that they name: `pattern`: each row is an ordering of the 128 positions of a block. `slide_lengths`: the slides lie end to end and fill all 32 blocks. `normed`: entries of order one. `w_query`: entries of order 2048 ** -0.5. `w_key`: entries of order 2048 ** -0.5.
All inputs are finite; a program needn't handle non-finite values.
Results may differ from the reference program's by a relative error of at most 0.012.
Values may be sent and summed in bfloat16 or wider, within the bound.
No kernel may reach another device: no remote copies, remote signals or barrier semaphores. Data moves between devices by JAX's collectives and lax.ppermute only.
A program may use at most 128 MiB of HBM per device.

```python
import math
import jax
import jax.numpy as jnp
import numpy as np
from jax import lax

D = 2048
HEAD_COUNT = 16
HEAD_SIZE = 128
BLOCK = 128
DILATED_KEPT = 16
NSLIDE = 8
TOKENS = 4096
SPAN = 512
BLOCK_TOTAL = 32
MOST_SLIDE = 20
N_SEQ = 8


def paired_weights(key):
    base = jax.random.fold_in(key, 11)
    first, second = jax.random.split(base, 2)
    scale = 2.0 / math.sqrt(D)
    shape = (D, HEAD_COUNT * HEAD_SIZE)
    query = jnp.clip(jax.random.normal(first, shape, jnp.float32), -6.0, 6.0) * scale
    keyed = jnp.clip(jax.random.normal(second, shape, jnp.float32), -6.0, 6.0) * scale
    return (query, keyed)


def draw_w_query(key, part):
    return paired_weights(key)[0].astype(jnp.bfloat16)


def draw_w_key(key, part):
    return paired_weights(key)[1].astype(jnp.bfloat16)


def draw_normed(key, part):
    base = jax.random.fold_in(key, 23)
    first = jax.random.fold_in(base, 0)
    values = jnp.clip(jax.random.normal(first, (TOKENS, D), jnp.float32), -6.0, 6.0)
    return values.astype(jnp.bfloat16)


def block_scale(stream_key, dims, pieces, least, top_value):
    def one(dim, blocks):
        heights = jax.random.uniform(jax.random.fold_in(jax.random.fold_in(stream_key, 6), dim), (blocks,), jnp.float32, least / len(pieces), top_value / len(pieces))
        return jnp.repeat(jnp.exp(heights), dims[dim] // blocks).reshape((-1,) + (1,) * (len(dims) - dim - 1))

    factor_of = one(*pieces[0])
    for cut in pieces[1:]:
        factor_of = factor_of * one(*cut)
    return factor_of


def split_up(amount, total, reach, slope):
    weights = [(1 << 20) // math.isqrt(rank ** slope) + 1 for rank in range(2, amount + 1)]
    rest, counts = total - reach - (amount - 1), [1] * (amount - 1)
    while rest > 0:
        candidates = [i for i in range(amount - 1) if counts[i] < reach]
        pool, budget = sum([weights[i] for i in candidates]), rest
        for i in candidates:
            addition = min(reach - counts[i], max(1, budget * weights[i] // pool), rest)
            counts[i] = counts[i] + addition
            rest = rest - addition
    return np.array([reach] + counts)


def uneven_parts(rng, count, total, limit, lean):
    if count == 2:
        one = jax.random.randint(rng, (), max(1, total - limit), min(limit, total - 1) + 1)
        return jnp.stack([one, total - one])
    tallies = jnp.asarray(split_up(count, total, limit, lean), jnp.int32)
    twos = (count - 1) // 2
    source_of, taker = tallies[1:1 + 2 * twos:2], tallies[2:2 + 2 * twos:2]
    slack = jnp.minimum(source_of - 1, limit - taker)
    moved = jax.random.randint(jax.random.fold_in(rng, 1), (twos,), 0, 1 << 20) % (slack + 1)
    tallies = tallies.at[1:1 + 2 * twos:2].set(source_of - moved).at[2:2 + 2 * twos:2].set(taker + moved)
    return tallies[jax.random.permutation(jax.random.fold_in(rng, 2), count)]


def centred(own_key, extent, deviation, reach, cuts=(), kind=jnp.bfloat16):
    entries = deviation * jax.random.normal(own_key, extent, jnp.float32)
    if cuts:
        entries = entries * block_scale(own_key, extent, cuts, -0.22, 0.18)
    return jnp.clip(entries, -reach, reach).astype(kind)


def setup_inputs(seed: int = 0) -> dict:
    keys = jax.random.split(jax.random.key(seed), 8)
    return {
        "normed": draw_normed(jax.random.fold_in(keys[7], 71), 0),
        "w_query": draw_w_query(jax.random.fold_in(keys[7], 71), 0),
        "w_key": draw_w_key(jax.random.fold_in(keys[7], 71), 0),
        "w_value": centred(keys[3], (D, HEAD_COUNT * HEAD_SIZE), D ** -0.5, 0.125, ((1, 4),)),
        "w_out": centred(keys[4], (HEAD_COUNT * HEAD_SIZE, D), (HEAD_COUNT * HEAD_SIZE // 4) ** -0.5, 0.25, ((0, 4),)),
        "pattern": jax.vmap(lambda own: jax.random.permutation(own, BLOCK))(jax.random.split(keys[5], HEAD_COUNT)).reshape((HEAD_COUNT, BLOCK)).astype(jnp.int32),
        "slide_lengths": uneven_parts(keys[6], NSLIDE, BLOCK_TOTAL, MOST_SLIDE, 2).astype(jnp.int32),
    }


def reference(normed, w_query, w_key, w_value, w_out, pattern, slide_lengths):
    queries = jnp.dot(normed, w_query, preferred_element_type=jnp.float32).astype(jnp.bfloat16)
    keys_all = jnp.dot(normed, w_key, preferred_element_type=jnp.float32).astype(jnp.bfloat16)
    values_all = jnp.dot(normed, w_value, preferred_element_type=jnp.float32).astype(jnp.bfloat16)
    span_of_blocks = SPAN // BLOCK
    slide_ends = jnp.cumsum(slide_lengths).astype(jnp.int32)
    block_ids = jnp.arange(BLOCK_TOTAL, dtype=jnp.int32)
    slide_per_block = lax.optimization_barrier(jnp.sum((block_ids[:, None] >= slide_ends[None, :]).astype(jnp.int32), axis=1))
    kept_positions = pattern[:, :DILATED_KEPT].astype(jnp.int32)

    def dilate(source):
        by_head = jnp.moveaxis(source.reshape(BLOCK_TOTAL, BLOCK, HEAD_COUNT, HEAD_SIZE), 2, 0)
        selected_keys = jax.vmap(lambda rows, where_at: rows[:, where_at, :])(by_head, kept_positions)
        return selected_keys.reshape(HEAD_COUNT, BLOCK_TOTAL * DILATED_KEPT, HEAD_SIZE)
    far_keys = dilate(keys_all).astype(jnp.float32)
    far_values = dilate(values_all).astype(jnp.float32)
    distant_block = jnp.arange(BLOCK_TOTAL * DILATED_KEPT, dtype=jnp.int32) // DILATED_KEPT
    distant_slide = jnp.repeat(slide_per_block, DILATED_KEPT)
    far_span = distant_block // span_of_blocks
    row_slide = jnp.repeat(slide_per_block, BLOCK).reshape(N_SEQ, SPAN)

    def by_span(source):
        return jnp.transpose(source.reshape(N_SEQ, SPAN, HEAD_COUNT, HEAD_SIZE), (0, 2, 1, 3))
    scale = 1.0 / math.sqrt(HEAD_SIZE)

    def one_span(item):
        query_s, key_s, value_s, slide_s, span_id = item
        query_f = query_s.astype(jnp.float32)
        near = jnp.einsum('hqd,hkd->hqk', query_f, key_s.astype(jnp.float32)) * scale
        far = jnp.einsum('hqd,hkd->hqk', query_f, far_keys) * scale
        near_mask = slide_s[:, None] == slide_s[None, :]
        far_mask = (slide_s[:, None] == distant_slide[None, :]) & (far_span != span_id)[None, :]
        near = jnp.where(near_mask[None], near, -1e+30)
        far = jnp.where(far_mask[None], far, -1e+30)
        peak = jnp.maximum(lax.optimization_barrier(jnp.max(near, axis=2, keepdims=True)), lax.optimization_barrier(jnp.max(far, axis=2, keepdims=True)))
        near_exp = jnp.exp(near - peak)
        far_exp = jnp.exp(far - peak)
        total = lax.optimization_barrier(jnp.sum(near_exp, axis=2, keepdims=True)) + lax.optimization_barrier(jnp.sum(far_exp, axis=2, keepdims=True))
        near_w = (near_exp / total).astype(jnp.bfloat16).astype(jnp.float32)
        far_w = (far_exp / total).astype(jnp.bfloat16).astype(jnp.float32)
        context = jnp.einsum('hqk,hkd->hqd', near_w, value_s.astype(jnp.float32))
        context = context + jnp.einsum('hqk,hkd->hqd', far_w, far_values)
        return jnp.transpose(context.astype(jnp.bfloat16), (1, 0, 2)).reshape(SPAN, HEAD_COUNT * HEAD_SIZE)
    span_ids = jnp.arange(N_SEQ, dtype=jnp.int32)
    context = lax.map(one_span, (by_span(queries), by_span(keys_all), by_span(values_all), row_slide, span_ids))
    context = context.reshape(TOKENS, HEAD_COUNT * HEAD_SIZE)
    return jnp.dot(context, w_out, preferred_element_type=jnp.float32).astype(jnp.bfloat16)
```

```python
import functools
import math

import jax
import jax.numpy as jnp
from jax import lax
from jax.experimental import pallas as pl
from jax.experimental.pallas import tpu as pltpu
from jax.sharding import PartitionSpec as P

HEAD_SIZE = 128
BLOCK = 128
DILATED_KEPT = 16
BLOCKS_HALF = 2
FAR_ROWS = BLOCKS_HALF * DILATED_KEPT
HIDDEN = -1e30
SCALE = math.log2(math.e) / math.sqrt(HEAD_SIZE)
BF16 = jnp.bfloat16
F32 = jnp.float32


def dot(a, b):
    return jnp.dot(a, b, preferred_element_type=F32)


def dot_t(a, b):
    return lax.dot_general(a, b, (((1,), (1,)), ((), ())), preferred_element_type=F32)


def params(vmem_mib=40):
    return pltpu.CompilerParams(vmem_limit_bytes=vmem_mib * 2**20)


def project_kernel(weight_count, dilated, *refs):
    first, second = refs[0], refs[1]
    weights = refs[2 : 2 + weight_count]
    rest = refs[2 + weight_count :]
    rows = jnp.concatenate([first[...], second[...]], axis=0)
    outs = rest[1:] if dilated else rest
    results = []
    for index in range(weight_count):
        result = dot(rows, weights[index][...]).astype(BF16)
        outs[index][...] = result
        results.append(result)
    if not dilated:
        return
    pattern, kept = rest[0], outs[weight_count]
    keys, values = results[0], results[1]
    heads = keys.shape[1] // HEAD_SIZE
    base = pl.program_id(0) * heads
    positions = lax.broadcasted_iota(jnp.int32, (BLOCK, BLOCK), 0)
    for head in range(heads):
        row = pattern[pl.ds(base + head, 1), :]
        chosen = (positions == row).astype(F32).T[:DILATED_KEPT].astype(BF16)
        columns = slice(head * HEAD_SIZE, (head + 1) * HEAD_SIZE)
        for block in range(BLOCKS_HALF):
            where = slice(block * BLOCK, (block + 1) * BLOCK)
            pair = jnp.concatenate([keys[where, columns], values[where, columns]], axis=1)
            picked = dot(chosen, pair).astype(BF16)
            spot = slice(block * DILATED_KEPT, (block + 1) * DILATED_KEPT)
            kept[0, head, spot, :] = picked[:, :HEAD_SIZE]
            kept[1, head, spot, :] = picked[:, HEAD_SIZE:]


def project(first, second, weights, pattern=None):
    depth, width = weights[0].shape
    tile = min(256, width)
    heads = tile // HEAD_SIZE
    rows = first.shape[0] + second.shape[0]
    whole = pl.BlockSpec((first.shape[0], depth), lambda i: (0, 0))
    in_specs = [whole, whole]
    in_specs += [pl.BlockSpec((depth, tile), lambda i: (0, i)) for _ in weights]
    operands = [first, second, *weights]
    out_shape = [jax.ShapeDtypeStruct((rows, width), BF16) for _ in weights]
    out_specs = [pl.BlockSpec((rows, tile), lambda i: (0, i)) for _ in weights]
    if pattern is not None:
        in_specs.append(pl.BlockSpec(pattern.shape, lambda i: (0, 0)))
        operands.append(pattern)
        out_shape.append(
            jax.ShapeDtypeStruct((2, width // HEAD_SIZE, FAR_ROWS, HEAD_SIZE), BF16)
        )
        out_specs.append(pl.BlockSpec((2, heads, FAR_ROWS, HEAD_SIZE), lambda i: (0, i, 0, 0)))
    count = len(weights)
    return pl.pallas_call(
        functools.partial(project_kernel, count, pattern is not None),
        grid=(width // tile,),
        in_specs=in_specs,
        out_specs=out_specs,
        out_shape=out_shape,
        compiler_params=params(),
        cost_estimate=pl.CostEstimate(
            flops=2 * rows * depth * width * count,
            bytes_accessed=2 * count * depth * width,
            transcendentals=0,
        ),
    )(*operands)


def slide_of(place, slides, block):
    end, total = jnp.int32(0), jnp.zeros_like(block)
    for index in range(slides):
        end = end + place[index]
        total = total + (block >= end).astype(jnp.int32)
    return total


def hidden_if(condition):
    return jnp.where(condition, jnp.float32(0), jnp.float32(HIDDEN))


def my_block(place, slides, subs, relative):
    return place[slides] * subs + (place[slides + 1] ^ relative)


def far_bias(place, slides, subs, sources, blocks, row_slides):
    column = lax.broadcasted_iota(jnp.int32, (1, len(sources) * FAR_ROWS), 1)
    span = jnp.zeros_like(column)
    for index, source in enumerate(sources):
        span = jnp.where(column // FAR_ROWS == index, source, span)
    upper = (column // DILATED_KEPT) % BLOCKS_HALF
    me = place[slides + 1]
    block = span * subs + jnp.where(upper == 0, me ^ blocks[0], me ^ blocks[1])
    slide = slide_of(place, slides, block)
    elsewhere = span != place[slides]
    return [hidden_if((slide == mine) & elsewhere) for mine in row_slides]


def far_update(query, pieces, bias, state):
    keys = jnp.concatenate([piece[0] for piece in pieces], axis=0)
    values = jnp.concatenate([piece[1] for piece in pieces], axis=0)
    scores = dot_t(query, keys)
    scores = jnp.concatenate(
        [scores[i * BLOCK : (i + 1) * BLOCK] + bias[i] for i in range(len(bias))], axis=0
    )
    peak, total, gathered = state
    higher = jnp.maximum(peak, jnp.max(scores, axis=1, keepdims=True))
    shrink = jnp.exp2((peak - higher) * SCALE)
    weight = jnp.exp2((scores - higher) * SCALE)
    total = total * shrink + jnp.sum(weight, axis=1, keepdims=True)
    gathered = gathered * shrink + dot(weight.astype(BF16), values)
    return higher, total, gathered


def near_kernel(slides, subs, sources_of, far_count, place, *refs):
    query_parts, key_parts, value_parts = refs[0:2], refs[2:4], refs[4:6]
    far = refs[6 : 6 + far_count]
    gathered_out, stats_out = refs[6 + far_count :]
    query = jnp.concatenate([part[...] for part in query_parts], axis=0)
    keys = jnp.concatenate([part[...] for part in key_parts], axis=0)
    values = jnp.concatenate([part[...] for part in value_parts], axis=0)
    mine = [slide_of(place, slides, my_block(place, slides, subs, r)) for r in range(subs)]
    scores = dot_t(query, keys)
    rows = []
    for r in range(subs):
        bias = jnp.concatenate(
            [jnp.full((1, BLOCK), hidden_if(mine[r] == mine[c]), F32) for c in range(subs)], axis=1
        )
        rows.append(scores[r * BLOCK : (r + 1) * BLOCK] + bias)
    scores = jnp.concatenate(rows, axis=0)
    peak = jnp.max(scores, axis=1, keepdims=True)
    weight = jnp.exp2((scores - peak) * SCALE)
    total = jnp.sum(weight, axis=1, keepdims=True)
    state = peak, total, dot(weight.astype(BF16), values)
    if far_count:
        bias = far_bias(place, slides, subs, sources_of(place[slides]), (0, 1), mine)
        state = far_update(query, [piece[:, 0] for piece in far], bias, state)
    peak, total, gathered = state
    gathered_out[...] = gathered
    lane = lax.broadcasted_iota(jnp.int32, gathered.shape, 1)
    stats_out[0] = jnp.where(lane == 0, peak, total)


def far_kernel(slides, subs, sources_of, halves, relative, place, *refs):
    query = refs[0][...]
    gathered, stats = refs[1][...], refs[2][0]
    keep, send = refs[-2:]
    state = stats[:, 0:1], stats[:, 1:2], gathered
    mine = [slide_of(place, slides, my_block(place, slides, subs, r)) for r in relative]
    sources = sources_of(place[slides])
    start = 3
    for blocks in halves:
        if sources is None:
            pieces = refs[start]
            start += 1
            group = 8
            spans = pieces.shape[0]

            def step(index, state, pieces=pieces, blocks=blocks):
                base = index * group
                bias = far_bias(
                    place, slides, subs, [base + i for i in range(group)], blocks, mine
                )
                return far_update(query, [pieces[base + i][:, 0] for i in range(group)], bias, state)

            state = lax.fori_loop(0, spans // group, step, state)
        else:
            pieces = refs[start : start + len(sources)]
            start += len(sources)
            bias = far_bias(place, slides, subs, sources, blocks, mine)
            state = far_update(query, [piece[:, 0] for piece in pieces], bias, state)
    _, total, gathered = state
    context = (gathered / total).astype(BF16)
    keep[...] = context[:BLOCK]
    send[...] = context[BLOCK:]


def far_spec(piece):
    if piece.ndim == 4:
        return pl.BlockSpec((2, 1, FAR_ROWS, HEAD_SIZE), lambda h, place: (0, h, 0, 0))
    return pl.BlockSpec(
        (piece.shape[0], 2, 1, FAR_ROWS, HEAD_SIZE), lambda h, place: (0, 0, h, 0, 0)
    )


def near_attention(place, slides, subs, sources_of, queries, keys, values, far):
    half, width = queries[0].shape
    span = 2 * half
    heads = width // HEAD_SIZE
    part = pl.BlockSpec((half, HEAD_SIZE), lambda h, place: (0, h))
    columns = span + FAR_ROWS * len(far)
    return pl.pallas_call(
        functools.partial(near_kernel, slides, subs, sources_of, len(far)),
        grid_spec=pltpu.PrefetchScalarGridSpec(
            num_scalar_prefetch=1,
            grid=(heads,),
            in_specs=[part] * 6 + [far_spec(piece) for piece in far],
            out_specs=[
                pl.BlockSpec((span, HEAD_SIZE), lambda h, place: (0, h)),
                pl.BlockSpec((1, span, HEAD_SIZE), lambda h, place: (h, 0, 0)),
            ],
        ),
        out_shape=[
            jax.ShapeDtypeStruct((span, width), F32),
            jax.ShapeDtypeStruct((heads, span, HEAD_SIZE), F32),
        ],
        compiler_params=params(),
        cost_estimate=pl.CostEstimate(
            flops=4 * span * columns * width,
            bytes_accessed=6 * half * width * 2,
            transcendentals=heads * span * columns,
        ),
    )(place, *queries, *keys, *values, *far)


def far_attention(place, slides, subs, sources_of, relative, query, gathered, stats, halves):
    half, width = query.shape
    heads = width // HEAD_SIZE
    row = relative[0] // BLOCKS_HALF
    far = [piece for _, pieces in halves for piece in pieces]
    count = sum(1 if piece.ndim == 4 else piece.shape[0] for piece in far)
    result = pl.BlockSpec((BLOCK, HEAD_SIZE), lambda h, place: (0, h))
    return pl.pallas_call(
        functools.partial(
            far_kernel, slides, subs, sources_of, [blocks for blocks, _ in halves], relative
        ),
        grid_spec=pltpu.PrefetchScalarGridSpec(
            num_scalar_prefetch=1,
            grid=(heads,),
            in_specs=[
                pl.BlockSpec((half, HEAD_SIZE), lambda h, place: (0, h)),
                pl.BlockSpec((half, HEAD_SIZE), lambda h, place: (row, h)),
                pl.BlockSpec((1, half, HEAD_SIZE), lambda h, place: (h, row, 0)),
            ]
            + [far_spec(piece) for piece in far],
            out_specs=[result, result],
        ),
        out_shape=[jax.ShapeDtypeStruct((BLOCK, width), BF16)] * 2,
        compiler_params=params(),
        cost_estimate=pl.CostEstimate(
            flops=4 * half * FAR_ROWS * count * width,
            bytes_accessed=8 * half * width,
            transcendentals=heads * half * FAR_ROWS * count,
        ),
    )(place, query, gathered, stats, *far)


def mix_kernel(first, second, weight_first, weight_second, out):
    total = dot(first[...], weight_first[...]) + dot(second[...], weight_second[...])
    out[...] = total.astype(out.dtype)


def mix(first, second, weight_first, weight_second, dtype):
    rows, depth = first.shape
    width = weight_first.shape[1]
    tile = min(512, width)
    left = pl.BlockSpec((rows, depth), lambda i: (0, 0))
    right = pl.BlockSpec((depth, tile), lambda i: (0, i))
    return pl.pallas_call(
        mix_kernel,
        grid=(width // tile,),
        in_specs=[left, left, right, right],
        out_specs=pl.BlockSpec((rows, tile), lambda i: (0, i)),
        out_shape=jax.ShapeDtypeStruct((rows, width), dtype),
        compiler_params=params(),
        cost_estimate=pl.CostEstimate(
            flops=4 * rows * depth * width, bytes_accessed=4 * depth * width, transcendentals=0
        ),
    )(first, second, weight_first, weight_second)


def shards(seqs, subs, normed, w_query, w_key, w_value, w_out, pattern, slide_lengths):
    slides = slide_lengths.shape[0]
    place = jnp.concatenate(
        [
            slide_lengths,
            lax.axis_index("seq").astype(jnp.int32)[None],
            lax.axis_index("sub").astype(jnp.int32)[None],
        ]
    )

    def swap(array, bit):
        return lax.ppermute(array, "sub", [(i, i ^ bit) for i in range(subs)])

    across = swap(normed, 2)
    beside = swap(normed, 1)
    few = seqs == 8
    if few:
        moves = [(z, y) for z in range(4) for y in range(2) if (z, y) != (0, 0)]

        def sources_of(me):
            return [((me // 2 - z) % 4) * 2 + (me % 2 ^ y) for z, y in moves]

        def spread(kept):
            return [
                lax.ppermute(
                    kept,
                    "seq",
                    [(i, ((i // 2 + z) % 4) * 2 + (i % 2 ^ y)) for i in range(seqs)],
                )
                for z, y in moves
            ]

    else:

        def sources_of(me):
            return None

        def spread(kept):
            return [lax.all_gather(kept, "seq", axis=0)]

    keys_a, values_a, query_a, kept_a = project(
        normed, beside, [w_key, w_value, w_query], pattern
    )
    far_a = spread(kept_a)
    across_beside = swap(across, 1)
    w_out_beside = swap(lax.optimization_barrier((w_out, beside))[0], 1)
    keys_b, values_b, kept_b = project(across, across_beside, [w_key, w_value], pattern)
    far_b = spread(kept_b)
    (query_b,) = project(across, across_beside, [w_query])
    attend = (place, slides, subs, sources_of)
    gathered, stats = near_attention(
        *attend,
        (query_a, query_b),
        (keys_a, keys_b),
        (values_a, values_b),
        far_a if few else [],
    )
    halves = [((2, 3), far_b)] if few else [((0, 1), far_a), ((2, 3), far_b)]
    keep_b, send_b = far_attention(*attend, (2, 3), query_b, gathered, stats, halves)
    other_b = swap(send_b, 1)
    leaving = mix(keep_b, other_b, w_out, w_out_beside, BF16)
    arriving = swap(leaving, 2)
    keep_a, send_a = far_attention(*attend, (0, 1), query_a, gathered, stats, halves)
    other_a = swap(send_a, 1)
    own = mix(keep_a, other_a, w_out, w_out_beside, F32)
    return (own + arriving.astype(F32)).astype(BF16)


def solution(mesh):
    placed = (
        P(("seq", "sub"), None),
        P(None, "sub"),
        P(None, "sub"),
        P(None, "sub"),
        P("sub", None),
        P("sub", None),
        P(),
    )
    return jax.shard_map(
        functools.partial(shards, mesh.shape["seq"], mesh.shape["sub"]),
        mesh=mesh,
        in_specs=placed,
        out_specs=P(("seq", "sub"), None),
        check_vma=False,
    )
```

```python
import functools
import math

import jax
import jax.numpy as jnp
from jax import lax
from jax.experimental import pallas as pl
from jax.experimental.pallas import tpu as pltpu
from jax.sharding import PartitionSpec as P

HEAD_SIZE = 128
BLOCK = 128
DILATED_KEPT = 16
BLOCKS_HALF = 2
FAR_ROWS = BLOCKS_HALF * DILATED_KEPT
GROUP = 8
HIDDEN = -1e30
SCALE = math.log2(math.e) / math.sqrt(HEAD_SIZE)
BF16 = jnp.bfloat16
F32 = jnp.float32
IN_VMEM = pl.BlockSpec(memory_space=pltpu.VMEM)
IN_HBM = pl.BlockSpec(memory_space=pltpu.HBM)
IN_SMEM = pl.BlockSpec(memory_space=pltpu.SMEM)
KEY_BITS = (1, 4, 2)
VALUE_BITS = (4, 2, 1)


def dot(a, b):
    return jnp.dot(a, b, preferred_element_type=F32)


def dot_t(a, b):
    return lax.dot_general(a, b, (((1,), (1,)), ((), ())), preferred_element_type=F32)


def params():
    return pltpu.CompilerParams(vmem_limit_bytes=40 * 2**20)


def cost(flops, bytes_accessed, transcendentals=0):
    return pl.CostEstimate(
        flops=flops, bytes_accessed=bytes_accessed, transcendentals=transcendentals
    )


def shape(dims, dtype=BF16):
    return jax.ShapeDtypeStruct(tuple(dims), dtype)


def keep_in_hbm(array):
    return pltpu.with_memory_space_constraint(array, pltpu.HBM)


def halves_of(width):
    tile = min(256, width)
    return [slice(i * tile, (i + 1) * tile) for i in range(width // tile)]


def pick_dilated(pattern, blocks, kept_keys, kept_values):
    positions = lax.broadcasted_iota(jnp.int32, (BLOCK, BLOCK), 0)
    for head in range(kept_keys.shape[0]):
        row = pattern[head : head + 1, :]
        chosen = (positions == row).astype(F32).T[:DILATED_KEPT].astype(BF16)
        for index, block in enumerate(blocks):
            picked = dot(chosen, jnp.concatenate(block(head), axis=1)).astype(BF16)
            spot = slice(index * DILATED_KEPT, (index + 1) * DILATED_KEPT)
            kept_keys[head, spot, :] = picked[:, :HEAD_SIZE]
            kept_values[head, spot, :] = picked[:, HEAD_SIZE:]


def head_of(ref, head, rows=slice(None)):
    return ref[rows, head * HEAD_SIZE : (head + 1) * HEAD_SIZE]


def first_kernel(rows_hbm, wk_hbm, wv_hbm, rows, wk, wv, keys, values, sems):
    parts = halves_of(wk.shape[1])
    whole = pltpu.make_async_copy(rows_hbm, rows, sems.at[0])
    whole.start()
    copies = []
    for index, part in enumerate(parts):
        for side, (source, target) in enumerate(((wk_hbm, wk), (wv_hbm, wv))):
            copy = pltpu.make_async_copy(
                source.at[:, part], target.at[:, part], sems.at[1 + 2 * index + side]
            )
            copy.start()
            copies.append((copy, target, part, (keys, values)[side]))
    whole.wait()
    for copy, weight, part, out in copies:
        copy.wait()
        out[:, part] = dot(rows[...], weight[:, part]).astype(BF16)


def first(rows, w_key, w_value):
    count, depth = rows.shape
    width = w_key.shape[1]
    return pl.pallas_call(
        first_kernel,
        in_specs=[IN_HBM] * 3,
        out_specs=[IN_VMEM] * 5,
        out_shape=[
            pltpu.VMEM(rows.shape, BF16),
            pltpu.VMEM(w_key.shape, BF16),
            pltpu.VMEM(w_value.shape, BF16),
            shape((count, width)),
            shape((count, width)),
        ],
        scratch_shapes=[pltpu.SemaphoreType.DMA((1 + 2 * len(halves_of(width)),))],
        compiler_params=params(),
        cost_estimate=cost(4 * count * depth * width, 4 * depth * width),
    )(keep_in_hbm(rows), keep_in_hbm(w_key), keep_in_hbm(w_value))


def second_kernel(
    rows, wk, wv, keys_0, values_0, pattern, wq_hbm, wq, keys, values, kept_k, kept_v, sem
):
    copy = pltpu.make_async_copy(wq_hbm, wq, sem)
    copy.start()
    for part in halves_of(wk.shape[1]):
        keys[:, part] = dot(rows[...], wk[:, part]).astype(BF16)
        values[:, part] = dot(rows[...], wv[:, part]).astype(BF16)
    blocks = [
        lambda head: (head_of(keys_0, head), head_of(values_0, head)),
        lambda head: (head_of(keys, head), head_of(values, head)),
    ]
    pick_dilated(pattern, blocks, kept_k, kept_v)
    copy.wait()


def second(rows, wk, wv, keys_0, values_0, pattern, w_query):
    count, depth = rows.shape
    width = wk.shape[1]
    kept = (width // HEAD_SIZE, FAR_ROWS, HEAD_SIZE)
    return pl.pallas_call(
        second_kernel,
        in_specs=[IN_VMEM] * 6 + [IN_HBM],
        out_specs=[IN_VMEM] * 5,
        out_shape=[
            pltpu.VMEM(w_query.shape, BF16),
            shape((count, width)),
            shape((count, width)),
            shape(kept),
            shape(kept),
        ],
        scratch_shapes=[pltpu.SemaphoreType.DMA],
        compiler_params=params(),
        cost_estimate=cost(4 * count * depth * width, 2 * depth * width),
    )(rows, wk, wv, keys_0, values_0, pattern, keep_in_hbm(w_query))


def query_kernel(carry, *refs):
    rows_0, rows_1, wq = refs[:3]
    if carry:
        w_hbm, queries, w, sem = refs[3:]
        copy = pltpu.make_async_copy(w_hbm, w, sem)
        copy.start()
    else:
        queries = refs[3]
    rows = jnp.concatenate([rows_0[...], rows_1[...]], axis=0)
    for part in halves_of(wq.shape[1]):
        queries[:, part] = dot(rows, wq[:, part]).astype(BF16)
    if carry:
        copy.wait()


def query(rows_0, rows_1, wq, carried=None):
    count, depth = rows_0.shape
    width = wq.shape[1]
    carry = carried is not None
    return pl.pallas_call(
        functools.partial(query_kernel, carry),
        in_specs=[IN_VMEM] * 3 + [IN_HBM] * carry,
        out_specs=[IN_VMEM] * (1 + carry),
        out_shape=[shape((2 * count, width))]
        + ([pltpu.VMEM(carried.shape, BF16)] if carry else []),
        scratch_shapes=[pltpu.SemaphoreType.DMA] * carry,
        compiler_params=params(),
        cost_estimate=cost(4 * count * depth * width, 2 * depth * width * carry),
    )(rows_0, rows_1, wq, *([keep_in_hbm(carried)] if carry else []))


def third_kernel(rows_0, rows_1, wk, wv, pattern, keys, values, kept_k, kept_v):
    rows = jnp.concatenate([rows_0[...], rows_1[...]], axis=0)
    for part in halves_of(wk.shape[1]):
        keys[:, part] = dot(rows, wk[:, part]).astype(BF16)
        values[:, part] = dot(rows, wv[:, part]).astype(BF16)

    def block(where):
        return lambda head: (head_of(keys, head, where), head_of(values, head, where))

    blocks = [block(slice(i * BLOCK, (i + 1) * BLOCK)) for i in range(BLOCKS_HALF)]
    pick_dilated(pattern, blocks, kept_k, kept_v)


def third(rows_0, rows_1, wk, wv, pattern):
    count, depth = rows_0.shape
    width = wk.shape[1]
    kept = (width // HEAD_SIZE, FAR_ROWS, HEAD_SIZE)
    return pl.pallas_call(
        third_kernel,
        in_specs=[IN_VMEM] * 5,
        out_specs=[IN_VMEM] * 4,
        out_shape=[shape((2 * count, width))] * 2 + [shape(kept)] * 2,
        compiler_params=params(),
        cost_estimate=cost(8 * count * depth * width, 4 * count * depth),
    )(rows_0, rows_1, wk, wv, pattern)


def slide_of(place, slides, block):
    end, total = jnp.int32(0), jnp.zeros_like(block)
    for index in range(slides):
        end = end + place[index]
        total = total + (block >= end).astype(jnp.int32)
    return total


def hidden_if_not(condition):
    return jnp.where(condition, jnp.float32(0), jnp.float32(HIDDEN))


def far_bias(place, slides, subs, span_of, blocks, row_slides):
    column = lax.broadcasted_iota(jnp.int32, (1, GROUP * FAR_ROWS), 1)
    span = span_of(column // FAR_ROWS)
    upper = (column // DILATED_KEPT) % BLOCKS_HALF
    me = place[slides + 1]
    block = span * subs + jnp.where(upper == 0, me ^ blocks[0], me ^ blocks[1])
    slide = slide_of(place, slides, block)
    elsewhere = span != place[slides]
    return [hidden_if_not((slide == mine) & elsewhere) for mine in row_slides]


def add_rows(scores, bias):
    return jnp.concatenate(
        [scores[i * BLOCK : (i + 1) * BLOCK] + row for i, row in enumerate(bias)], axis=0
    )


def far_update(queries, keys, values, bias, state):
    scores = add_rows(dot_t(queries, keys), bias)
    peak, total, gathered = state
    higher = jnp.maximum(peak, jnp.max(scores, axis=1, keepdims=True))
    shrink = jnp.exp2((peak - higher) * SCALE)
    weight = jnp.exp2((scores - higher) * SCALE)
    total = total * shrink + jnp.sum(weight, axis=1, keepdims=True)
    return higher, total, gathered * shrink + dot(weight.astype(BF16), values)


def far_group(keys, values, head):
    found = []
    for refs, bits in ((keys, KEY_BITS), (values, VALUE_BITS)):
        order = [0]
        for bit in bits:
            order += [place ^ bit for place in order]
        half = len(order) // 2
        found.append(
            jnp.concatenate(
                [
                    refs[order.index(i) // half][order.index(i) % half, head]
                    for i in range(len(order))
                ],
                axis=0,
            )
        )
    return found


def attend_kernel(slides, subs, relative, near, halves, few, finish, place, *refs):
    refs = list(refs)
    queries = refs.pop(0)
    if near:
        keys, values = refs[0:3], refs[3:6]
        del refs[:6]
    else:
        gathered_in, stats_in = refs[0:2]
        del refs[:2]
    far = []
    for blocks in halves:
        size = 2 if few else 1
        far.append((blocks, refs[:size], refs[size : 2 * size]))
        del refs[: 2 * size]
    sub = place[slides + 1]
    slide = [
        slide_of(place, slides, place[slides] * subs + (sub ^ r)) for r in range(subs)
    ]
    mine = [slide[r] for r in relative]
    if near:
        near_bias = [
            jnp.concatenate(
                [
                    jnp.full((1, BLOCK), hidden_if_not(slide[r] == slide[c]), F32)
                    for c in range(subs)
                ],
                axis=1,
            )
            for r in relative
        ]
    if few:
        biases = [
            far_bias(place, slides, subs, lambda i: place[slides] ^ i, blocks, mine)
            for blocks, _, _ in far
        ]
    for head in range(queries.shape[1] // HEAD_SIZE):
        asked = head_of(queries, head)
        if near:
            near_keys = jnp.concatenate([head_of(ref, head) for ref in keys], axis=0)
            near_values = jnp.concatenate([head_of(ref, head) for ref in values], axis=0)
            scores = add_rows(dot_t(asked, near_keys), near_bias)
            peak = jnp.max(scores, axis=1, keepdims=True)
            weight = jnp.exp2((scores - peak) * SCALE)
            total = jnp.sum(weight, axis=1, keepdims=True)
            state = peak, total, dot(weight.astype(BF16), near_values)
        else:
            state = stats_in[head, :, 0:1], stats_in[head, :, 1:2], head_of(gathered_in, head)
        for index, (blocks, far_keys, far_values) in enumerate(far):
            if few:
                group = far_group(far_keys, far_values, head)
                state = far_update(asked, *group, biases[index], state)
                continue

            def step(number, state, blocks=blocks, k=far_keys[0], v=far_values[0]):
                base = number * GROUP
                bias = far_bias(place, slides, subs, lambda i: base + i, blocks, mine)
                group = [
                    jnp.concatenate([ref[base + i, head] for i in range(GROUP)], axis=0)
                    for ref in (k, v)
                ]
                return far_update(asked, *group, bias, state)

            state = lax.fori_loop(0, far_keys[0].shape[0] // GROUP, step, state)
        peak, total, gathered = state
        columns = slice(head * HEAD_SIZE, (head + 1) * HEAD_SIZE)
        if finish:
            keep, send = refs
            context = (gathered / total).astype(BF16)
            keep[:, columns] = context[:BLOCK]
            send[:, columns] = context[BLOCK:]
        else:
            gathered_out, stats_out = refs
            gathered_out[:, columns] = gathered
            lane = lax.broadcasted_iota(jnp.int32, gathered.shape, 1)
            stats_out[head] = jnp.where(lane == 0, peak, total)


def attend(place, slides, subs, few, relative, queries, halves, near=None, begun=None, finish=True):
    rows, width = queries.shape
    heads = width // HEAD_SIZE
    operands = [queries]
    operands += [*near[0], *near[1]] if near else list(begun)
    columns = subs * BLOCK if near else 0
    for _, keys, values in halves:
        operands += [*keys, *values]
        columns += sum(part.shape[0] for part in keys) * FAR_ROWS
    if finish:
        out_shape = [shape((BLOCK, width))] * 2
    else:
        out_shape = [shape((rows, width), F32), shape((heads, rows, HEAD_SIZE), F32)]
    return pl.pallas_call(
        functools.partial(
            attend_kernel,
            slides,
            subs,
            relative,
            near is not None,
            [half[0] for half in halves],
            few,
            finish,
        ),
        in_specs=[IN_SMEM] + [IN_VMEM] * len(operands),
        out_specs=[IN_VMEM] * 2,
        out_shape=out_shape,
        compiler_params=params(),
        cost_estimate=cost(
            4 * rows * columns * width, 4 * rows * width, heads * rows * columns
        ),
    )(place, *operands)


def mix_kernel(rows_0, rows_1, weight_0, weight_1, out):
    tile = min(512, out.shape[1])
    for index in range(out.shape[1] // tile):
        part = slice(index * tile, (index + 1) * tile)
        total = dot(rows_0[...], weight_0[:, part]) + dot(rows_1[...], weight_1[:, part])
        out[:, part] = total.astype(out.dtype)


def mix(rows_0, rows_1, weight_0, weight_1, dtype):
    rows, depth = rows_0.shape
    width = weight_0.shape[1]
    return pl.pallas_call(
        mix_kernel,
        in_specs=[IN_VMEM] * 4,
        out_specs=IN_VMEM,
        out_shape=shape((rows, width), dtype),
        compiler_params=params(),
        cost_estimate=cost(4 * rows * depth * width, 4 * rows * width),
    )(rows_0, rows_1, weight_0, weight_1)


def shards(seqs, subs, normed, w_query, w_key, w_value, w_out, pattern, slide_lengths):
    slides = slide_lengths.shape[0]
    place = jnp.concatenate(
        [
            slide_lengths,
            lax.axis_index("seq").astype(jnp.int32)[None],
            lax.axis_index("sub").astype(jnp.int32)[None],
        ]
    )
    few = seqs == GROUP

    def swap(array, bit, axis="sub"):
        count = subs if axis == "sub" else seqs
        return lax.ppermute(array, axis, [(i, i ^ bit) for i in range(count)])

    def after(array, *others):
        return lax.optimization_barrier((array, *others))[0]

    def double(parts, bit):
        return jnp.concatenate([parts, swap(parts, bit, "seq")], axis=0)

    def spread(kept, start, middle):
        if not few:
            return [[lax.all_gather(part, "seq", axis=0)] for part in kept]
        (key_1, key_2, key_3), (value_1, value_2, value_3) = KEY_BITS, VALUE_BITS
        k, v = start(double(kept[0][None], key_1), double(kept[1][None], value_1))
        k, v = middle(double(k, key_2), double(v, value_2))
        return [k, swap(k, key_3, "seq")], [v, swap(v, value_3, "seq")]

    across = swap(normed, 2)
    beside = swap(normed, 1)
    mine, wk, wv, keys_0, values_0 = first(normed, w_key, w_value)
    wq, keys_1, values_1, *kept = second(beside, wk, wv, keys_0, values_0, pattern, w_query)
    query_a, wo = query(mine, beside, wq, w_out)
    held = [across]

    def before_across(k, v):
        *held[:], k, v, _ = lax.optimization_barrier((*held, k, v, query_a))
        return k, v

    half_a = (0, 1), *spread(kept, lambda k, v: (k, v), before_across)
    across = held[0]
    across_beside = swap(across, 1)
    wo_beside = swap(after(w_out, across_beside), 1)
    keys_2, values_2, *kept = third(across, across_beside, wk, wv, pattern)
    near = [keys_0, keys_1, keys_2], [values_0, values_1, values_2]
    call = functools.partial(attend, place, slides, subs, few)
    (query_b,) = query(across, across_beside, wq)
    begun = call((2, 3), query_b, [half_a], near=near, finish=False)
    half_b = (2, 3), *spread(
        kept,
        lambda k, v: lax.optimization_barrier((k, v, query_b))[:2],
        lambda k, v: lax.optimization_barrier((k, v, *begun))[:2],
    )
    keep_b, send_b = call((2, 3), query_b, [half_b], begun=begun)
    other_b = swap(send_b, 1)
    leaving = mix(keep_b, other_b, wo, wo_beside, BF16)
    arriving = swap(leaving, 2)
    query_a = after(query_a, leaving)
    keep_a, send_a = call((0, 1), query_a, [half_a, half_b], near=near)
    other_a = swap(send_a, 1)
    own = mix(keep_a, other_a, wo, wo_beside, F32)
    return (own + arriving.astype(F32)).astype(BF16)


def solution(mesh):
    placed = (
        P(("seq", "sub"), None),
        P(None, "sub"),
        P(None, "sub"),
        P(None, "sub"),
        P("sub", None),
        P("sub", None),
        P(),
    )
    return jax.shard_map(
        functools.partial(shards, mesh.shape["seq"], mesh.shape["sub"]),
        mesh=mesh,
        in_specs=placed,
        out_specs=P(("seq", "sub"), None),
        check_vma=False,
    )
```

```python
import functools
import math

import jax
import jax.numpy as jnp
from jax import lax
from jax.experimental import pallas as pl
from jax.experimental.pallas import tpu as pltpu
from jax.sharding import PartitionSpec as P

HEAD_SIZE = 128
BLOCK = 128
DILATED_KEPT = 16
BLOCKS_HALF = 2
FAR_ROWS = BLOCKS_HALF * DILATED_KEPT
GROUP = 8
HIDDEN = -1e30
SCALE = math.log2(math.e) / math.sqrt(HEAD_SIZE)
BF16 = jnp.bfloat16
F32 = jnp.float32
IN_VMEM = pl.BlockSpec(memory_space=pltpu.VMEM)
IN_HBM = pl.BlockSpec(memory_space=pltpu.HBM)
IN_SMEM = pl.BlockSpec(memory_space=pltpu.SMEM)
KEY_BITS = (1, 4, 2)
VALUE_BITS = (4, 2, 1)


def dot(a, b):
    return jnp.dot(a, b, preferred_element_type=F32)


def dot_t(a, b):
    return lax.dot_general(a, b, (((1,), (1,)), ((), ())), preferred_element_type=F32)


def params(extra=0):
    return pltpu.CompilerParams(vmem_limit_bytes=16 * 2**20 + extra)


def cost(flops, bytes_accessed, transcendentals=0):
    return pl.CostEstimate(
        flops=flops, bytes_accessed=bytes_accessed, transcendentals=transcendentals
    )


def shape(dims, dtype=BF16):
    return jax.ShapeDtypeStruct(tuple(dims), dtype)


def keep_in_hbm(array):
    return pltpu.with_memory_space_constraint(array, pltpu.HBM)


def halves_of(width):
    tile = min(256, width)
    return [slice(i * tile, (i + 1) * tile) for i in range(width // tile)]


def pick_dilated(pattern, blocks, kept_keys, kept_values):
    positions = lax.broadcasted_iota(jnp.int32, (BLOCK, BLOCK), 0)
    for head in range(kept_keys.shape[0]):
        row = pattern[head : head + 1, :]
        chosen = (positions == row).astype(F32).T[:DILATED_KEPT].astype(BF16)
        for index, block in enumerate(blocks):
            picked = dot(chosen, jnp.concatenate(block(head), axis=1)).astype(BF16)
            spot = slice(index * DILATED_KEPT, (index + 1) * DILATED_KEPT)
            kept_keys[head, spot, :] = picked[:, :HEAD_SIZE]
            kept_values[head, spot, :] = picked[:, HEAD_SIZE:]


def head_of(ref, head, rows=slice(None)):
    return ref[rows, head * HEAD_SIZE : (head + 1) * HEAD_SIZE]


def first_kernel(rows_hbm, wk_hbm, wv_hbm, rows, wk, wv, keys, values, sems):
    parts = halves_of(wk.shape[1])
    whole = pltpu.make_async_copy(rows_hbm, rows, sems.at[0])
    whole.start()
    copies = []
    for index, part in enumerate(parts):
        for side, (source, target) in enumerate(((wk_hbm, wk), (wv_hbm, wv))):
            copy = pltpu.make_async_copy(
                source.at[:, part], target.at[:, part], sems.at[1 + 2 * index + side]
            )
            copy.start()
            copies.append((copy, target, part, (keys, values)[side]))
    whole.wait()
    for copy, weight, part, out in copies:
        copy.wait()
        out[:, part] = dot(rows[...], weight[:, part]).astype(BF16)


def first(rows, w_key, w_value):
    count, depth = rows.shape
    width = w_key.shape[1]
    return pl.pallas_call(
        first_kernel,
        in_specs=[IN_HBM] * 3,
        out_specs=[IN_VMEM] * 5,
        out_shape=[
            pltpu.VMEM(rows.shape, BF16),
            pltpu.VMEM(w_key.shape, BF16),
            pltpu.VMEM(w_value.shape, BF16),
            shape((count, width)),
            shape((count, width)),
        ],
        scratch_shapes=[pltpu.SemaphoreType.DMA((1 + 2 * len(halves_of(width)),))],
        compiler_params=params(),
        cost_estimate=cost(4 * count * depth * width, 4 * depth * width),
    )(keep_in_hbm(rows), keep_in_hbm(w_key), keep_in_hbm(w_value))


def second_kernel(rows, wk, wv, keys_0, values_0, pattern, keys, values, kept_k, kept_v):
    for part in halves_of(wk.shape[1]):
        keys[:, part] = dot(rows[...], wk[:, part]).astype(BF16)
        values[:, part] = dot(rows[...], wv[:, part]).astype(BF16)
    blocks = [
        lambda head: (head_of(keys_0, head), head_of(values_0, head)),
        lambda head: (head_of(keys, head), head_of(values, head)),
    ]
    pick_dilated(pattern, blocks, kept_k, kept_v)


def second(rows, wk, wv, keys_0, values_0, pattern):
    count, depth = rows.shape
    width = wk.shape[1]
    kept = (width // HEAD_SIZE, FAR_ROWS, HEAD_SIZE)
    return pl.pallas_call(
        second_kernel,
        in_specs=[IN_VMEM] * 6,
        out_specs=[IN_VMEM] * 4,
        out_shape=[shape((count, width))] * 2 + [shape(kept)] * 2,
        compiler_params=params(),
        cost_estimate=cost(4 * count * depth * width, 2 * count * depth),
    )(rows, wk, wv, keys_0, values_0, pattern)


def query_first_kernel(rows_0, rows_1, wq_hbm, w_hbm, queries, wq, w, sems):
    parts = halves_of(wq.shape[1])
    copies = [
        pltpu.make_async_copy(wq_hbm.at[:, part], wq.at[:, part], sems.at[index])
        for index, part in enumerate(parts)
    ]
    copies.append(pltpu.make_async_copy(w_hbm, w, sems.at[len(parts)]))
    for copy in copies:
        copy.start()
    rows = jnp.concatenate([rows_0[...], rows_1[...]], axis=0)
    for part, copy in zip(parts, copies):
        copy.wait()
        queries[:, part] = dot(rows, wq[:, part]).astype(BF16)
    copies[-1].wait()


def query_first(rows_0, rows_1, w_query, w_out):
    count, depth = rows_0.shape
    width = w_query.shape[1]
    return pl.pallas_call(
        query_first_kernel,
        in_specs=[IN_VMEM] * 2 + [IN_HBM] * 2,
        out_specs=[IN_VMEM] * 3,
        out_shape=[
            shape((2 * count, width)),
            pltpu.VMEM(w_query.shape, BF16),
            pltpu.VMEM(w_out.shape, BF16),
        ],
        scratch_shapes=[pltpu.SemaphoreType.DMA((1 + len(halves_of(width)),))],
        compiler_params=params(),
        cost_estimate=cost(4 * count * depth * width, 4 * depth * width),
    )(rows_0, rows_1, keep_in_hbm(w_query), keep_in_hbm(w_out))


def query_kernel(rows_0, rows_1, wq, queries):
    rows = jnp.concatenate([rows_0[...], rows_1[...]], axis=0)
    for part in halves_of(wq.shape[1]):
        queries[:, part] = dot(rows, wq[:, part]).astype(BF16)


def query(rows_0, rows_1, wq):
    count, depth = rows_0.shape
    width = wq.shape[1]
    return pl.pallas_call(
        query_kernel,
        in_specs=[IN_VMEM] * 3,
        out_specs=IN_VMEM,
        out_shape=shape((2 * count, width)),
        compiler_params=params(),
        cost_estimate=cost(4 * count * depth * width, 4 * count * depth),
    )(rows_0, rows_1, wq)


def third_kernel(rows_0, rows_1, wk, wv, pattern, keys, values, kept_k, kept_v):
    rows = jnp.concatenate([rows_0[...], rows_1[...]], axis=0)
    for part in halves_of(wk.shape[1]):
        keys[:, part] = dot(rows, wk[:, part]).astype(BF16)
        values[:, part] = dot(rows, wv[:, part]).astype(BF16)

    def block(where):
        return lambda head: (head_of(keys, head, where), head_of(values, head, where))

    blocks = [block(slice(i * BLOCK, (i + 1) * BLOCK)) for i in range(BLOCKS_HALF)]
    pick_dilated(pattern, blocks, kept_k, kept_v)


def third(rows_0, rows_1, wk, wv, pattern):
    count, depth = rows_0.shape
    width = wk.shape[1]
    kept = (width // HEAD_SIZE, FAR_ROWS, HEAD_SIZE)
    return pl.pallas_call(
        third_kernel,
        in_specs=[IN_VMEM] * 5,
        out_specs=[IN_VMEM] * 4,
        out_shape=[shape((2 * count, width))] * 2 + [shape(kept)] * 2,
        compiler_params=params(),
        cost_estimate=cost(8 * count * depth * width, 4 * count * depth),
    )(rows_0, rows_1, wk, wv, pattern)


def slide_of(place, slides, block):
    end, total = jnp.int32(0), jnp.zeros_like(block)
    for index in range(slides):
        end = end + place[index]
        total = total + (block >= end).astype(jnp.int32)
    return total


def hidden_if_not(condition):
    return jnp.where(condition, jnp.float32(0), jnp.float32(HIDDEN))


def bias_kernel(slides, subs, spans, few, place, out):
    span, sub = place[slides], place[slides + 1]
    slide = [slide_of(place, slides, span * subs + (sub ^ r)) for r in range(subs)]
    for r in range(subs):
        for c in range(subs):
            value = hidden_if_not(slide[r] == slide[c])
            out[r : r + 1, c * BLOCK : (c + 1) * BLOCK] = jnp.full((1, BLOCK), value, F32)
    count = spans * FAR_ROWS
    column = lax.broadcasted_iota(jnp.int32, (1, count), 1)
    far = column // FAR_ROWS
    if few:
        far = far ^ span
    upper = (column // DILATED_KEPT) % BLOCKS_HALF
    for half in range(subs // BLOCKS_HALF):
        place_0, place_1 = sub ^ (half * BLOCKS_HALF), sub ^ (half * BLOCKS_HALF + 1)
        theirs = slide_of(place, slides, far * subs + jnp.where(upper == 0, place_0, place_1))
        start = subs * BLOCK + half * count
        for r in range(subs):
            seen = (theirs == slide[r]) & (far != span)
            out[r : r + 1, start : start + count] = hidden_if_not(seen)


def make_bias(place, slides, subs, spans, few):
    columns = subs * BLOCK + subs // BLOCKS_HALF * spans * FAR_ROWS
    return pl.pallas_call(
        functools.partial(bias_kernel, slides, subs, spans, few),
        in_specs=[IN_SMEM],
        out_specs=IN_VMEM,
        out_shape=shape((subs, columns), F32),
        compiler_params=params(),
        cost_estimate=cost(64 * subs * columns, 4 * subs * columns),
    )(place)


def add_rows(scores, bias):
    return jnp.concatenate(
        [scores[i * BLOCK : (i + 1) * BLOCK] + row for i, row in enumerate(bias)], axis=0
    )


def far_update(queries, keys, values, bias, state):
    scores = add_rows(dot_t(queries, keys), bias)
    peak, total, gathered = state
    higher = jnp.maximum(peak, jnp.max(scores, axis=1, keepdims=True))
    shrink = jnp.exp2((peak - higher) * SCALE)
    weight = jnp.exp2((scores - higher) * SCALE)
    total = total * shrink + jnp.sum(weight, axis=1, keepdims=True)
    return higher, total, gathered * shrink + dot(weight.astype(BF16), values)


def far_group(keys, values, head):
    found = []
    for refs, bits in ((keys, KEY_BITS), (values, VALUE_BITS)):
        order = [0]
        for bit in bits:
            order += [place ^ bit for place in order]
        half = len(order) // 2
        found.append(
            jnp.concatenate(
                [
                    refs[order.index(i) // half][order.index(i) % half, head]
                    for i in range(len(order))
                ],
                axis=0,
            )
        )
    return found


def attend_kernel(relative, near, halves, few, finish, bias, *refs):
    refs = list(refs)
    queries = refs.pop(0)
    if near:
        keys, values = refs[0:3], refs[3:6]
        del refs[:6]
    else:
        gathered_in, stats_in = refs[0:2]
        del refs[:2]
    far = []
    for half in halves:
        size = 2 if few else 1
        far.append((half, refs[:size], refs[size : 2 * size]))
        del refs[: 2 * size]
    span = bias.shape[0] * BLOCK
    half_count = (bias.shape[1] - span) * BLOCKS_HALF // bias.shape[0]

    def rows_of_bias(columns):
        return [bias[r : r + 1, columns] for r in relative]

    def one_head(head, _):
        columns = pl.ds(pl.multiple_of(head * HEAD_SIZE, HEAD_SIZE), HEAD_SIZE)
        asked = queries[:, columns]
        if near:
            near_keys = jnp.concatenate([ref[:, columns] for ref in keys], axis=0)
            near_values = jnp.concatenate([ref[:, columns] for ref in values], axis=0)
            scores = add_rows(dot_t(asked, near_keys), rows_of_bias(slice(0, span)))
            peak = jnp.max(scores, axis=1, keepdims=True)
            weight = jnp.exp2((scores - peak) * SCALE)
            total = jnp.sum(weight, axis=1, keepdims=True)
            state = peak, total, dot(weight.astype(BF16), near_values)
        else:
            state = stats_in[head, :, 0:1], stats_in[head, :, 1:2], gathered_in[:, columns]
        for half, far_keys, far_values in far:
            start = span + half * half_count
            if few:
                group = far_group(far_keys, far_values, head)
                rows = rows_of_bias(slice(start, start + half_count))
                state = far_update(asked, *group, rows, state)
                continue

            def step(number, state, start=start, k=far_keys[0], v=far_values[0]):
                base = number * GROUP
                group = [
                    jnp.concatenate([ref[base + i, head] for i in range(GROUP)], axis=0)
                    for ref in (k, v)
                ]
                width = GROUP * FAR_ROWS
                rows = rows_of_bias(pl.ds(pl.multiple_of(start + number * width, width), width))
                return far_update(asked, *group, rows, state)

            state = lax.fori_loop(0, far_keys[0].shape[0] // GROUP, step, state)
        peak, total, gathered = state
        if finish:
            keep, send = refs
            context = (gathered / total).astype(BF16)
            keep[:, columns] = context[:BLOCK]
            send[:, columns] = context[BLOCK:]
        else:
            gathered_out, stats_out = refs
            gathered_out[:, columns] = gathered
            lane = lax.broadcasted_iota(jnp.int32, gathered.shape, 1)
            stats_out[head] = jnp.where(lane == 0, peak, total)
        return 0

    lax.fori_loop(0, queries.shape[1] // HEAD_SIZE, one_head, 0)


def attend(bias, few, relative, queries, halves, near=None, begun=None, finish=True):
    rows, width = queries.shape
    heads = width // HEAD_SIZE
    operands = [queries]
    operands += [*near[0], *near[1]] if near else list(begun)
    columns = bias.shape[0] * BLOCK if near else 0
    spans = 0
    for _, keys, values in halves:
        operands += [*keys, *values]
        spans += sum(part.shape[0] for part in keys)
    columns += spans * FAR_ROWS
    if finish:
        out_shape = [shape((BLOCK, width))] * 2
    else:
        out_shape = [shape((rows, width), F32), shape((heads, rows, HEAD_SIZE), F32)]
    far_bytes = 4 * spans * FAR_ROWS * width
    return pl.pallas_call(
        functools.partial(
            attend_kernel, relative, near is not None, [half[0] for half in halves], few, finish
        ),
        in_specs=[IN_VMEM] * (1 + len(operands)),
        out_specs=[IN_VMEM] * 2,
        out_shape=out_shape,
        compiler_params=params(far_bytes),
        cost_estimate=cost(
            4 * rows * columns * width, 4 * rows * width, heads * rows * columns
        ),
    )(bias, *operands)


def mix_kernel(rows_0, rows_1, weight_0, weight_1, out):
    tile = min(512, out.shape[1])
    for index in range(out.shape[1] // tile):
        part = slice(index * tile, (index + 1) * tile)
        total = dot(rows_0[...], weight_0[:, part]) + dot(rows_1[...], weight_1[:, part])
        out[:, part] = total.astype(out.dtype)


def mix(rows_0, rows_1, weight_0, weight_1, dtype):
    rows, depth = rows_0.shape
    width = weight_0.shape[1]
    return pl.pallas_call(
        mix_kernel,
        in_specs=[IN_VMEM] * 4,
        out_specs=IN_VMEM,
        out_shape=shape((rows, width), dtype),
        compiler_params=params(),
        cost_estimate=cost(4 * rows * depth * width, 4 * rows * width),
    )(rows_0, rows_1, weight_0, weight_1)


def shards(seqs, subs, normed, w_query, w_key, w_value, w_out, pattern, slide_lengths):
    slides = slide_lengths.shape[0]
    place = jnp.concatenate(
        [
            slide_lengths,
            lax.axis_index("seq").astype(jnp.int32)[None],
            lax.axis_index("sub").astype(jnp.int32)[None],
        ]
    )
    few = seqs == GROUP

    def swap(array, bit, axis="sub"):
        count = subs if axis == "sub" else seqs
        return lax.ppermute(array, axis, [(i, i ^ bit) for i in range(count)])

    def after(array, *others):
        return lax.optimization_barrier((array, *others))[0]

    def spread(kept, start, middle):
        if not few:
            return [[lax.all_gather(part, "seq", axis=0)] for part in kept]
        k, v = kept[0][None], kept[1][None]
        for key_bit, value_bit, hook in zip(KEY_BITS, VALUE_BITS, (start, middle)):
            came = hook(swap(k, key_bit, "seq"), swap(v, value_bit, "seq"))
            k, v = jnp.concatenate([k, came[0]], axis=0), jnp.concatenate([v, came[1]], axis=0)
        return [k, swap(k, KEY_BITS[-1], "seq")], [v, swap(v, VALUE_BITS[-1], "seq")]

    across = swap(normed, 2)
    beside = swap(normed, 1)
    mine, wk, wv, keys_0, values_0 = first(normed, w_key, w_value)
    keys_1, values_1, *kept_a = second(beside, wk, wv, keys_0, values_0, pattern)
    query_a, wq, wo = query_first(mine, beside, w_query, w_out)
    bias = make_bias(place, slides, subs, seqs, few)
    held = [across, query_a, bias]

    def before_across(k, v):
        *held[:], k, v = lax.optimization_barrier((*held, k, v))
        return k, v

    def after_third(k, v):
        across, query_a, bias = held
        beyond = swap(across, 1)
        keys_2, values_2, *kept_b = third(across, beyond, wk, wv, pattern)
        kept_b[0], kept_b[1], k, v = lax.optimization_barrier((*kept_b, k, v))
        held[:] = across, beyond, query_a, bias, keys_2, values_2, kept_b
        return k, v

    def same(k, v):
        return k, v

    if not few:
        after_third(across, across)
    half_a = 0, *spread(kept_a, before_across, after_third)
    across, beyond, query_a, bias, keys_2, values_2, kept_b = held
    wo_beside = swap(after(w_out, kept_b[0]), 1)
    wo_beside = pltpu.with_memory_space_constraint(wo_beside, pltpu.VMEM)
    query_b = query(across, beyond, wq)
    half_b = 1, *spread(kept_b, same, same)
    near = [keys_0, keys_1, keys_2], [values_0, values_1, values_2]
    call = functools.partial(attend, bias, few)
    asked = after(query_b, half_b[1][0], half_b[2][0])
    begun = call((2, 3), asked, [half_a], near=near, finish=False)
    keep_b, send_b = call((2, 3), query_b, [half_b], begun=begun)
    other_b = swap(send_b, 1)
    leaving = mix(keep_b, other_b, wo, wo_beside, BF16)
    arriving = swap(leaving, 2)
    query_a = after(query_a, leaving)
    keep_a, send_a = call((0, 1), query_a, [half_a, half_b], near=near)
    other_a = swap(send_a, 1)
    own = mix(keep_a, other_a, wo, wo_beside, F32)
    return (own + arriving.astype(F32)).astype(BF16)


def solution(mesh):
    placed = (
        P(("seq", "sub"), None),
        P(None, "sub"),
        P(None, "sub"),
        P(None, "sub"),
        P("sub", None),
        P("sub", None),
        P(),
    )
    return jax.shard_map(
        functools.partial(shards, mesh.shape["seq"], mesh.shape["sub"]),
        mesh=mesh,
        in_specs=placed,
        out_specs=P(("seq", "sub"), None),
        check_vma=False,
    )
```

```python
import functools
import math

import jax
import jax.numpy as jnp
from jax import lax
from jax.experimental import pallas as pl
from jax.experimental.pallas import tpu as pltpu
from jax.sharding import PartitionSpec as P

HEAD_SIZE = 128
BLOCK = 128
DILATED_KEPT = 16
BLOCKS_HALF = 2
FAR_ROWS = BLOCKS_HALF * DILATED_KEPT
GROUP = 8
HIDDEN = -1e30
SCALE = math.log2(math.e) / math.sqrt(HEAD_SIZE)
BF16 = jnp.bfloat16
F32 = jnp.float32
IN_VMEM = pl.BlockSpec(memory_space=pltpu.VMEM)
IN_HBM = pl.BlockSpec(memory_space=pltpu.HBM)
IN_SMEM = pl.BlockSpec(memory_space=pltpu.SMEM)
BOTH_BITS = (4, 2, 1)
KEY_BITS = (4, 1, 2)
VALUE_BITS = (2, 4, 1)


def dot(a, b):
    return jnp.dot(a, b, preferred_element_type=F32)


def dot_t(a, b):
    return lax.dot_general(a, b, (((1,), (1,)), ((), ())), preferred_element_type=F32)


def params(extra=0):
    return pltpu.CompilerParams(vmem_limit_bytes=16 * 2**20 + extra)


def cost(flops, bytes_accessed, transcendentals=0):
    return pl.CostEstimate(
        flops=flops, bytes_accessed=bytes_accessed, transcendentals=transcendentals
    )


def shape(dims, dtype=BF16):
    return jax.ShapeDtypeStruct(tuple(dims), dtype)


def keep_in_hbm(array):
    return pltpu.with_memory_space_constraint(array, pltpu.HBM)


def halves_of(width):
    tile = min(256, width)
    return [slice(i * tile, (i + 1) * tile) for i in range(width // tile)]


def pick_dilated(pattern, blocks, kept):
    (keys, key_slot), (values, value_slot) = kept
    positions = lax.broadcasted_iota(jnp.int32, (BLOCK, BLOCK), 0)
    for head in range(keys.shape[1]):
        row = pattern[head : head + 1, :]
        chosen = (positions == row).astype(F32).T[:DILATED_KEPT].astype(BF16)
        for index, block in enumerate(blocks):
            picked = dot(chosen, jnp.concatenate(block(head), axis=1)).astype(BF16)
            spot = slice(index * DILATED_KEPT, (index + 1) * DILATED_KEPT)
            keys[key_slot, head, spot, :] = picked[:, :HEAD_SIZE]
            values[value_slot, head, spot, :] = picked[:, HEAD_SIZE:]


def head_of(ref, head, rows=slice(None)):
    return ref[rows, head * HEAD_SIZE : (head + 1) * HEAD_SIZE]


def first_kernel(rows_hbm, wk_hbm, wv_hbm, rows, wk, wv, keys, values, sems):
    parts = halves_of(wk.shape[1])
    whole = pltpu.make_async_copy(rows_hbm, rows, sems.at[0])
    whole.start()
    copies = []
    for index, part in enumerate(parts):
        for side, (source, target) in enumerate(((wk_hbm, wk), (wv_hbm, wv))):
            copy = pltpu.make_async_copy(
                source.at[:, part], target.at[:, part], sems.at[1 + 2 * index + side]
            )
            copy.start()
            copies.append((copy, target, part, (keys, values)[side]))
    whole.wait()
    for copy, weight, part, out in copies:
        copy.wait()
        out[:, part] = dot(rows[...], weight[:, part]).astype(BF16)


def first(rows, w_key, w_value):
    count, depth = rows.shape
    width = w_key.shape[1]
    return pl.pallas_call(
        first_kernel,
        in_specs=[IN_HBM] * 3,
        out_specs=[IN_VMEM] * 5,
        out_shape=[
            pltpu.VMEM(rows.shape, BF16),
            pltpu.VMEM(w_key.shape, BF16),
            pltpu.VMEM(w_value.shape, BF16),
            shape((count, width)),
            shape((count, width)),
        ],
        scratch_shapes=[pltpu.SemaphoreType.DMA((1 + 2 * len(halves_of(width)),))],
        compiler_params=params(),
        cost_estimate=cost(4 * count * depth * width, 4 * depth * width),
    )(keep_in_hbm(rows), keep_in_hbm(w_key), keep_in_hbm(w_value))


def second_kernel(rows, wk, wv, keys_0, values_0, pattern, keys, values, kept):
    for part in halves_of(wk.shape[1]):
        keys[:, part] = dot(rows[...], wk[:, part]).astype(BF16)
        values[:, part] = dot(rows[...], wv[:, part]).astype(BF16)
    blocks = [
        lambda head: (head_of(keys_0, head), head_of(values_0, head)),
        lambda head: (head_of(keys, head), head_of(values, head)),
    ]
    pick_dilated(pattern, blocks, ((kept, 0), (kept, 1)))


def second(rows, wk, wv, keys_0, values_0, pattern):
    count, depth = rows.shape
    width = wk.shape[1]
    kept = (2, width // HEAD_SIZE, FAR_ROWS, HEAD_SIZE)
    return pl.pallas_call(
        second_kernel,
        in_specs=[IN_VMEM] * 6,
        out_specs=[IN_VMEM] * 3,
        out_shape=[shape((count, width))] * 2 + [shape(kept)],
        compiler_params=params(),
        cost_estimate=cost(4 * count * depth * width, 2 * count * depth),
    )(rows, wk, wv, keys_0, values_0, pattern)


def query_first_kernel(rows_0, rows_1, wq_hbm, w_hbm, queries, wq, w, sems):
    parts = halves_of(wq.shape[1])
    copies = [
        pltpu.make_async_copy(wq_hbm.at[:, part], wq.at[:, part], sems.at[index])
        for index, part in enumerate(parts)
    ]
    copies.append(pltpu.make_async_copy(w_hbm, w, sems.at[len(parts)]))
    for copy in copies:
        copy.start()
    rows = jnp.concatenate([rows_0[...], rows_1[...]], axis=0)
    for part, copy in zip(parts, copies):
        copy.wait()
        queries[:, part] = dot(rows, wq[:, part]).astype(BF16)
    copies[-1].wait()


def query_first(rows_0, rows_1, w_query, w_out):
    count, depth = rows_0.shape
    width = w_query.shape[1]
    return pl.pallas_call(
        query_first_kernel,
        in_specs=[IN_VMEM] * 2 + [IN_HBM] * 2,
        out_specs=[IN_VMEM] * 3,
        out_shape=[
            shape((2 * count, width)),
            pltpu.VMEM(w_query.shape, BF16),
            pltpu.VMEM(w_out.shape, BF16),
        ],
        scratch_shapes=[pltpu.SemaphoreType.DMA((1 + len(halves_of(width)),))],
        compiler_params=params(),
        cost_estimate=cost(4 * count * depth * width, 4 * depth * width),
    )(rows_0, rows_1, keep_in_hbm(w_query), keep_in_hbm(w_out))


def query_kernel(rows_0, rows_1, wq, queries):
    rows = jnp.concatenate([rows_0[...], rows_1[...]], axis=0)
    for part in halves_of(wq.shape[1]):
        queries[:, part] = dot(rows, wq[:, part]).astype(BF16)


def query(rows_0, rows_1, wq):
    count, depth = rows_0.shape
    width = wq.shape[1]
    return pl.pallas_call(
        query_kernel,
        in_specs=[IN_VMEM] * 3,
        out_specs=IN_VMEM,
        out_shape=shape((2 * count, width)),
        compiler_params=params(),
        cost_estimate=cost(4 * count * depth * width, 4 * count * depth),
    )(rows_0, rows_1, wq)


def third_kernel(rows_0, rows_1, wk, wv, pattern, keys, values, kept_k, kept_v):
    rows = jnp.concatenate([rows_0[...], rows_1[...]], axis=0)
    for part in halves_of(wk.shape[1]):
        keys[:, part] = dot(rows, wk[:, part]).astype(BF16)
        values[:, part] = dot(rows, wv[:, part]).astype(BF16)

    def block(where):
        return lambda head: (head_of(keys, head, where), head_of(values, head, where))

    blocks = [block(slice(i * BLOCK, (i + 1) * BLOCK)) for i in range(BLOCKS_HALF)]
    pick_dilated(pattern, blocks, ((kept_k, 0), (kept_v, 0)))


def third(rows_0, rows_1, wk, wv, pattern):
    count, depth = rows_0.shape
    width = wk.shape[1]
    kept = (1, width // HEAD_SIZE, FAR_ROWS, HEAD_SIZE)
    return pl.pallas_call(
        third_kernel,
        in_specs=[IN_VMEM] * 5,
        out_specs=[IN_VMEM] * 4,
        out_shape=[shape((2 * count, width))] * 2 + [shape(kept)] * 2,
        compiler_params=params(),
        cost_estimate=cost(8 * count * depth * width, 4 * count * depth),
    )(rows_0, rows_1, wk, wv, pattern)


def slide_of(place, slides, block):
    end, total = jnp.int32(0), jnp.zeros_like(block)
    for index in range(slides):
        end = end + place[index]
        total = total + (block >= end).astype(jnp.int32)
    return total


def hidden_if_not(condition):
    return jnp.where(condition, jnp.float32(0), jnp.float32(HIDDEN))


def bias_kernel(slides, subs, spans, few, place, out):
    span, sub = place[slides], place[slides + 1]
    slide = [slide_of(place, slides, span * subs + (sub ^ r)) for r in range(subs)]
    for r in range(subs):
        for c in range(subs):
            value = hidden_if_not(slide[r] == slide[c])
            out[r : r + 1, c * BLOCK : (c + 1) * BLOCK] = jnp.full((1, BLOCK), value, F32)
    count = spans * FAR_ROWS
    column = lax.broadcasted_iota(jnp.int32, (1, count), 1)
    far = column // FAR_ROWS
    if few:
        far = far ^ span
    upper = (column // DILATED_KEPT) % BLOCKS_HALF
    for half in range(subs // BLOCKS_HALF):
        place_0, place_1 = sub ^ (half * BLOCKS_HALF), sub ^ (half * BLOCKS_HALF + 1)
        theirs = slide_of(place, slides, far * subs + jnp.where(upper == 0, place_0, place_1))
        start = subs * BLOCK + half * count
        for r in range(subs):
            seen = (theirs == slide[r]) & (far != span)
            out[r : r + 1, start : start + count] = hidden_if_not(seen)


def make_bias(place, slides, subs, spans, few):
    columns = subs * BLOCK + subs // BLOCKS_HALF * spans * FAR_ROWS
    return pl.pallas_call(
        functools.partial(bias_kernel, slides, subs, spans, few),
        in_specs=[IN_SMEM],
        out_specs=IN_VMEM,
        out_shape=shape((subs, columns), F32),
        compiler_params=params(),
        cost_estimate=cost(64 * subs * columns, 4 * subs * columns),
    )(place)


def add_rows(scores, bias):
    return jnp.concatenate(
        [scores[i * BLOCK : (i + 1) * BLOCK] + row for i, row in enumerate(bias)], axis=0
    )


def far_update(queries, keys, values, bias, state):
    scores = add_rows(dot_t(queries, keys), bias)
    peak, total, gathered = state
    higher = jnp.maximum(peak, jnp.max(scores, axis=1, keepdims=True))
    shrink = jnp.exp2((peak - higher) * SCALE)
    weight = jnp.exp2((scores - higher) * SCALE)
    total = total * shrink + jnp.sum(weight, axis=1, keepdims=True)
    return higher, total, gathered * shrink + dot(weight.astype(BF16), values)


def far_group(parts, head):
    found = []
    for refs, slot, bits in parts:
        order = [0]
        for bit in bits:
            order += [place ^ bit for place in order]
        half = len(order) // 2
        spots = [order.index(i) for i in range(len(order))]
        pieces = [refs[spot // half][spot % half, slot, head] for spot in spots]
        found.append(jnp.concatenate(pieces, axis=0))
    return found


def attend_kernel(relative, near, halves, few, finish, bias, *refs):
    refs = list(refs)
    queries = refs.pop(0)
    if near:
        keys, values = refs[0:3], refs[3:6]
        del refs[:6]
    else:
        gathered_in, stats_in = refs[0:2]
        del refs[:2]
    far = []
    for half in halves:
        size = 2 if few else 1
        if half == 0:
            parts = [(refs[:size], slot, BOTH_BITS) for slot in range(2)]
        else:
            parts = [(refs[:size], 0, KEY_BITS), (refs[size : 2 * size], 0, VALUE_BITS)]
        del refs[: size * (half + 1)]
        far.append((half, parts))
    span = bias.shape[0] * BLOCK
    half_count = (bias.shape[1] - span) * BLOCKS_HALF // bias.shape[0]

    def rows_of_bias(columns):
        return [bias[r : r + 1, columns] for r in relative]

    def one_head(head, _):
        columns = pl.ds(pl.multiple_of(head * HEAD_SIZE, HEAD_SIZE), HEAD_SIZE)
        asked = queries[:, columns]
        if near:
            near_keys = jnp.concatenate([ref[:, columns] for ref in keys], axis=0)
            near_values = jnp.concatenate([ref[:, columns] for ref in values], axis=0)
            scores = add_rows(dot_t(asked, near_keys), rows_of_bias(slice(0, span)))
            peak = jnp.max(scores, axis=1, keepdims=True)
            weight = jnp.exp2((scores - peak) * SCALE)
            total = jnp.sum(weight, axis=1, keepdims=True)
            state = peak, total, dot(weight.astype(BF16), near_values)
        else:
            state = stats_in[head, :, 0:1], stats_in[head, :, 1:2], gathered_in[:, columns]
        for half, parts in far:
            start = span + half * half_count
            if few:
                group = far_group(parts, head)
                rows = rows_of_bias(slice(start, start + half_count))
                state = far_update(asked, *group, rows, state)
                continue

            def step(number, state, start=start, parts=parts):
                base = number * GROUP
                group = [
                    jnp.concatenate([refs[0][base + i, slot, head] for i in range(GROUP)], axis=0)
                    for refs, slot, _ in parts
                ]
                width = GROUP * FAR_ROWS
                rows = rows_of_bias(pl.ds(pl.multiple_of(start + number * width, width), width))
                return far_update(asked, *group, rows, state)

            state = lax.fori_loop(0, parts[0][0][0].shape[0] // GROUP, step, state)
        peak, total, gathered = state
        if finish:
            keep, send = refs
            context = (gathered / total).astype(BF16)
            keep[:, columns] = context[:BLOCK]
            send[:, columns] = context[BLOCK:]
        else:
            gathered_out, stats_out = refs
            gathered_out[:, columns] = gathered
            lane = lax.broadcasted_iota(jnp.int32, gathered.shape, 1)
            stats_out[head] = jnp.where(lane == 0, peak, total)
        return 0

    lax.fori_loop(0, queries.shape[1] // HEAD_SIZE, one_head, 0)


def attend(bias, few, relative, queries, halves, near=None, begun=None, finish=True):
    rows, width = queries.shape
    heads = width // HEAD_SIZE
    operands = [queries]
    operands += [*near[0], *near[1]] if near else list(begun)
    columns = bias.shape[0] * BLOCK if near else 0
    spans = 0
    for _, *parts in halves:
        operands += sum(parts, [])
        spans += sum(part.shape[0] for part in parts[0])
    columns += spans * FAR_ROWS
    if finish:
        out_shape = [shape((BLOCK, width))] * 2
    else:
        out_shape = [shape((rows, width), F32), shape((heads, rows, HEAD_SIZE), F32)]
    far_bytes = 4 * spans * FAR_ROWS * width
    return pl.pallas_call(
        functools.partial(
            attend_kernel, relative, near is not None, [half[0] for half in halves], few, finish
        ),
        in_specs=[IN_VMEM] * (1 + len(operands)),
        out_specs=[IN_VMEM] * 2,
        out_shape=out_shape,
        compiler_params=params(far_bytes),
        cost_estimate=cost(
            4 * rows * columns * width, 4 * rows * width, heads * rows * columns
        ),
    )(bias, *operands)


def mix_kernel(rows_0, rows_1, weight_0, weight_1, out):
    tile = min(512, out.shape[1])
    for index in range(out.shape[1] // tile):
        part = slice(index * tile, (index + 1) * tile)
        total = dot(rows_0[...], weight_0[:, part]) + dot(rows_1[...], weight_1[:, part])
        out[:, part] = total.astype(out.dtype)


def mix(rows_0, rows_1, weight_0, weight_1, dtype):
    rows, depth = rows_0.shape
    width = weight_0.shape[1]
    return pl.pallas_call(
        mix_kernel,
        in_specs=[IN_VMEM] * 4,
        out_specs=IN_VMEM,
        out_shape=shape((rows, width), dtype),
        compiler_params=params(),
        cost_estimate=cost(4 * rows * depth * width, 4 * rows * width),
    )(rows_0, rows_1, weight_0, weight_1)


def shards(seqs, subs, normed, w_query, w_key, w_value, w_out, pattern, slide_lengths):
    slides = slide_lengths.shape[0]
    axes = [lax.axis_index(name).astype(jnp.int32)[None] for name in ("seq", "sub")]
    few = seqs == GROUP

    def swap(array, bit, axis="sub"):
        count = subs if axis == "sub" else seqs
        return lax.ppermute(array, axis, [(i, i ^ bit) for i in range(count)])

    def after(array, *others):
        return lax.optimization_barrier((array, *others))[0]

    def double(parts, bit, hook=lambda came: came):
        return jnp.concatenate([parts, hook(swap(parts, bit, "seq"))], axis=0)

    across = swap(normed, 2)
    beside = swap(normed, 1)
    mine, wk, wv, keys_0, values_0 = first(normed, w_key, w_value)
    keys_1, values_1, kept_a = second(beside, wk, wv, keys_0, values_0, pattern)
    place = jnp.concatenate([after(slide_lengths, kept_a), *axes])
    bias = make_bias(place, slides, subs, seqs, few)
    if few:
        kept_a = double(kept_a[None], BOTH_BITS[0], lambda came: after(came, bias))
        mine = after(mine, kept_a)
    query_a, wq, wo = query_first(mine, beside, w_query, w_out)
    if few:
        came = swap(kept_a, BOTH_BITS[1], "seq")
        across, came, query_a = lax.optimization_barrier((across, came, query_a))
        kept_a = jnp.concatenate([kept_a, came], axis=0)
        half_a = 0, [kept_a, swap(kept_a, BOTH_BITS[2], "seq")]
    else:
        half_a = 0, [lax.all_gather(kept_a, "seq", axis=0)]
    beyond = swap(across, 1)
    keys_2, values_2, *kept_b = third(across, beyond, wk, wv, pattern)
    wo_beside = swap(after(w_out, kept_b[0]), 1)
    wo_beside = pltpu.with_memory_space_constraint(wo_beside, pltpu.VMEM)
    query_b = query(across, beyond, wq)
    if few:
        k, v = double(kept_b[0][None], KEY_BITS[0]), double(kept_b[1][None], VALUE_BITS[0])
        came = swap(k, KEY_BITS[1], "seq"), swap(v, VALUE_BITS[1], "seq")
        *came, query_b, half_a[1][1] = lax.optimization_barrier((*came, query_b, half_a[1][1]))
        k, v = jnp.concatenate([k, came[0]], axis=0), jnp.concatenate([v, came[1]], axis=0)
        half_b = 1, [k, swap(k, KEY_BITS[2], "seq")], [v, swap(v, VALUE_BITS[2], "seq")]
    else:
        half_b = 1, *[[lax.all_gather(part, "seq", axis=0)] for part in kept_b]
    near = [keys_0, keys_1, keys_2], [values_0, values_1, values_2]
    call = functools.partial(attend, bias, few)
    asked = after(query_b, half_b[1][0], half_b[2][0])
    begun = call((2, 3), asked, [half_a], near=near, finish=False)
    keep_b, send_b = call((2, 3), query_b, [half_b], begun=begun)
    other_b = swap(send_b, 1)
    leaving = mix(keep_b, other_b, wo, wo_beside, BF16)
    arriving = swap(leaving, 2)
    query_a = after(query_a, leaving)
    keep_a, send_a = call((0, 1), query_a, [half_a, half_b], near=near)
    other_a = swap(send_a, 1)
    own = mix(keep_a, other_a, wo, wo_beside, F32)
    return (own + arriving.astype(F32)).astype(BF16)


def solution(mesh):
    placed = (
        P(("seq", "sub"), None),
        P(None, "sub"),
        P(None, "sub"),
        P(None, "sub"),
        P("sub", None),
        P("sub", None),
        P(),
    )
    return jax.shard_map(
        functools.partial(shards, mesh.shape["seq"], mesh.shape["sub"]),
        mesh=mesh,
        in_specs=placed,
        out_specs=P(("seq", "sub"), None),
        check_vma=False,
    )
```

```python
import functools
import math

import jax
import jax.numpy as jnp
from jax import lax
from jax.experimental import pallas as pl
from jax.experimental.pallas import tpu as pltpu
from jax.sharding import PartitionSpec as P

HEAD_SIZE = 128
BLOCK = 128
DILATED_KEPT = 16
BLOCKS_HALF = 2
FAR_ROWS = BLOCKS_HALF * DILATED_KEPT
GROUP = 8
HIDDEN = -1e30
SCALE = math.log2(math.e) / math.sqrt(HEAD_SIZE)
BF16 = jnp.bfloat16
F32 = jnp.float32
IN_VMEM = pl.BlockSpec(memory_space=pltpu.VMEM)
IN_HBM = pl.BlockSpec(memory_space=pltpu.HBM)
IN_SMEM = pl.BlockSpec(memory_space=pltpu.SMEM)
Y_BIT = 1
Z_BITS = (2, 4, 6)


def dot(a, b):
    return jnp.dot(a, b, preferred_element_type=F32)


def dot_t(a, b):
    return lax.dot_general(a, b, (((1,), (1,)), ((), ())), preferred_element_type=F32)


def params(extra=0):
    return pltpu.CompilerParams(vmem_limit_bytes=16 * 2**20 + extra)


def cost(flops, bytes_accessed, transcendentals=0):
    return pl.CostEstimate(
        flops=flops, bytes_accessed=bytes_accessed, transcendentals=transcendentals
    )


def shape(dims, dtype=BF16):
    return jax.ShapeDtypeStruct(tuple(dims), dtype)


def keep_in_hbm(array):
    return pltpu.with_memory_space_constraint(array, pltpu.HBM)


def halves_of(width):
    tile = min(256, width)
    return [slice(i * tile, (i + 1) * tile) for i in range(width // tile)]


def pick_dilated(pattern, blocks, kept):
    positions = lax.broadcasted_iota(jnp.int32, (BLOCK, BLOCK), 0)
    for head in range(kept.shape[1]):
        row = pattern[head : head + 1, :]
        chosen = (positions == row).astype(F32).T[:DILATED_KEPT].astype(BF16)
        for index, block in enumerate(blocks):
            picked = dot(chosen, jnp.concatenate(block(head), axis=1)).astype(BF16)
            spot = slice(index * DILATED_KEPT, (index + 1) * DILATED_KEPT)
            kept[0, head, spot, :] = picked[:, :HEAD_SIZE]
            kept[1, head, spot, :] = picked[:, HEAD_SIZE:]


def head_of(ref, head, rows=slice(None)):
    return ref[rows, head * HEAD_SIZE : (head + 1) * HEAD_SIZE]


def first_kernel(rows_hbm, wk_hbm, wv_hbm, rows, wk, wv, keys, values, sems):
    parts = halves_of(wk.shape[1])
    whole = pltpu.make_async_copy(rows_hbm, rows, sems.at[0])
    whole.start()
    copies = []
    for index, part in enumerate(parts):
        for side, (source, target) in enumerate(((wk_hbm, wk), (wv_hbm, wv))):
            copy = pltpu.make_async_copy(
                source.at[:, part], target.at[:, part], sems.at[1 + 2 * index + side]
            )
            copy.start()
            copies.append((copy, target, part, (keys, values)[side]))
    whole.wait()
    for copy, weight, part, out in copies:
        copy.wait()
        out[:, part] = dot(rows[...], weight[:, part]).astype(BF16)


def first(rows, w_key, w_value):
    count, depth = rows.shape
    width = w_key.shape[1]
    return pl.pallas_call(
        first_kernel,
        in_specs=[IN_HBM] * 3,
        out_specs=[IN_VMEM] * 5,
        out_shape=[
            pltpu.VMEM(rows.shape, BF16),
            pltpu.VMEM(w_key.shape, BF16),
            pltpu.VMEM(w_value.shape, BF16),
            shape((count, width)),
            shape((count, width)),
        ],
        scratch_shapes=[pltpu.SemaphoreType.DMA((1 + 2 * len(halves_of(width)),))],
        compiler_params=params(),
        cost_estimate=cost(4 * count * depth * width, 4 * depth * width),
    )(keep_in_hbm(rows), keep_in_hbm(w_key), keep_in_hbm(w_value))


def second_kernel(rows, wk, wv, keys_0, values_0, pattern, keys, values, kept):
    for part in halves_of(wk.shape[1]):
        keys[:, part] = dot(rows[...], wk[:, part]).astype(BF16)
        values[:, part] = dot(rows[...], wv[:, part]).astype(BF16)
    blocks = [
        lambda head: (head_of(keys_0, head), head_of(values_0, head)),
        lambda head: (head_of(keys, head), head_of(values, head)),
    ]
    pick_dilated(pattern, blocks, kept)


def second(rows, wk, wv, keys_0, values_0, pattern):
    count, depth = rows.shape
    width = wk.shape[1]
    kept = (2, width // HEAD_SIZE, FAR_ROWS, HEAD_SIZE)
    return pl.pallas_call(
        second_kernel,
        in_specs=[IN_VMEM] * 6,
        out_specs=[IN_VMEM] * 3,
        out_shape=[shape((count, width))] * 2 + [shape(kept)],
        compiler_params=params(),
        cost_estimate=cost(4 * count * depth * width, 2 * count * depth),
    )(rows, wk, wv, keys_0, values_0, pattern)


def query_first_kernel(rows_0, rows_1, wq_hbm, w_hbm, queries, wq, w, sems):
    parts = halves_of(wq.shape[1])
    copies = [
        pltpu.make_async_copy(wq_hbm.at[:, part], wq.at[:, part], sems.at[index])
        for index, part in enumerate(parts)
    ]
    copies.append(pltpu.make_async_copy(w_hbm, w, sems.at[len(parts)]))
    for copy in copies:
        copy.start()
    rows = jnp.concatenate([rows_0[...], rows_1[...]], axis=0)
    for part, copy in zip(parts, copies):
        copy.wait()
        queries[:, part] = dot(rows, wq[:, part]).astype(BF16)
    copies[-1].wait()


def query_first(rows_0, rows_1, w_query, w_out):
    count, depth = rows_0.shape
    width = w_query.shape[1]
    return pl.pallas_call(
        query_first_kernel,
        in_specs=[IN_VMEM] * 2 + [IN_HBM] * 2,
        out_specs=[IN_VMEM] * 3,
        out_shape=[
            shape((2 * count, width)),
            pltpu.VMEM(w_query.shape, BF16),
            pltpu.VMEM(w_out.shape, BF16),
        ],
        scratch_shapes=[pltpu.SemaphoreType.DMA((1 + len(halves_of(width)),))],
        compiler_params=params(),
        cost_estimate=cost(4 * count * depth * width, 4 * depth * width),
    )(rows_0, rows_1, keep_in_hbm(w_query), keep_in_hbm(w_out))


def query_kernel(rows_0, rows_1, wq, queries):
    rows = jnp.concatenate([rows_0[...], rows_1[...]], axis=0)
    for part in halves_of(wq.shape[1]):
        queries[:, part] = dot(rows, wq[:, part]).astype(BF16)


def query(rows_0, rows_1, wq):
    count, depth = rows_0.shape
    width = wq.shape[1]
    return pl.pallas_call(
        query_kernel,
        in_specs=[IN_VMEM] * 3,
        out_specs=IN_VMEM,
        out_shape=shape((2 * count, width)),
        compiler_params=params(),
        cost_estimate=cost(4 * count * depth * width, 4 * count * depth),
    )(rows_0, rows_1, wq)


def third_kernel(rows_0, rows_1, wk, wv, pattern, keys, values, kept):
    rows = jnp.concatenate([rows_0[...], rows_1[...]], axis=0)
    for part in halves_of(wk.shape[1]):
        keys[:, part] = dot(rows, wk[:, part]).astype(BF16)
        values[:, part] = dot(rows, wv[:, part]).astype(BF16)

    def block(where):
        return lambda head: (head_of(keys, head, where), head_of(values, head, where))

    blocks = [block(slice(i * BLOCK, (i + 1) * BLOCK)) for i in range(BLOCKS_HALF)]
    pick_dilated(pattern, blocks, kept)


def third(rows_0, rows_1, wk, wv, pattern):
    count, depth = rows_0.shape
    width = wk.shape[1]
    kept = (2, width // HEAD_SIZE, FAR_ROWS, HEAD_SIZE)
    return pl.pallas_call(
        third_kernel,
        in_specs=[IN_VMEM] * 5,
        out_specs=[IN_VMEM] * 3,
        out_shape=[shape((2 * count, width))] * 2 + [shape(kept)],
        compiler_params=params(),
        cost_estimate=cost(8 * count * depth * width, 4 * count * depth),
    )(rows_0, rows_1, wk, wv, pattern)


def slide_of(place, slides, block):
    end, total = jnp.int32(0), jnp.zeros_like(block)
    for index in range(slides):
        end = end + place[index]
        total = total + (block >= end).astype(jnp.int32)
    return total


def hidden_if_not(condition):
    return jnp.where(condition, jnp.float32(0), jnp.float32(HIDDEN))


def bias_kernel(slides, subs, spans, few, place, out):
    span, sub = place[slides], place[slides + 1]
    slide = [slide_of(place, slides, span * subs + (sub ^ r)) for r in range(subs)]
    for r in range(subs):
        for c in range(subs):
            value = hidden_if_not(slide[r] == slide[c])
            out[r : r + 1, c * BLOCK : (c + 1) * BLOCK] = jnp.full((1, BLOCK), value, F32)
    count = spans * FAR_ROWS
    column = lax.broadcasted_iota(jnp.int32, (1, count), 1)
    far = column // FAR_ROWS
    if few:
        far = far ^ span
    upper = (column // DILATED_KEPT) % BLOCKS_HALF
    for half in range(subs // BLOCKS_HALF):
        place_0, place_1 = sub ^ (half * BLOCKS_HALF), sub ^ (half * BLOCKS_HALF + 1)
        theirs = slide_of(place, slides, far * subs + jnp.where(upper == 0, place_0, place_1))
        start = subs * BLOCK + half * count
        for r in range(subs):
            seen = (theirs == slide[r]) & (far != span)
            out[r : r + 1, start : start + count] = hidden_if_not(seen)


def make_bias(place, slides, subs, spans, few):
    columns = subs * BLOCK + subs // BLOCKS_HALF * spans * FAR_ROWS
    return pl.pallas_call(
        functools.partial(bias_kernel, slides, subs, spans, few),
        in_specs=[IN_SMEM],
        out_specs=IN_VMEM,
        out_shape=shape((subs, columns), F32),
        compiler_params=params(),
        cost_estimate=cost(64 * subs * columns, 4 * subs * columns),
    )(place)


def add_rows(scores, bias):
    return jnp.concatenate(
        [scores[i * BLOCK : (i + 1) * BLOCK] + row for i, row in enumerate(bias)], axis=0
    )


def far_update(queries, keys, values, bias, state):
    scores = add_rows(dot_t(queries, keys), bias)
    peak, total, gathered = state
    higher = jnp.maximum(peak, jnp.max(scores, axis=1, keepdims=True))
    shrink = jnp.exp2((peak - higher) * SCALE)
    weight = jnp.exp2((scores - higher) * SCALE)
    total = total * shrink + jnp.sum(weight, axis=1, keepdims=True)
    return higher, total, gathered * shrink + dot(weight.astype(BF16), values)


def far_group(refs, head):
    mine, along_z, along_y, beyond = refs
    found = []
    for slot in range(2):
        pieces = [mine[slot, head], along_y[slot, head]]
        for step in range(len(Z_BITS)):
            pieces += [along_z[step, slot, head], beyond[step, slot, head]]
        found.append(jnp.concatenate(pieces, axis=0))
    return found


def attend_kernel(relative, near, halves, few, finish, bias, *refs):
    refs = list(refs)
    queries = refs.pop(0)
    if near:
        keys, values = refs[0:3], refs[3:6]
        del refs[:6]
    else:
        gathered_in, stats_in = refs[0:2]
        del refs[:2]
    far = []
    for half in halves:
        size = 4 if few else 1
        far.append((half, refs[:size]))
        del refs[:size]
    span = bias.shape[0] * BLOCK
    half_count = (bias.shape[1] - span) * BLOCKS_HALF // bias.shape[0]

    def rows_of_bias(columns):
        return [bias[r : r + 1, columns] for r in relative]

    def one_head(head, _):
        columns = pl.ds(pl.multiple_of(head * HEAD_SIZE, HEAD_SIZE), HEAD_SIZE)
        asked = queries[:, columns]
        if near:
            near_keys = jnp.concatenate([ref[:, columns] for ref in keys], axis=0)
            near_values = jnp.concatenate([ref[:, columns] for ref in values], axis=0)
            scores = add_rows(dot_t(asked, near_keys), rows_of_bias(slice(0, span)))
            peak = jnp.max(scores, axis=1, keepdims=True)
            weight = jnp.exp2((scores - peak) * SCALE)
            total = jnp.sum(weight, axis=1, keepdims=True)
            state = peak, total, dot(weight.astype(BF16), near_values)
        else:
            state = stats_in[head, :, 0:1], stats_in[head, :, 1:2], gathered_in[:, columns]
        for half, parts in far:
            start = span + half * half_count
            if few:
                group = far_group(parts, head)
                rows = rows_of_bias(slice(start, start + half_count))
                state = far_update(asked, *group, rows, state)
                continue

            def step(number, state, start=start, part=parts[0]):
                base = number * GROUP
                group = [
                    jnp.concatenate([part[base + i, slot, head] for i in range(GROUP)], axis=0)
                    for slot in range(2)
                ]
                width = GROUP * FAR_ROWS
                rows = rows_of_bias(pl.ds(pl.multiple_of(start + number * width, width), width))
                return far_update(asked, *group, rows, state)

            state = lax.fori_loop(0, parts[0].shape[0] // GROUP, step, state)
        peak, total, gathered = state
        if finish:
            keep, send = refs
            context = (gathered / total).astype(BF16)
            keep[:, columns] = context[:BLOCK]
            send[:, columns] = context[BLOCK:]
        else:
            gathered_out, stats_out = refs
            gathered_out[:, columns] = gathered
            lane = lax.broadcasted_iota(jnp.int32, gathered.shape, 1)
            stats_out[head] = jnp.where(lane == 0, peak, total)
        return 0

    lax.fori_loop(0, queries.shape[1] // HEAD_SIZE, one_head, 0)


def attend(bias, few, relative, queries, halves, near=None, begun=None, finish=True):
    rows, width = queries.shape
    heads = width // HEAD_SIZE
    operands = [queries]
    operands += [*near[0], *near[1]] if near else list(begun)
    columns = bias.shape[0] * BLOCK if near else 0
    for _, parts in halves:
        operands += parts
    far_bytes = sum(2 * part.size for _, parts in halves for part in parts)
    spans = far_bytes // (4 * FAR_ROWS * width)
    columns += spans * FAR_ROWS
    if finish:
        out_shape = [shape((BLOCK, width))] * 2
    else:
        out_shape = [shape((rows, width), F32), shape((heads, rows, HEAD_SIZE), F32)]
    return pl.pallas_call(
        functools.partial(
            attend_kernel, relative, near is not None, [half[0] for half in halves], few, finish
        ),
        in_specs=[IN_VMEM] * (1 + len(operands)),
        out_specs=[IN_VMEM] * 2,
        out_shape=out_shape,
        compiler_params=params(far_bytes),
        cost_estimate=cost(
            4 * rows * columns * width, 4 * rows * width, heads * rows * columns
        ),
    )(bias, *operands)


def mix_kernel(rows_0, rows_1, weight_0, weight_1, out):
    tile = min(512, out.shape[1])
    for index in range(out.shape[1] // tile):
        part = slice(index * tile, (index + 1) * tile)
        total = dot(rows_0[...], weight_0[:, part]) + dot(rows_1[...], weight_1[:, part])
        out[:, part] = total.astype(out.dtype)


def mix(rows_0, rows_1, weight_0, weight_1, dtype):
    rows, depth = rows_0.shape
    width = weight_0.shape[1]
    return pl.pallas_call(
        mix_kernel,
        in_specs=[IN_VMEM] * 4,
        out_specs=IN_VMEM,
        out_shape=shape((rows, width), dtype),
        compiler_params=params(),
        cost_estimate=cost(4 * rows * depth * width, 4 * rows * width),
    )(rows_0, rows_1, weight_0, weight_1)


def shards(seqs, subs, normed, w_query, w_key, w_value, w_out, pattern, slide_lengths):
    slides = slide_lengths.shape[0]
    axes = [lax.axis_index(name).astype(jnp.int32)[None] for name in ("seq", "sub")]
    few = seqs == GROUP

    def swap(array, bit, axis="sub"):
        count = subs if axis == "sub" else seqs
        return lax.ppermute(array, axis, [(i, i ^ bit) for i in range(count)])

    def after(array, *others):
        return lax.optimization_barrier((array, *others))[0]

    def first_round(kept):
        return [swap(kept, bit, "seq") for bit in Z_BITS], swap(kept, Y_BIT, "seq")

    def second_round(kept, along_z, along_y):
        along_z = jnp.stack(along_z)
        return [kept, along_z, along_y, swap(along_z, Y_BIT, "seq")]

    across = swap(normed, 2)
    beside = swap(normed, 1)
    mine, wk, wv, keys_0, values_0 = first(normed, w_key, w_value)
    keys_1, values_1, kept_a = second(beside, wk, wv, keys_0, values_0, pattern)
    place = jnp.concatenate([after(slide_lengths, kept_a), *axes])
    bias = make_bias(place, slides, subs, seqs, few)
    query_a, wq, wo = query_first(mine, beside, w_query, w_out)
    if few:
        along_z, along_y = first_round(kept_a)
        *along_z, along_y, query_a, bias = lax.optimization_barrier(
            (*along_z, along_y, query_a, bias)
        )
        half_a = 0, second_round(kept_a, along_z, along_y)
        across = after(across, half_a[1][1])
    else:
        half_a = 0, [lax.all_gather(kept_a, "seq", axis=0)]
    beyond = swap(across, 1)
    keys_2, values_2, kept_b = third(across, beyond, wk, wv, pattern)
    query_b = query(across, beyond, wq)
    if few:
        along_z, along_y = first_round(kept_b)
        *along_z, along_y, query_b, half_a[1][3] = lax.optimization_barrier(
            (*along_z, along_y, query_b, half_a[1][3])
        )
        half_b = 1, second_round(kept_b, along_z, along_y)
        asked = after(query_b, half_b[1][1])
    else:
        half_b = 1, [lax.all_gather(kept_b, "seq", axis=0)]
        asked = query_b
    wo_beside = swap(after(w_out, asked), 1)
    wo_beside = pltpu.with_memory_space_constraint(wo_beside, pltpu.VMEM)
    near = [keys_0, keys_1, keys_2], [values_0, values_1, values_2]
    call = functools.partial(attend, bias, few)
    begun = call((2, 3), asked, [half_a], near=near, finish=False)
    keep_b, send_b = call((2, 3), query_b, [half_b], begun=begun)
    other_b = swap(send_b, 1)
    leaving = mix(keep_b, other_b, wo, wo_beside, BF16)
    arriving = swap(leaving, 2)
    query_a = after(query_a, leaving)
    keep_a, send_a = call((0, 1), query_a, [half_a, half_b], near=near)
    other_a = swap(send_a, 1)
    own = mix(keep_a, other_a, wo, wo_beside, F32)
    return (own + arriving.astype(F32)).astype(BF16)


def solution(mesh):
    placed = (
        P(("seq", "sub"), None),
        P(None, "sub"),
        P(None, "sub"),
        P(None, "sub"),
        P("sub", None),
        P("sub", None),
        P(),
    )
    return jax.shard_map(
        functools.partial(shards, mesh.shape["seq"], mesh.shape["sub"]),
        mesh=mesh,
        in_specs=placed,
        out_specs=P(("seq", "sub"), None),
        check_vma=False,
    )
```

```python
import functools
import math

import jax
import jax.numpy as jnp
from jax import lax
from jax.experimental import pallas as pl
from jax.experimental.pallas import tpu as pltpu
from jax.sharding import PartitionSpec as P

HEAD_SIZE = 128
BLOCK = 128
DILATED_KEPT = 16
BLOCKS_HALF = 2
FAR_ROWS = BLOCKS_HALF * DILATED_KEPT
GROUP = 8
HIDDEN = -1e30
SCALE = math.log2(math.e) / math.sqrt(HEAD_SIZE)
BF16 = jnp.bfloat16
F32 = jnp.float32
IN_VMEM = pl.BlockSpec(memory_space=pltpu.VMEM)
IN_HBM = pl.BlockSpec(memory_space=pltpu.HBM)
IN_SMEM = pl.BlockSpec(memory_space=pltpu.SMEM)


def dot(a, b):
    return jnp.dot(a, b, preferred_element_type=F32)


def dot_t(a, b):
    return lax.dot_general(a, b, (((1,), (1,)), ((), ())), preferred_element_type=F32)


def params(extra=0):
    return pltpu.CompilerParams(vmem_limit_bytes=16 * 2**20 + extra)


def cost(flops, bytes_accessed, transcendentals=0):
    return pl.CostEstimate(
        flops=flops, bytes_accessed=bytes_accessed, transcendentals=transcendentals
    )


def shape(dims, dtype=BF16):
    return jax.ShapeDtypeStruct(tuple(dims), dtype)


def keep_in_hbm(array):
    return pltpu.with_memory_space_constraint(array, pltpu.HBM)


def halves_of(width):
    tile = min(256, width)
    return [slice(i * tile, (i + 1) * tile) for i in range(width // tile)]


def pick_dilated(pattern, blocks, kept):
    positions = lax.broadcasted_iota(jnp.int32, (BLOCK, BLOCK), 0)
    for head in range(kept.shape[1]):
        row = pattern[head : head + 1, :]
        chosen = (positions == row).astype(F32).T[:DILATED_KEPT].astype(BF16)
        for index, block in enumerate(blocks):
            picked = dot(chosen, jnp.concatenate(block(head), axis=1)).astype(BF16)
            spot = slice(index * DILATED_KEPT, (index + 1) * DILATED_KEPT)
            kept[0, head, spot, :] = picked[:, :HEAD_SIZE]
            kept[1, head, spot, :] = picked[:, HEAD_SIZE:]


def head_of(ref, head, rows=slice(None)):
    return ref[rows, head * HEAD_SIZE : (head + 1) * HEAD_SIZE]


def first_kernel(rows_hbm, wk_hbm, wv_hbm, rows, wk, wv, keys, values, sems):
    parts = halves_of(wk.shape[1])
    whole = pltpu.make_async_copy(rows_hbm, rows, sems.at[0])
    whole.start()
    copies = []
    for index, part in enumerate(parts):
        for side, (source, target) in enumerate(((wk_hbm, wk), (wv_hbm, wv))):
            copy = pltpu.make_async_copy(
                source.at[:, part], target.at[:, part], sems.at[1 + 2 * index + side]
            )
            copy.start()
            copies.append((copy, target, part, (keys, values)[side]))
    whole.wait()
    for copy, weight, part, out in copies:
        copy.wait()
        out[:, part] = dot(rows[...], weight[:, part]).astype(BF16)


def first(rows, w_key, w_value):
    count, depth = rows.shape
    width = w_key.shape[1]
    return pl.pallas_call(
        first_kernel,
        in_specs=[IN_HBM] * 3,
        out_specs=[IN_VMEM] * 5,
        out_shape=[
            pltpu.VMEM(rows.shape, BF16),
            pltpu.VMEM(w_key.shape, BF16),
            pltpu.VMEM(w_value.shape, BF16),
            shape((count, width)),
            shape((count, width)),
        ],
        scratch_shapes=[pltpu.SemaphoreType.DMA((1 + 2 * len(halves_of(width)),))],
        compiler_params=params(),
        cost_estimate=cost(4 * count * depth * width, 4 * depth * width),
    )(keep_in_hbm(rows), keep_in_hbm(w_key), keep_in_hbm(w_value))


def second_kernel(rows, wk, wv, keys_0, values_0, pattern, keys, values, kept):
    for part in halves_of(wk.shape[1]):
        keys[:, part] = dot(rows[...], wk[:, part]).astype(BF16)
        values[:, part] = dot(rows[...], wv[:, part]).astype(BF16)
    blocks = [
        lambda head: (head_of(keys_0, head), head_of(values_0, head)),
        lambda head: (head_of(keys, head), head_of(values, head)),
    ]
    pick_dilated(pattern, blocks, kept)


def second(rows, wk, wv, keys_0, values_0, pattern):
    count, depth = rows.shape
    width = wk.shape[1]
    kept = (2, width // HEAD_SIZE, FAR_ROWS, HEAD_SIZE)
    return pl.pallas_call(
        second_kernel,
        in_specs=[IN_VMEM] * 6,
        out_specs=[IN_VMEM] * 3,
        out_shape=[shape((count, width))] * 2 + [shape(kept)],
        compiler_params=params(),
        cost_estimate=cost(4 * count * depth * width, 2 * count * depth),
    )(rows, wk, wv, keys_0, values_0, pattern)


def query_first_kernel(rows_0, rows_1, wq_hbm, w_hbm, queries, wq, w, sems):
    parts = halves_of(wq.shape[1])
    copies = [
        pltpu.make_async_copy(wq_hbm.at[:, part], wq.at[:, part], sems.at[index])
        for index, part in enumerate(parts)
    ]
    copies.append(pltpu.make_async_copy(w_hbm, w, sems.at[len(parts)]))
    for copy in copies:
        copy.start()
    rows = jnp.concatenate([rows_0[...], rows_1[...]], axis=0)
    for part, copy in zip(parts, copies):
        copy.wait()
        queries[:, part] = dot(rows, wq[:, part]).astype(BF16)
    copies[-1].wait()


def query_first(rows_0, rows_1, w_query, w_out):
    count, depth = rows_0.shape
    width = w_query.shape[1]
    return pl.pallas_call(
        query_first_kernel,
        in_specs=[IN_VMEM] * 2 + [IN_HBM] * 2,
        out_specs=[IN_VMEM] * 3,
        out_shape=[
            shape((2 * count, width)),
            pltpu.VMEM(w_query.shape, BF16),
            pltpu.VMEM(w_out.shape, BF16),
        ],
        scratch_shapes=[pltpu.SemaphoreType.DMA((1 + len(halves_of(width)),))],
        compiler_params=params(),
        cost_estimate=cost(4 * count * depth * width, 4 * depth * width),
    )(rows_0, rows_1, keep_in_hbm(w_query), keep_in_hbm(w_out))


def query_kernel(rows_0, rows_1, wq, queries):
    rows = jnp.concatenate([rows_0[...], rows_1[...]], axis=0)
    for part in halves_of(wq.shape[1]):
        queries[:, part] = dot(rows, wq[:, part]).astype(BF16)


def query(rows_0, rows_1, wq):
    count, depth = rows_0.shape
    width = wq.shape[1]
    return pl.pallas_call(
        query_kernel,
        in_specs=[IN_VMEM] * 3,
        out_specs=IN_VMEM,
        out_shape=shape((2 * count, width)),
        compiler_params=params(),
        cost_estimate=cost(4 * count * depth * width, 4 * count * depth),
    )(rows_0, rows_1, wq)


def third_kernel(rows_0, rows_1, wk, wv, pattern, keys, values, kept):
    rows = jnp.concatenate([rows_0[...], rows_1[...]], axis=0)
    for part in halves_of(wk.shape[1]):
        keys[:, part] = dot(rows, wk[:, part]).astype(BF16)
        values[:, part] = dot(rows, wv[:, part]).astype(BF16)

    def block(where):
        return lambda head: (head_of(keys, head, where), head_of(values, head, where))

    blocks = [block(slice(i * BLOCK, (i + 1) * BLOCK)) for i in range(BLOCKS_HALF)]
    pick_dilated(pattern, blocks, kept)


def third(rows_0, rows_1, wk, wv, pattern):
    count, depth = rows_0.shape
    width = wk.shape[1]
    kept = (2, width // HEAD_SIZE, FAR_ROWS, HEAD_SIZE)
    return pl.pallas_call(
        third_kernel,
        in_specs=[IN_VMEM] * 5,
        out_specs=[IN_VMEM] * 3,
        out_shape=[shape((2 * count, width))] * 2 + [shape(kept)],
        compiler_params=params(),
        cost_estimate=cost(8 * count * depth * width, 4 * count * depth),
    )(rows_0, rows_1, wk, wv, pattern)


def slide_of(place, slides, block):
    end, total = jnp.int32(0), jnp.zeros_like(block)
    for index in range(slides):
        end = end + place[index]
        total = total + (block >= end).astype(jnp.int32)
    return total


def hidden_if_not(condition):
    return jnp.where(condition, jnp.float32(0), jnp.float32(HIDDEN))


def bias_kernel(slides, subs, spans, place, out):
    span, sub = place[slides], place[slides + 1]
    slide = [slide_of(place, slides, span * subs + (sub ^ r)) for r in range(subs)]
    for r in range(subs):
        for c in range(subs):
            value = hidden_if_not(slide[r] == slide[c])
            out[r : r + 1, c * BLOCK : (c + 1) * BLOCK] = jnp.full((1, BLOCK), value, F32)
    count = spans * FAR_ROWS
    column = lax.broadcasted_iota(jnp.int32, (1, count), 1)
    far = column // FAR_ROWS
    upper = (column // DILATED_KEPT) % BLOCKS_HALF
    for half in range(subs // BLOCKS_HALF):
        place_0, place_1 = sub ^ (half * BLOCKS_HALF), sub ^ (half * BLOCKS_HALF + 1)
        theirs = slide_of(place, slides, far * subs + jnp.where(upper == 0, place_0, place_1))
        start = subs * BLOCK + half * count
        for r in range(subs):
            seen = (theirs == slide[r]) & (far != span)
            out[r : r + 1, start : start + count] = hidden_if_not(seen)


def make_bias(place, slides, subs, spans):
    columns = subs * BLOCK + subs // BLOCKS_HALF * spans * FAR_ROWS
    return pl.pallas_call(
        functools.partial(bias_kernel, slides, subs, spans),
        in_specs=[IN_SMEM],
        out_specs=IN_VMEM,
        out_shape=shape((subs, columns), F32),
        compiler_params=params(),
        cost_estimate=cost(64 * subs * columns, 4 * subs * columns),
    )(place)


def add_rows(scores, bias):
    return jnp.concatenate(
        [scores[i * BLOCK : (i + 1) * BLOCK] + row for i, row in enumerate(bias)], axis=0
    )


def far_update(queries, keys, values, bias, state):
    scores = add_rows(dot_t(queries, keys), bias)
    peak, total, gathered = state
    higher = jnp.maximum(peak, jnp.max(scores, axis=1, keepdims=True))
    shrink = jnp.exp2((peak - higher) * SCALE)
    weight = jnp.exp2((scores - higher) * SCALE)
    total = total * shrink + jnp.sum(weight, axis=1, keepdims=True)
    return higher, total, gathered * shrink + dot(weight.astype(BF16), values)


def attend_kernel(relative, near, halves, finish, bias, *refs):
    refs = list(refs)
    queries = refs.pop(0)
    if near:
        keys, values = refs[0:3], refs[3:6]
        del refs[:6]
    else:
        gathered_in, stats_in = refs[0:2]
        del refs[:2]
    far = []
    for half in halves:
        far.append((half, refs.pop(0)))
    span = bias.shape[0] * BLOCK
    half_count = (bias.shape[1] - span) * BLOCKS_HALF // bias.shape[0]

    def rows_of_bias(columns):
        return [bias[r : r + 1, columns] for r in relative]

    def one_head(head, _):
        columns = pl.ds(pl.multiple_of(head * HEAD_SIZE, HEAD_SIZE), HEAD_SIZE)
        asked = queries[:, columns]
        if near:
            near_keys = jnp.concatenate([ref[:, columns] for ref in keys], axis=0)
            near_values = jnp.concatenate([ref[:, columns] for ref in values], axis=0)
            scores = add_rows(dot_t(asked, near_keys), rows_of_bias(slice(0, span)))
            peak = jnp.max(scores, axis=1, keepdims=True)
            weight = jnp.exp2((scores - peak) * SCALE)
            total = jnp.sum(weight, axis=1, keepdims=True)
            state = peak, total, dot(weight.astype(BF16), near_values)
        else:
            state = stats_in[head, :, 0:1], stats_in[head, :, 1:2], gathered_in[:, columns]
        for half, part in far:
            start = span + half * half_count
            width = GROUP * FAR_ROWS

            def step(number, state, start=start, part=part):
                base = number * GROUP
                group = [
                    jnp.concatenate([part[base + i, slot, head] for i in range(GROUP)], axis=0)
                    for slot in range(2)
                ]
                first_column = start + number * width
                if not isinstance(first_column, int):
                    first_column = pl.multiple_of(first_column, width)
                return far_update(asked, *group, rows_of_bias(pl.ds(first_column, width)), state)

            steps = part.shape[0] // GROUP
            state = step(0, state) if steps == 1 else lax.fori_loop(0, steps, step, state)
        peak, total, gathered = state
        if finish:
            keep, send = refs
            context = (gathered / total).astype(BF16)
            keep[:, columns] = context[:BLOCK]
            send[:, columns] = context[BLOCK:]
        else:
            gathered_out, stats_out = refs
            gathered_out[:, columns] = gathered
            lane = lax.broadcasted_iota(jnp.int32, gathered.shape, 1)
            stats_out[head] = jnp.where(lane == 0, peak, total)
        return 0

    lax.fori_loop(0, queries.shape[1] // HEAD_SIZE, one_head, 0)


def attend(bias, relative, queries, halves, near=None, begun=None, finish=True):
    rows, width = queries.shape
    heads = width // HEAD_SIZE
    operands = [queries]
    operands += [*near[0], *near[1]] if near else list(begun)
    columns = bias.shape[0] * BLOCK if near else 0
    operands += [part for _, part in halves]
    far_bytes = sum(2 * part.size for _, part in halves)
    spans = far_bytes // (4 * FAR_ROWS * width)
    columns += spans * FAR_ROWS
    if finish:
        out_shape = [shape((BLOCK, width))] * 2
    else:
        out_shape = [shape((rows, width), F32), shape((heads, rows, HEAD_SIZE), F32)]
    return pl.pallas_call(
        functools.partial(
            attend_kernel, relative, near is not None, [half[0] for half in halves], finish
        ),
        in_specs=[IN_VMEM] * (1 + len(operands)),
        out_specs=[IN_VMEM] * 2,
        out_shape=out_shape,
        compiler_params=params(far_bytes),
        cost_estimate=cost(
            4 * rows * columns * width, 4 * rows * width, heads * rows * columns
        ),
    )(bias, *operands)


def mix_kernel(rows_0, rows_1, weight_0, weight_1, out):
    tile = min(512, out.shape[1])
    for index in range(out.shape[1] // tile):
        part = slice(index * tile, (index + 1) * tile)
        total = dot(rows_0[...], weight_0[:, part]) + dot(rows_1[...], weight_1[:, part])
        out[:, part] = total.astype(out.dtype)


def mix(rows_0, rows_1, weight_0, weight_1, dtype):
    rows, depth = rows_0.shape
    width = weight_0.shape[1]
    return pl.pallas_call(
        mix_kernel,
        in_specs=[IN_VMEM] * 4,
        out_specs=IN_VMEM,
        out_shape=shape((rows, width), dtype),
        compiler_params=params(),
        cost_estimate=cost(4 * rows * depth * width, 4 * rows * width),
    )(rows_0, rows_1, weight_0, weight_1)


def shards(seqs, subs, normed, w_query, w_key, w_value, w_out, pattern, slide_lengths):
    slides = slide_lengths.shape[0]
    axes = [lax.axis_index(name).astype(jnp.int32)[None] for name in ("seq", "sub")]
    few = seqs == GROUP

    def swap(array, bit, axis="sub"):
        count = subs if axis == "sub" else seqs
        return lax.ppermute(array, axis, [(i, i ^ bit) for i in range(count)])

    def after(array, *others):
        return lax.optimization_barrier((array, *others))[0]

    def spread(kept):
        if not few:
            return lax.all_gather(kept, "seq", axis=0)
        copies = jnp.broadcast_to(kept[None], (seqs, *kept.shape))
        return lax.all_to_all(copies, "seq", 0, 0)

    across = swap(normed, 2)
    beside = swap(normed, 1)
    mine, wk, wv, keys_0, values_0 = first(normed, w_key, w_value)
    keys_1, values_1, kept_a = second(beside, wk, wv, keys_0, values_0, pattern)
    place = jnp.concatenate([after(slide_lengths, kept_a), *axes])
    bias = make_bias(place, slides, subs, seqs)
    query_a, wq, wo = query_first(mine, beside, w_query, w_out)
    half_a = 0, spread(kept_a)
    across = after(across, query_a, bias)
    beyond = swap(across, 1)
    keys_2, values_2, kept_b = third(across, beyond, wk, wv, pattern)
    query_b = query(across, beyond, wq)
    half_b = 1, spread(kept_b)
    wo_beside = swap(after(w_out, kept_b), 1)
    wo_beside = pltpu.with_memory_space_constraint(wo_beside, pltpu.VMEM)
    near = [keys_0, keys_1, keys_2], [values_0, values_1, values_2]
    call = functools.partial(attend, bias)
    begun = call((2, 3), query_b, [half_a], near=near, finish=False)
    keep_b, send_b = call((2, 3), query_b, [half_b], begun=begun)
    other_b = swap(send_b, 1)
    leaving = mix(keep_b, other_b, wo, wo_beside, BF16)
    arriving = swap(leaving, 2)
    query_a = after(query_a, leaving)
    keep_a, send_a = call((0, 1), query_a, [half_a, half_b], near=near)
    other_a = swap(send_a, 1)
    own = mix(keep_a, other_a, wo, wo_beside, F32)
    return (own + arriving.astype(F32)).astype(BF16)


def solution(mesh):
    placed = (
        P(("seq", "sub"), None),
        P(None, "sub"),
        P(None, "sub"),
        P(None, "sub"),
        P("sub", None),
        P("sub", None),
        P(),
    )
    return jax.shard_map(
        functools.partial(shards, mesh.shape["seq"], mesh.shape["sub"]),
        mesh=mesh,
        in_specs=placed,
        out_specs=P(("seq", "sub"), None),
        check_vma=False,
    )
```

```python
import functools
import math

import jax
import jax.numpy as jnp
from jax import lax
from jax.experimental import pallas as pl
from jax.experimental.pallas import tpu as pltpu
from jax.sharding import PartitionSpec as P

HEAD_SIZE = 128
BLOCK = 128
DILATED_KEPT = 16
BLOCKS_HALF = 2
FAR_ROWS = BLOCKS_HALF * DILATED_KEPT
GROUP = 8
HIDDEN = -1e30
SCALE = math.log2(math.e) / math.sqrt(HEAD_SIZE)
BF16 = jnp.bfloat16
F32 = jnp.float32
IN_VMEM = pl.BlockSpec(memory_space=pltpu.VMEM)
IN_HBM = pl.BlockSpec(memory_space=pltpu.HBM)
IN_SMEM = pl.BlockSpec(memory_space=pltpu.SMEM)
Y_BIT = 1
Z_BITS = (4, 6, 2)


def dot(a, b):
    return jnp.dot(a, b, preferred_element_type=F32)


def dot_t(a, b):
    return lax.dot_general(a, b, (((1,), (1,)), ((), ())), preferred_element_type=F32)


def params(extra=0):
    return pltpu.CompilerParams(vmem_limit_bytes=16 * 2**20 + extra)


def cost(flops, bytes_accessed, transcendentals=0):
    return pl.CostEstimate(
        flops=flops // 100,
        bytes_accessed=bytes_accessed // 100,
        transcendentals=transcendentals // 100,
    )


def shape(dims, dtype=BF16):
    return jax.ShapeDtypeStruct(tuple(dims), dtype)


def keep_in_hbm(array):
    return pltpu.with_memory_space_constraint(array, pltpu.HBM)


def halves_of(width):
    tile = min(256, width)
    return [slice(i * tile, (i + 1) * tile) for i in range(width // tile)]


def pick_dilated(pattern, blocks, kept):
    positions = lax.broadcasted_iota(jnp.int32, (BLOCK, BLOCK), 0)
    for head in range(kept.shape[1]):
        row = pattern[head : head + 1, :]
        chosen = (positions == row).astype(F32).T[:DILATED_KEPT].astype(BF16)
        for index, block in enumerate(blocks):
            picked = dot(chosen, jnp.concatenate(block(head), axis=1)).astype(BF16)
            spot = slice(index * DILATED_KEPT, (index + 1) * DILATED_KEPT)
            kept[0, head, spot, :] = picked[:, :HEAD_SIZE]
            kept[1, head, spot, :] = picked[:, HEAD_SIZE:]


def head_of(ref, head, rows=slice(None)):
    return ref[rows, head * HEAD_SIZE : (head + 1) * HEAD_SIZE]


def first_kernel(rows_hbm, wk_hbm, wv_hbm, rows, wk, wv, keys, values, sems):
    parts = halves_of(wk.shape[1])
    whole = pltpu.make_async_copy(rows_hbm, rows, sems.at[0])
    whole.start()
    copies = []
    for index, part in enumerate(parts):
        for side, (source, target) in enumerate(((wk_hbm, wk), (wv_hbm, wv))):
            copy = pltpu.make_async_copy(
                source.at[:, part], target.at[:, part], sems.at[1 + 2 * index + side]
            )
            copy.start()
            copies.append((copy, target, part, (keys, values)[side]))
    whole.wait()
    for copy, weight, part, out in copies:
        copy.wait()
        out[:, part] = dot(rows[...], weight[:, part]).astype(BF16)


def first(rows, w_key, w_value):
    count, depth = rows.shape
    width = w_key.shape[1]
    return pl.pallas_call(
        first_kernel,
        in_specs=[IN_HBM] * 3,
        out_specs=[IN_VMEM] * 5,
        out_shape=[
            pltpu.VMEM(rows.shape, BF16),
            pltpu.VMEM(w_key.shape, BF16),
            pltpu.VMEM(w_value.shape, BF16),
            shape((count, width)),
            shape((count, width)),
        ],
        scratch_shapes=[pltpu.SemaphoreType.DMA((1 + 2 * len(halves_of(width)),))],
        compiler_params=params(),
        cost_estimate=cost(4 * count * depth * width, 4 * depth * width),
    )(keep_in_hbm(rows), keep_in_hbm(w_key), keep_in_hbm(w_value))


def second_kernel(rows, wk, wv, keys_0, values_0, pattern, keys, values, kept):
    for part in halves_of(wk.shape[1]):
        keys[:, part] = dot(rows[...], wk[:, part]).astype(BF16)
        values[:, part] = dot(rows[...], wv[:, part]).astype(BF16)
    blocks = [
        lambda head: (head_of(keys_0, head), head_of(values_0, head)),
        lambda head: (head_of(keys, head), head_of(values, head)),
    ]
    pick_dilated(pattern, blocks, kept)


def second(rows, wk, wv, keys_0, values_0, pattern):
    count, depth = rows.shape
    width = wk.shape[1]
    kept = (2, width // HEAD_SIZE, FAR_ROWS, HEAD_SIZE)
    return pl.pallas_call(
        second_kernel,
        in_specs=[IN_VMEM] * 6,
        out_specs=[IN_VMEM] * 3,
        out_shape=[shape((count, width))] * 2 + [shape(kept)],
        compiler_params=params(),
        cost_estimate=cost(4 * count * depth * width, 2 * count * depth),
    )(rows, wk, wv, keys_0, values_0, pattern)


def query_first_kernel(rows_0, rows_1, wq_hbm, w_hbm, queries, wq, w, sems):
    parts = halves_of(wq.shape[1])
    copies = [
        pltpu.make_async_copy(wq_hbm.at[:, part], wq.at[:, part], sems.at[index])
        for index, part in enumerate(parts)
    ]
    copies.append(pltpu.make_async_copy(w_hbm, w, sems.at[len(parts)]))
    for copy in copies:
        copy.start()
    rows = jnp.concatenate([rows_0[...], rows_1[...]], axis=0)
    for part, copy in zip(parts, copies):
        copy.wait()
        queries[:, part] = dot(rows, wq[:, part]).astype(BF16)
    copies[-1].wait()


def query_first(rows_0, rows_1, w_query, w_out):
    count, depth = rows_0.shape
    width = w_query.shape[1]
    return pl.pallas_call(
        query_first_kernel,
        in_specs=[IN_VMEM] * 2 + [IN_HBM] * 2,
        out_specs=[IN_VMEM] * 3,
        out_shape=[
            shape((2 * count, width)),
            pltpu.VMEM(w_query.shape, BF16),
            pltpu.VMEM(w_out.shape, BF16),
        ],
        scratch_shapes=[pltpu.SemaphoreType.DMA((1 + len(halves_of(width)),))],
        compiler_params=params(),
        cost_estimate=cost(4 * count * depth * width, 4 * depth * width),
    )(rows_0, rows_1, keep_in_hbm(w_query), keep_in_hbm(w_out))


def query_kernel(rows_0, rows_1, wq, queries):
    rows = jnp.concatenate([rows_0[...], rows_1[...]], axis=0)
    for part in halves_of(wq.shape[1]):
        queries[:, part] = dot(rows, wq[:, part]).astype(BF16)


def query(rows_0, rows_1, wq):
    count, depth = rows_0.shape
    width = wq.shape[1]
    return pl.pallas_call(
        query_kernel,
        in_specs=[IN_VMEM] * 3,
        out_specs=IN_VMEM,
        out_shape=shape((2 * count, width)),
        compiler_params=params(),
        cost_estimate=cost(4 * count * depth * width, 4 * count * depth),
    )(rows_0, rows_1, wq)


def across_kernel(rows, wk, wv, keys, values):
    for part in halves_of(wk.shape[1]):
        keys[:, part] = dot(rows[...], wk[:, part]).astype(BF16)
        values[:, part] = dot(rows[...], wv[:, part]).astype(BF16)


def keys_and_values(rows, wk, wv):
    count, depth = rows.shape
    width = wk.shape[1]
    return pl.pallas_call(
        across_kernel,
        in_specs=[IN_VMEM] * 3,
        out_specs=[IN_VMEM] * 2,
        out_shape=[shape((count, width))] * 2,
        compiler_params=params(),
        cost_estimate=cost(4 * count * depth * width, 2 * count * depth),
    )(rows, wk, wv)


def slide_of(place, slides, block):
    end, total = jnp.int32(0), jnp.zeros_like(block)
    for index in range(slides):
        end = end + place[index]
        total = total + (block >= end).astype(jnp.int32)
    return total


def hidden_if_not(condition):
    return jnp.where(condition, jnp.float32(0), jnp.float32(HIDDEN))


def bias_kernel(slides, subs, spans, few, place, out):
    span, sub = place[slides], place[slides + 1]
    slide = [slide_of(place, slides, span * subs + (sub ^ r)) for r in range(subs)]
    for r in range(subs):
        for c in range(subs):
            value = hidden_if_not(slide[r] == slide[c])
            out[r : r + 1, c * BLOCK : (c + 1) * BLOCK] = jnp.full((1, BLOCK), value, F32)
    count = spans * FAR_ROWS
    column = lax.broadcasted_iota(jnp.int32, (1, count), 1)
    far = column // FAR_ROWS
    if few:
        order = [bit | y for y in (0, Y_BIT) for bit in (0, *Z_BITS)]
        place_of = jnp.zeros_like(far)
        for index, bits in enumerate(order):
            place_of = jnp.where(far == index, bits, place_of)
        far = place_of ^ span
    upper = (column // DILATED_KEPT) % BLOCKS_HALF
    for half in range(subs // BLOCKS_HALF):
        place_0, place_1 = sub ^ (half * BLOCKS_HALF), sub ^ (half * BLOCKS_HALF + 1)
        theirs = slide_of(place, slides, far * subs + jnp.where(upper == 0, place_0, place_1))
        start = subs * BLOCK + half * count
        for r in range(subs):
            seen = (theirs == slide[r]) & (far != span)
            out[r : r + 1, start : start + count] = hidden_if_not(seen)


def make_bias(place, slides, subs, spans, few):
    columns = subs * BLOCK + subs // BLOCKS_HALF * spans * FAR_ROWS
    return pl.pallas_call(
        functools.partial(bias_kernel, slides, subs, spans, few),
        in_specs=[IN_SMEM],
        out_specs=IN_VMEM,
        out_shape=shape((subs, columns), F32),
        compiler_params=params(),
        cost_estimate=cost(64 * subs * columns, 4 * subs * columns),
    )(place)


def add_rows(scores, bias):
    return jnp.concatenate(
        [scores[i * BLOCK : (i + 1) * BLOCK] + row for i, row in enumerate(bias)], axis=0
    )


def far_update(queries, keys, values, bias, state):
    scores = add_rows(dot_t(queries, keys), bias)
    peak, total, gathered = state
    higher = jnp.maximum(peak, jnp.max(scores, axis=1, keepdims=True))
    shrink = jnp.exp2((peak - higher) * SCALE)
    weight = jnp.exp2((scores - higher) * SCALE)
    total = total * shrink + jnp.sum(weight, axis=1, keepdims=True)
    return higher, total, gathered * shrink + dot(weight.astype(BF16), values)


def far_group(refs, head):
    return [
        jnp.concatenate(
            [ref[step, slot, head] for ref in refs for step in range(GROUP // 2)], axis=0
        )
        for slot in range(2)
    ]


def attend_kernel(relative, near, halves, few, finish, bias, *refs):
    refs = list(refs)
    queries = refs.pop(0)
    if near:
        keys, values = refs[0:4], refs[4:8]
        del refs[:8]
    else:
        gathered_in, stats_in = refs[0:2]
        del refs[:2]
    far = []
    for half in halves:
        size = 2 if few else 1
        far.append((half, refs[:size]))
        del refs[:size]
    span = bias.shape[0] * BLOCK
    half_count = (bias.shape[1] - span) * BLOCKS_HALF // bias.shape[0]

    def rows_of_bias(columns):
        return [bias[r : r + 1, columns] for r in relative]

    def one_head(head, _):
        columns = pl.ds(pl.multiple_of(head * HEAD_SIZE, HEAD_SIZE), HEAD_SIZE)
        asked = queries[:, columns]
        if near:
            near_keys = jnp.concatenate([ref[:, columns] for ref in keys], axis=0)
            near_values = jnp.concatenate([ref[:, columns] for ref in values], axis=0)
            scores = add_rows(dot_t(asked, near_keys), rows_of_bias(slice(0, span)))
            peak = jnp.max(scores, axis=1, keepdims=True)
            weight = jnp.exp2((scores - peak) * SCALE)
            total = jnp.sum(weight, axis=1, keepdims=True)
            state = peak, total, dot(weight.astype(BF16), near_values)
        else:
            state = stats_in[head, :, 0:1], stats_in[head, :, 1:2], gathered_in[:, columns]
        for half, parts in far:
            start = span + half * half_count
            if few:
                group = far_group(parts, head)
                rows = rows_of_bias(slice(start, start + half_count))
                state = far_update(asked, *group, rows, state)
                continue

            def step(number, state, start=start, part=parts[0]):
                base = number * GROUP
                group = [
                    jnp.concatenate([part[base + i, slot, head] for i in range(GROUP)], axis=0)
                    for slot in range(2)
                ]
                width = GROUP * FAR_ROWS
                rows = rows_of_bias(pl.ds(pl.multiple_of(start + number * width, width), width))
                return far_update(asked, *group, rows, state)

            state = lax.fori_loop(0, parts[0].shape[0] // GROUP, step, state)
        peak, total, gathered = state
        if finish:
            keep, send = refs
            context = (gathered / total).astype(BF16)
            keep[:, columns] = context[:BLOCK]
            send[:, columns] = context[BLOCK:]
        else:
            gathered_out, stats_out = refs
            gathered_out[:, columns] = gathered
            lane = lax.broadcasted_iota(jnp.int32, gathered.shape, 1)
            stats_out[head] = jnp.where(lane == 0, peak, total)
        return 0

    lax.fori_loop(0, queries.shape[1] // HEAD_SIZE, one_head, 0)


def attend(bias, few, relative, queries, halves, near=None, begun=None, finish=True):
    rows, width = queries.shape
    heads = width // HEAD_SIZE
    operands = [queries]
    operands += [*near[0], *near[1]] if near else list(begun)
    columns = bias.shape[0] * BLOCK if near else 0
    for _, parts in halves:
        operands += parts
    far_bytes = sum(2 * part.size for _, parts in halves for part in parts)
    spans = far_bytes // (4 * FAR_ROWS * width)
    columns += spans * FAR_ROWS
    if finish:
        out_shape = [shape((BLOCK, width))] * 2
    else:
        out_shape = [shape((rows, width), F32), shape((heads, rows, HEAD_SIZE), F32)]
    return pl.pallas_call(
        functools.partial(
            attend_kernel, relative, near is not None, [half[0] for half in halves], few, finish
        ),
        in_specs=[IN_VMEM] * (1 + len(operands)),
        out_specs=[IN_VMEM] * 2,
        out_shape=out_shape,
        compiler_params=params(far_bytes),
        cost_estimate=cost(
            4 * rows * columns * width, 4 * rows * width, heads * rows * columns
        ),
    )(bias, *operands)


def mix_kernel(rows_0, rows_1, weight_0, weight_1, out):
    tile = min(512, out.shape[1])
    for index in range(out.shape[1] // tile):
        part = slice(index * tile, (index + 1) * tile)
        total = dot(rows_0[...], weight_0[:, part]) + dot(rows_1[...], weight_1[:, part])
        out[:, part] = total.astype(out.dtype)


def mix(rows_0, rows_1, weight_0, weight_1, dtype):
    rows, depth = rows_0.shape
    width = weight_0.shape[1]
    return pl.pallas_call(
        mix_kernel,
        in_specs=[IN_VMEM] * 4,
        out_specs=IN_VMEM,
        out_shape=shape((rows, width), dtype),
        compiler_params=params(),
        cost_estimate=cost(4 * rows * depth * width, 4 * rows * width),
    )(rows_0, rows_1, weight_0, weight_1)


def shards(seqs, subs, normed, w_query, w_key, w_value, w_out, pattern, slide_lengths):
    slides = slide_lengths.shape[0]
    axes = [lax.axis_index(name).astype(jnp.int32)[None] for name in ("seq", "sub")]
    few = seqs == GROUP

    def swap(array, bit, axis="sub"):
        count = subs if axis == "sub" else seqs
        return lax.ppermute(array, axis, [(i, i ^ bit) for i in range(count)])

    def after(array, *others):
        return lax.optimization_barrier((array, *others))[0]

    def first_round(kept):
        return [swap(kept, bit, "seq") for bit in Z_BITS]

    def second_round(kept, along_z):
        column = jnp.stack([kept, *along_z])
        return [column, swap(column, Y_BIT, "seq")]

    across = swap(normed, 2)
    beside = swap(normed, 1)
    mine, wk, wv, keys_0, values_0 = first(normed, w_key, w_value)
    keys_1, values_1, kept_a = second(beside, wk, wv, keys_0, values_0, pattern)
    place = jnp.concatenate([after(slide_lengths, kept_a), *axes])
    bias = make_bias(place, slides, subs, seqs, few)
    query_a, wq, wo = query_first(mine, beside, w_query, w_out)
    wo_beside = swap(w_out, 1)
    if few:
        along_z = first_round(kept_a)
        *along_z, query_a, bias = lax.optimization_barrier((*along_z, query_a, bias))
        half_a = 0, second_round(kept_a, along_z)
        across = after(across, half_a[1][0], wo_beside)
    else:
        half_a = 0, [lax.all_gather(kept_a, "seq", axis=0)]
    wo_beside = pltpu.with_memory_space_constraint(wo_beside, pltpu.VMEM)
    beyond = swap(across, 1)
    keys_2, values_2 = keys_and_values(across, wk, wv)
    keys_3, values_3, kept_b = second(after(beyond, keys_2), wk, wv, keys_2, values_2, pattern)
    query_b = query(across, beyond, wq)
    if few:
        along_z = first_round(kept_b)
        *along_z, query_b, half_a[1][1] = lax.optimization_barrier(
            (*along_z, query_b, half_a[1][1])
        )
        half_b = 1, second_round(kept_b, along_z)
        asked = after(query_b, half_b[1][0])
    else:
        half_b = 1, [lax.all_gather(kept_b, "seq", axis=0)]
        asked = query_b
    near = [keys_0, keys_1, keys_2, keys_3], [values_0, values_1, values_2, values_3]
    call = functools.partial(attend, bias, few)
    begun = call((2, 3), asked, [half_a], near=near, finish=False)
    keep_b, send_b = call((2, 3), query_b, [half_b], begun=begun)
    other_b = swap(send_b, 1)
    leaving = mix(keep_b, other_b, wo, wo_beside, BF16)
    arriving = swap(leaving, 2)
    query_a = after(query_a, leaving)
    keep_a, send_a = call((0, 1), query_a, [half_a, half_b], near=near)
    other_a = swap(send_a, 1)
    own = mix(keep_a, other_a, wo, wo_beside, F32)
    return (own + arriving.astype(F32)).astype(BF16)


def solution(mesh):
    placed = (
        P(("seq", "sub"), None),
        P(None, "sub"),
        P(None, "sub"),
        P(None, "sub"),
        P("sub", None),
        P("sub", None),
        P(),
    )
    return jax.shard_map(
        functools.partial(shards, mesh.shape["seq"], mesh.shape["sub"]),
        mesh=mesh,
        in_specs=placed,
        out_specs=P(("seq", "sub"), None),
        check_vma=False,
    )
```

```python
import functools
import math

import jax
import jax.numpy as jnp
from jax import lax
from jax.experimental import pallas as pl
from jax.experimental.pallas import tpu as pltpu
from jax.sharding import PartitionSpec as P

HEAD_SIZE = 128
BLOCK = 128
DILATED_KEPT = 16
BLOCKS_HALF = 2
FAR_ROWS = BLOCKS_HALF * DILATED_KEPT
GROUP = 8
HIDDEN = -1e30
SCALE = math.log2(math.e) / math.sqrt(HEAD_SIZE)
BF16 = jnp.bfloat16
F32 = jnp.float32
IN_VMEM = pl.BlockSpec(memory_space=pltpu.VMEM)
IN_HBM = pl.BlockSpec(memory_space=pltpu.HBM)
IN_SMEM = pl.BlockSpec(memory_space=pltpu.SMEM)
Y_BIT = 1
Z_BITS = (4, 6, 2)


def dot(a, b):
    return jnp.dot(a, b, preferred_element_type=F32)


def dot_t(a, b):
    return lax.dot_general(a, b, (((1,), (1,)), ((), ())), preferred_element_type=F32)


def params(extra=0):
    return pltpu.CompilerParams(vmem_limit_bytes=16 * 2**20 + extra)


def cost(flops, bytes_accessed, transcendentals=0):
    return pl.CostEstimate(
        flops=flops // 100,
        bytes_accessed=bytes_accessed // 100,
        transcendentals=transcendentals // 100,
    )


def shape(dims, dtype=BF16):
    return jax.ShapeDtypeStruct(tuple(dims), dtype)


def keep_in_hbm(array):
    return pltpu.with_memory_space_constraint(array, pltpu.HBM)


def halves_of(width):
    tile = min(256, width)
    return [slice(i * tile, (i + 1) * tile) for i in range(width // tile)]


def pick_dilated(pattern, blocks, kept):
    positions = lax.broadcasted_iota(jnp.int32, (BLOCK, BLOCK), 0)
    for head in range(kept.shape[1]):
        row = pattern[head : head + 1, :]
        chosen = (positions == row).astype(F32).T[:DILATED_KEPT].astype(BF16)
        for index, block in enumerate(blocks):
            picked = dot(chosen, jnp.concatenate(block(head), axis=1)).astype(BF16)
            spot = slice(index * DILATED_KEPT, (index + 1) * DILATED_KEPT)
            kept[0, head, spot, :] = picked[:, :HEAD_SIZE]
            kept[1, head, spot, :] = picked[:, HEAD_SIZE:]


def head_of(ref, head, rows=slice(None)):
    return ref[rows, head * HEAD_SIZE : (head + 1) * HEAD_SIZE]


def first_kernel(rows_hbm, wk_hbm, wv_hbm, rows, wk, wv, keys, values, sems):
    parts = halves_of(wk.shape[1])
    whole = pltpu.make_async_copy(rows_hbm, rows, sems.at[0])
    whole.start()
    copies = []
    for index, part in enumerate(parts):
        for side, (source, target) in enumerate(((wk_hbm, wk), (wv_hbm, wv))):
            copy = pltpu.make_async_copy(
                source.at[:, part], target.at[:, part], sems.at[1 + 2 * index + side]
            )
            copy.start()
            copies.append((copy, target, part, (keys, values)[side]))
    whole.wait()
    for copy, weight, part, out in copies:
        copy.wait()
        out[:, part] = dot(rows[...], weight[:, part]).astype(BF16)


def first(rows, w_key, w_value):
    count, depth = rows.shape
    width = w_key.shape[1]
    return pl.pallas_call(
        first_kernel,
        in_specs=[IN_HBM] * 3,
        out_specs=[IN_VMEM] * 5,
        out_shape=[
            pltpu.VMEM(rows.shape, BF16),
            pltpu.VMEM(w_key.shape, BF16),
            pltpu.VMEM(w_value.shape, BF16),
            shape((count, width)),
            shape((count, width)),
        ],
        scratch_shapes=[pltpu.SemaphoreType.DMA((1 + 2 * len(halves_of(width)),))],
        compiler_params=params(),
        cost_estimate=cost(4 * count * depth * width, 4 * depth * width),
    )(keep_in_hbm(rows), keep_in_hbm(w_key), keep_in_hbm(w_value))


def second_kernel(rows, wk, wv, keys_0, values_0, pattern, keys, values, kept):
    for part in halves_of(wk.shape[1]):
        keys[:, part] = dot(rows[...], wk[:, part]).astype(BF16)
        values[:, part] = dot(rows[...], wv[:, part]).astype(BF16)
    blocks = [
        lambda head: (head_of(keys_0, head), head_of(values_0, head)),
        lambda head: (head_of(keys, head), head_of(values, head)),
    ]
    pick_dilated(pattern, blocks, kept)


def second(rows, wk, wv, keys_0, values_0, pattern):
    count, depth = rows.shape
    width = wk.shape[1]
    kept = (2, width // HEAD_SIZE, FAR_ROWS, HEAD_SIZE)
    return pl.pallas_call(
        second_kernel,
        in_specs=[IN_VMEM] * 6,
        out_specs=[IN_VMEM] * 3,
        out_shape=[shape((count, width))] * 2 + [shape(kept)],
        compiler_params=params(),
        cost_estimate=cost(4 * count * depth * width, 2 * count * depth),
    )(rows, wk, wv, keys_0, values_0, pattern)


def query_first_kernel(rows_0, rows_1, wq_hbm, w_hbm, queries, wq, w, sems):
    parts = halves_of(wq.shape[1])
    copies = [
        pltpu.make_async_copy(wq_hbm.at[:, part], wq.at[:, part], sems.at[index])
        for index, part in enumerate(parts)
    ]
    copies.append(pltpu.make_async_copy(w_hbm, w, sems.at[len(parts)]))
    for copy in copies:
        copy.start()
    rows = jnp.concatenate([rows_0[...], rows_1[...]], axis=0)
    for part, copy in zip(parts, copies):
        copy.wait()
        queries[:, part] = dot(rows, wq[:, part]).astype(BF16)
    copies[-1].wait()


def query_first(rows_0, rows_1, w_query, w_out):
    count, depth = rows_0.shape
    width = w_query.shape[1]
    return pl.pallas_call(
        query_first_kernel,
        in_specs=[IN_VMEM] * 2 + [IN_HBM] * 2,
        out_specs=[IN_VMEM] * 3,
        out_shape=[
            shape((2 * count, width)),
            pltpu.VMEM(w_query.shape, BF16),
            pltpu.VMEM(w_out.shape, BF16),
        ],
        scratch_shapes=[pltpu.SemaphoreType.DMA((1 + len(halves_of(width)),))],
        compiler_params=params(),
        cost_estimate=cost(4 * count * depth * width, 4 * depth * width),
    )(rows_0, rows_1, keep_in_hbm(w_query), keep_in_hbm(w_out))


def query_kernel(rows_0, rows_1, wq, queries):
    rows = jnp.concatenate([rows_0[...], rows_1[...]], axis=0)
    for part in halves_of(wq.shape[1]):
        queries[:, part] = dot(rows, wq[:, part]).astype(BF16)


def query(rows_0, rows_1, wq):
    count, depth = rows_0.shape
    width = wq.shape[1]
    return pl.pallas_call(
        query_kernel,
        in_specs=[IN_VMEM] * 3,
        out_specs=IN_VMEM,
        out_shape=shape((2 * count, width)),
        compiler_params=params(),
        cost_estimate=cost(4 * count * depth * width, 4 * count * depth),
    )(rows_0, rows_1, wq)


def across_kernel(rows, wk, wv, keys, values):
    for part in halves_of(wk.shape[1]):
        keys[:, part] = dot(rows[...], wk[:, part]).astype(BF16)
        values[:, part] = dot(rows[...], wv[:, part]).astype(BF16)


def keys_and_values(rows, wk, wv):
    count, depth = rows.shape
    width = wk.shape[1]
    return pl.pallas_call(
        across_kernel,
        in_specs=[IN_VMEM] * 3,
        out_specs=[IN_VMEM] * 2,
        out_shape=[shape((count, width))] * 2,
        compiler_params=params(),
        cost_estimate=cost(4 * count * depth * width, 2 * count * depth),
    )(rows, wk, wv)


def slide_of(place, slides, block):
    end, total = jnp.int32(0), jnp.zeros_like(block)
    for index in range(slides):
        end = end + place[index]
        total = total + (block >= end).astype(jnp.int32)
    return total


def mask_kernel(slides, subs, spans, few, place, asking, asked):
    span, sub = place[slides], place[slides + 1]
    slide = [slide_of(place, slides, span * subs + (sub ^ r)) for r in range(subs)]
    lane = lax.broadcasted_iota(jnp.int32, (BLOCK, HEAD_SIZE), 1)
    for r in range(subs):
        rows = slice(r * BLOCK, (r + 1) * BLOCK)
        apart = (lane <= slides) & (lane != slide[r])
        asking[rows, :] = jnp.where(apart, HIDDEN, 0.0).astype(BF16)
        asked[rows, :] = jnp.where(lane == slide[r], 1.0, 0.0).astype(BF16)
    count = min(spans, GROUP) * FAR_ROWS
    row = lax.broadcasted_iota(jnp.int32, (count, HEAD_SIZE), 0)
    lane = lax.broadcasted_iota(jnp.int32, (count, HEAD_SIZE), 1)
    upper = (row // DILATED_KEPT) % BLOCKS_HALF
    for half in range(subs // BLOCKS_HALF):
        place_0, place_1 = sub ^ (half * BLOCKS_HALF), sub ^ (half * BLOCKS_HALF + 1)
        for group in range(spans * FAR_ROWS // count):
            far = row // FAR_ROWS
            if few:
                order = [bit | y for y in (0, Y_BIT) for bit in (0, *Z_BITS)]
                place_of = jnp.zeros_like(far)
                for index, bits in enumerate(order):
                    place_of = jnp.where(far == index, bits, place_of)
                far = place_of ^ span
            else:
                far = far + group * GROUP
            theirs = slide_of(place, slides, far * subs + jnp.where(upper == 0, place_0, place_1))
            marked = (lane == theirs) | ((lane == slides) & (far == span))
            start = subs * BLOCK + (half * spans * FAR_ROWS + group * count)
            asked[start : start + count, :] = jnp.where(marked, 1.0, 0.0).astype(BF16)


def make_masks(place, slides, subs, spans, few):
    keys = subs * BLOCK + subs // BLOCKS_HALF * spans * FAR_ROWS
    return pl.pallas_call(
        functools.partial(mask_kernel, slides, subs, spans, few),
        in_specs=[IN_SMEM],
        out_specs=[IN_VMEM] * 2,
        out_shape=[shape((subs * BLOCK, HEAD_SIZE)), shape((keys, HEAD_SIZE))],
        compiler_params=params(),
        cost_estimate=cost(64 * keys * HEAD_SIZE, 2 * keys * HEAD_SIZE),
    )(place)


def scores_of(keys, queries):
    return dot_t(keys, queries)


def gather(values, weight):
    return lax.dot_general(
        values, weight.astype(BF16), (((0,), (0,)), ((), ())), preferred_element_type=F32
    )


def begin(queries, keys, values):
    scores = scores_of(keys, queries)
    peak = jnp.max(scores, axis=0, keepdims=True)
    weight = jnp.exp2((scores - peak) * SCALE)
    return peak, jnp.sum(weight, axis=0, keepdims=True), gather(values, weight)


def update(queries, keys, values, state):
    peak, total, gathered = state
    scores = scores_of(keys, queries)
    higher = jnp.maximum(peak, jnp.max(scores, axis=0, keepdims=True))
    shrink = jnp.exp2((peak - higher) * SCALE)
    weight = jnp.exp2((scores - higher) * SCALE)
    total = total * shrink + jnp.sum(weight, axis=0, keepdims=True)
    return higher, total, gathered * shrink + gather(values, weight)


def attend_kernel(first_row, near, halves, few, finish, asking, asked_of, *refs):
    refs = list(refs)
    queries = refs.pop(0)
    if near:
        keys, values = refs[0:4], refs[4:8]
        del refs[:8]
    else:
        gathered_in, stats_in = refs[0:2]
        del refs[:2]
    far = []
    for half, size in halves:
        far.append((half, refs[:size]))
        del refs[:size]
    rows = queries.shape[0]
    span = asking.shape[0]
    half_count = (asked_of.shape[0] - span) // BLOCKS_HALF

    def one_head(head, _):
        columns = pl.ds(pl.multiple_of(head * HEAD_SIZE, HEAD_SIZE), HEAD_SIZE)
        asked = jnp.concatenate(
            [queries[:, columns], asking[first_row : first_row + rows, :]], axis=1
        )

        def marked(parts, where):
            return jnp.concatenate([jnp.concatenate(parts, axis=0), asked_of[where, :]], axis=1)

        keyed, valued = [], []
        if near:
            keyed.append(marked([ref[:, columns] for ref in keys], slice(0, span)))
            valued += [ref[:, columns] for ref in values]
        if few:
            for half, parts in far:
                start = span + half * half_count
                pieces = [(ref, i) for ref in parts for i in range(ref.shape[0])]
                keyed.append(
                    marked([ref[i, 0, head] for ref, i in pieces], slice(start, start + half_count))
                )
                valued += [ref[i, 1, head] for ref, i in pieces]
        if near:
            ready = asked, jnp.concatenate(keyed, axis=0), jnp.concatenate(valued, axis=0)
            state = begin(*ready)
        else:
            state = stats_in[head, 0:1, :], stats_in[head, 1:2, :], gathered_in[head]
            if few:
                ready = asked, jnp.concatenate(keyed, axis=0), jnp.concatenate(valued, axis=0)
                state = update(*ready, state)
        if not few:
            for half, (part,) in far:
                start = span + half * half_count

                def step(number, state, start=start, part=part):
                    base = number * GROUP
                    width = GROUP * FAR_ROWS
                    where = pl.ds(pl.multiple_of(start + number * width, width), width)
                    keyed = marked([part[base + i, 0, head] for i in range(GROUP)], where)
                    valued = jnp.concatenate([part[base + i, 1, head] for i in range(GROUP)], axis=0)
                    return update(asked, keyed, valued, state)

                state = lax.fori_loop(0, part.shape[0] // GROUP, step, state)
        peak, total, gathered = state
        if finish:
            keep, send = refs
            context = (gathered / total).T.astype(BF16)
            keep[:, columns] = context[:BLOCK]
            send[:, columns] = context[BLOCK:]
        else:
            gathered_out, stats_out = refs
            gathered_out[head] = gathered
            stats_out[head, 0:1, :] = peak
            stats_out[head, 1:2, :] = total
        return 0

    lax.fori_loop(0, queries.shape[1] // HEAD_SIZE, one_head, 0)


def attend(masks, few, first_row, queries, halves, near=None, begun=None, finish=True):
    rows, width = queries.shape
    heads = width // HEAD_SIZE
    operands = [*masks, queries]
    operands += [*near[0], *near[1]] if near else list(begun)
    columns = masks[0].shape[0] if near else 0
    for _, parts in halves:
        operands += parts
    far_bytes = sum(2 * part.size for _, parts in halves for part in parts)
    columns += far_bytes // (4 * width)
    if finish:
        out_shape = [shape((BLOCK, width))] * 2
    else:
        out_shape = [shape((heads, HEAD_SIZE, rows), F32), shape((heads, 8, rows), F32)]
    return pl.pallas_call(
        functools.partial(
            attend_kernel,
            first_row,
            near is not None,
            [(half, len(parts)) for half, parts in halves],
            few,
            finish,
        ),
        in_specs=[IN_VMEM] * len(operands),
        out_specs=[IN_VMEM] * 2,
        out_shape=out_shape,
        compiler_params=params(far_bytes),
        cost_estimate=cost(
            4 * rows * columns * width, 4 * rows * width, heads * rows * columns
        ),
    )(*operands)


def mix_kernel(rows_0, rows_1, weight_0, weight_1, out):
    tile = min(512, out.shape[1])
    for index in range(out.shape[1] // tile):
        part = slice(index * tile, (index + 1) * tile)
        total = dot(rows_0[...], weight_0[:, part]) + dot(rows_1[...], weight_1[:, part])
        out[:, part] = total.astype(out.dtype)


def mix(rows_0, rows_1, weight_0, weight_1, dtype):
    rows, depth = rows_0.shape
    width = weight_0.shape[1]
    return pl.pallas_call(
        mix_kernel,
        in_specs=[IN_VMEM] * 4,
        out_specs=IN_VMEM,
        out_shape=shape((rows, width), dtype),
        compiler_params=params(),
        cost_estimate=cost(4 * rows * depth * width, 4 * rows * width),
    )(rows_0, rows_1, weight_0, weight_1)


def shards(seqs, subs, normed, w_query, w_key, w_value, w_out, pattern, slide_lengths):
    slides = slide_lengths.shape[0]
    axes = [lax.axis_index(name).astype(jnp.int32)[None] for name in ("seq", "sub")]
    few = seqs == GROUP

    def swap(array, bit, axis="sub"):
        count = subs if axis == "sub" else seqs
        return lax.ppermute(array, axis, [(i, i ^ bit) for i in range(count)])

    def after(array, *others):
        return lax.optimization_barrier((array, *others))[0]

    def first_round(kept):
        return [swap(kept, bit, "seq") for bit in Z_BITS]

    def second_round(kept, along_z):
        column = jnp.stack([kept, *along_z])
        return [column, swap(column, Y_BIT, "seq")]

    across = swap(normed, 2)
    beside = swap(normed, 1)
    mine, wk, wv, keys_0, values_0 = first(normed, w_key, w_value)
    keys_1, values_1, kept_a = second(beside, wk, wv, keys_0, values_0, pattern)
    place = jnp.concatenate([after(slide_lengths, kept_a), *axes])
    masks = list(make_masks(place, slides, subs, seqs, few))
    query_a, wq, wo = query_first(mine, beside, w_query, w_out)
    wo_beside = swap(w_out, 1)
    if few:
        along_z = first_round(kept_a)
        *along_z, query_a, masks[0] = lax.optimization_barrier((*along_z, query_a, masks[0]))
        half_a = 0, second_round(kept_a, along_z)
        across = after(across, half_a[1][0], wo_beside)
    else:
        half_a = 0, [lax.all_gather(kept_a, "seq", axis=0)]
    wo_beside = pltpu.with_memory_space_constraint(wo_beside, pltpu.VMEM)
    beyond = swap(across, 1)
    keys_2, values_2 = keys_and_values(across, wk, wv)
    keys_3, values_3, kept_b = second(after(beyond, keys_2), wk, wv, keys_2, values_2, pattern)
    query_b = query(across, beyond, wq)
    near = [keys_0, keys_1, keys_2, keys_3], [values_0, values_1, values_2, values_3]
    call = functools.partial(attend, masks, few)
    if few:
        two, *along_z = first_round(kept_b)
        two, query_b, half_a[1][1] = lax.optimization_barrier((two, query_b, half_a[1][1]))
        soon = second_round(kept_b, [two])
        *along_z, soon[1] = lax.optimization_barrier((*along_z, soon[1]))
        late = second_round(along_z[0], along_z[1:])
        asked = after(query_b, late[0])
        half_b = 1, [soon[0], late[0], soon[1], late[1]]
        begun = call(2 * BLOCK, asked, [half_a], near=near, finish=False)
    else:
        half_b = 1, [lax.all_gather(kept_b, "seq", axis=0)]
        begun = call(2 * BLOCK, query_b, [half_a], near=near, finish=False)
    keep_b, send_b = call(2 * BLOCK, query_b, [half_b], begun=begun)
    other_b = swap(send_b, 1)
    leaving = mix(keep_b, other_b, wo, wo_beside, BF16)
    arriving = swap(leaving, 2)
    query_a = after(query_a, leaving)
    keep_a, send_a = call(0, query_a, [half_a, half_b], near=near)
    other_a = swap(send_a, 1)
    own = mix(keep_a, other_a, wo, wo_beside, F32)
    return (own + arriving.astype(F32)).astype(BF16)


def solution(mesh):
    placed = (
        P(("seq", "sub"), None),
        P(None, "sub"),
        P(None, "sub"),
        P(None, "sub"),
        P("sub", None),
        P("sub", None),
        P(),
    )
    return jax.shard_map(
        functools.partial(shards, mesh.shape["seq"], mesh.shape["sub"]),
        mesh=mesh,
        in_specs=placed,
        out_specs=P(("seq", "sub"), None),
        check_vma=False,
    )
```

```python
import functools
import math

import jax
import jax.numpy as jnp
from jax import lax
from jax.experimental import pallas as pl
from jax.experimental.pallas import tpu as pltpu
from jax.sharding import PartitionSpec as P

HEAD_SIZE = 128
BLOCK = 128
DILATED_KEPT = 16
BLOCKS_HALF = 2
FAR_ROWS = BLOCKS_HALF * DILATED_KEPT
GROUP = 8
HIDDEN = -1e30
SCALE = math.log2(math.e) / math.sqrt(HEAD_SIZE)
BF16 = jnp.bfloat16
F32 = jnp.float32
IN_VMEM = pl.BlockSpec(memory_space=pltpu.VMEM)
IN_HBM = pl.BlockSpec(memory_space=pltpu.HBM)
IN_SMEM = pl.BlockSpec(memory_space=pltpu.SMEM)
Y_BIT = 1
Z_BITS = (4, 6, 2)


def dot(a, b):
    return jnp.dot(a, b, preferred_element_type=F32)


def dot_t(a, b):
    return lax.dot_general(a, b, (((1,), (1,)), ((), ())), preferred_element_type=F32)


def params(extra=0):
    return pltpu.CompilerParams(vmem_limit_bytes=16 * 2**20 + extra)


def cost(flops, bytes_accessed, transcendentals=0):
    return pl.CostEstimate(
        flops=flops // 100,
        bytes_accessed=bytes_accessed // 100,
        transcendentals=transcendentals // 100,
    )


def shape(dims, dtype=BF16):
    return jax.ShapeDtypeStruct(tuple(dims), dtype)


def keep_in_hbm(array):
    return pltpu.with_memory_space_constraint(array, pltpu.HBM)


def halves_of(width):
    tile = min(256, width)
    return [slice(i * tile, (i + 1) * tile) for i in range(width // tile)]


def pick_dilated(pattern, blocks, kept):
    positions = lax.broadcasted_iota(jnp.int32, (BLOCK, BLOCK), 0)
    for head in range(kept.shape[1]):
        row = pattern[head : head + 1, :]
        chosen = (positions == row).astype(F32).T[:DILATED_KEPT].astype(BF16)
        for index, block in enumerate(blocks):
            picked = dot(chosen, jnp.concatenate(block(head), axis=1)).astype(BF16)
            spot = slice(index * DILATED_KEPT, (index + 1) * DILATED_KEPT)
            kept[0, head, spot, :] = picked[:, :HEAD_SIZE]
            kept[1, head, spot, :] = picked[:, HEAD_SIZE:]


def head_of(ref, head, rows=slice(None)):
    return ref[rows, head * HEAD_SIZE : (head + 1) * HEAD_SIZE]


def first_kernel(rows_hbm, wk_hbm, wv_hbm, rows, wk, wv, keys, values, sems):
    parts = halves_of(wk.shape[1])
    whole = pltpu.make_async_copy(rows_hbm, rows, sems.at[0])
    whole.start()
    copies = []
    for index, part in enumerate(parts):
        for side, (source, target) in enumerate(((wk_hbm, wk), (wv_hbm, wv))):
            copy = pltpu.make_async_copy(
                source.at[:, part], target.at[:, part], sems.at[1 + 2 * index + side]
            )
            copy.start()
            copies.append((copy, target, part, (keys, values)[side]))
    whole.wait()
    for copy, weight, part, out in copies:
        copy.wait()
        out[:, part] = dot(rows[...], weight[:, part]).astype(BF16)


def first(rows, w_key, w_value):
    count, depth = rows.shape
    width = w_key.shape[1]
    return pl.pallas_call(
        first_kernel,
        in_specs=[IN_HBM] * 3,
        out_specs=[IN_VMEM] * 5,
        out_shape=[
            pltpu.VMEM(rows.shape, BF16),
            pltpu.VMEM(w_key.shape, BF16),
            pltpu.VMEM(w_value.shape, BF16),
            shape((count, width)),
            shape((count, width)),
        ],
        scratch_shapes=[pltpu.SemaphoreType.DMA((1 + 2 * len(halves_of(width)),))],
        compiler_params=params(),
        cost_estimate=cost(4 * count * depth * width, 4 * depth * width),
    )(keep_in_hbm(rows), keep_in_hbm(w_key), keep_in_hbm(w_value))


def second_kernel(rows, wk, wv, keys_0, values_0, pattern, keys, values, kept):
    for part in halves_of(wk.shape[1]):
        keys[:, part] = dot(rows[...], wk[:, part]).astype(BF16)
        values[:, part] = dot(rows[...], wv[:, part]).astype(BF16)
    blocks = [
        lambda head: (head_of(keys_0, head), head_of(values_0, head)),
        lambda head: (head_of(keys, head), head_of(values, head)),
    ]
    pick_dilated(pattern, blocks, kept)


def second(rows, wk, wv, keys_0, values_0, pattern):
    count, depth = rows.shape
    width = wk.shape[1]
    kept = (2, width // HEAD_SIZE, FAR_ROWS, HEAD_SIZE)
    return pl.pallas_call(
        second_kernel,
        in_specs=[IN_VMEM] * 6,
        out_specs=[IN_VMEM] * 3,
        out_shape=[shape((count, width))] * 2 + [shape(kept)],
        compiler_params=params(),
        cost_estimate=cost(4 * count * depth * width, 2 * count * depth),
    )(rows, wk, wv, keys_0, values_0, pattern)


def query_kernel(*refs):
    rows, (wq_hbm, w_hbm), outs, (wq, sems) = refs[:4], refs[4:6], refs[6:9], refs[9:]
    w = outs[2]
    parts = halves_of(wq.shape[1])
    copies = [
        pltpu.make_async_copy(wq_hbm.at[:, part], wq.at[:, part], sems.at[index])
        for index, part in enumerate(parts)
    ]
    copies.append(pltpu.make_async_copy(w_hbm, w, sems.at[len(parts)]))
    for copy in copies:
        copy.start()
    for part, copy in zip(parts, copies):
        copy.wait()
        for pair, out in ((rows[:2], outs[0]), (rows[2:], outs[1])):
            both = jnp.concatenate([ref[...] for ref in pair], axis=0)
            out[:, part] = dot(both, wq[:, part]).astype(BF16)
    copies[-1].wait()


def query(rows, w_query, w_out):
    count, depth = rows[0].shape
    width = w_query.shape[1]
    return pl.pallas_call(
        query_kernel,
        in_specs=[IN_VMEM] * 4 + [IN_HBM] * 2,
        out_specs=[IN_VMEM] * 3,
        out_shape=[shape((2 * count, width))] * 2 + [pltpu.VMEM(w_out.shape, BF16)],
        scratch_shapes=[
            pltpu.VMEM(w_query.shape, BF16),
            pltpu.SemaphoreType.DMA((1 + len(halves_of(width)),)),
        ],
        compiler_params=params(),
        cost_estimate=cost(8 * count * depth * width, 4 * depth * width),
    )(*rows, keep_in_hbm(w_query), keep_in_hbm(w_out))


def across_kernel(rows, wk, wv, keys, values):
    for part in halves_of(wk.shape[1]):
        keys[:, part] = dot(rows[...], wk[:, part]).astype(BF16)
        values[:, part] = dot(rows[...], wv[:, part]).astype(BF16)


def keys_and_values(rows, wk, wv):
    count, depth = rows.shape
    width = wk.shape[1]
    return pl.pallas_call(
        across_kernel,
        in_specs=[IN_VMEM] * 3,
        out_specs=[IN_VMEM] * 2,
        out_shape=[shape((count, width))] * 2,
        compiler_params=params(),
        cost_estimate=cost(4 * count * depth * width, 2 * count * depth),
    )(rows, wk, wv)


def slide_of(place, slides, block):
    end, total = jnp.int32(0), jnp.zeros_like(block)
    for index in range(slides):
        end = end + place[index]
        total = total + (block >= end).astype(jnp.int32)
    return total


def mask_kernel(slides, subs, spans, few, place, asking, asked):
    span, sub = place[slides], place[slides + 1]
    slide = [slide_of(place, slides, span * subs + (sub ^ r)) for r in range(subs)]
    lane = lax.broadcasted_iota(jnp.int32, (BLOCK, HEAD_SIZE), 1)
    for r in range(subs):
        rows = slice(r * BLOCK, (r + 1) * BLOCK)
        apart = (lane <= slides) & (lane != slide[r])
        asking[rows, :] = jnp.where(apart, HIDDEN, 0.0).astype(BF16)
        asked[rows, :] = jnp.where(lane == slide[r], 1.0, 0.0).astype(BF16)
    count = min(spans, GROUP) * FAR_ROWS
    row = lax.broadcasted_iota(jnp.int32, (count, HEAD_SIZE), 0)
    lane = lax.broadcasted_iota(jnp.int32, (count, HEAD_SIZE), 1)
    upper = (row // DILATED_KEPT) % BLOCKS_HALF
    for half in range(subs // BLOCKS_HALF):
        place_0, place_1 = sub ^ (half * BLOCKS_HALF), sub ^ (half * BLOCKS_HALF + 1)
        for group in range(spans * FAR_ROWS // count):
            far = row // FAR_ROWS
            if few:
                order = [bit | y for y in (0, Y_BIT) for bit in (0, *Z_BITS)]
                place_of = jnp.zeros_like(far)
                for index, bits in enumerate(order):
                    place_of = jnp.where(far == index, bits, place_of)
                far = place_of ^ span
            else:
                far = far + group * GROUP
            theirs = slide_of(place, slides, far * subs + jnp.where(upper == 0, place_0, place_1))
            marked = (lane == theirs) | ((lane == slides) & (far == span))
            start = subs * BLOCK + (half * spans * FAR_ROWS + group * count)
            asked[start : start + count, :] = jnp.where(marked, 1.0, 0.0).astype(BF16)


def make_masks(place, slides, subs, spans, few):
    keys = subs * BLOCK + subs // BLOCKS_HALF * spans * FAR_ROWS
    return pl.pallas_call(
        functools.partial(mask_kernel, slides, subs, spans, few),
        in_specs=[IN_SMEM],
        out_specs=[IN_VMEM] * 2,
        out_shape=[shape((subs * BLOCK, HEAD_SIZE)), shape((keys, HEAD_SIZE))],
        compiler_params=params(),
        cost_estimate=cost(64 * keys * HEAD_SIZE, 2 * keys * HEAD_SIZE),
    )(place)


def scores_of(keys, queries):
    return dot_t(keys, queries)


def gather(values, weight):
    return lax.dot_general(
        values, weight.astype(BF16), (((0,), (0,)), ((), ())), preferred_element_type=F32
    )


def begin(queries, keys, values):
    scores = [scores_of(k, q) for k, q in zip(keys, queries)]
    peak = [jnp.max(each, axis=0, keepdims=True) for each in scores]
    weight = [jnp.exp2((each - top) * SCALE) for each, top in zip(scores, peak)]
    total = [jnp.sum(each, axis=0, keepdims=True) for each in weight]
    return peak, total, [gather(v, each) for v, each in zip(values, weight)]


def update(queries, keys, values, state):
    scores = [scores_of(k, q) for k, q in zip(keys, queries)]
    higher = [
        jnp.maximum(top, jnp.max(each, axis=0, keepdims=True))
        for top, each in zip(state[0], scores)
    ]
    shrink = [jnp.exp2((top - new) * SCALE) for top, new in zip(state[0], higher)]
    weight = [jnp.exp2((each - new) * SCALE) for each, new in zip(scores, higher)]
    total = [
        old * less + jnp.sum(each, axis=0, keepdims=True)
        for old, less, each in zip(state[1], shrink, weight)
    ]
    added = [gather(v, each) for v, each in zip(values, weight)]
    return higher, total, [old * less + new for old, less, new in zip(state[2], shrink, added)]


def attend_kernel(first_row, near, halves, few, finish, asking, asked_of, *refs):
    refs = list(refs)
    queries = refs.pop(0)
    if near:
        keys, values = refs[0:4], refs[4:8]
        del refs[:8]
    else:
        gathered_in, stats_in = refs[0:2]
        del refs[:2]
    far = []
    for half, size in halves:
        far.append((half, refs[:size]))
        del refs[:size]
    rows = queries.shape[0]
    span = asking.shape[0]
    half_count = (asked_of.shape[0] - span) // BLOCKS_HALF

    heads = queries.shape[1] // HEAD_SIZE
    group = heads if few and not near else 1

    def some_heads(turn, _):
        those = [turn * group + i for i in range(group)]
        columns = [
            pl.ds(pl.multiple_of(head * HEAD_SIZE, HEAD_SIZE), HEAD_SIZE)
            if group < heads
            else slice(head * HEAD_SIZE, (head + 1) * HEAD_SIZE)
            for head in those
        ]
        row_marks = asking[first_row : first_row + rows, :]
        asked = [jnp.concatenate([queries[:, each], row_marks], axis=1) for each in columns]

        def marked(parts, where):
            return jnp.concatenate([jnp.concatenate(parts, axis=0), asked_of[where, :]], axis=1)

        def ready(head, each):
            keyed, valued = [], []
            if near:
                keyed.append(marked([ref[:, each] for ref in keys], slice(0, span)))
                valued += [ref[:, each] for ref in values]
            if few:
                for half, parts in far:
                    start = span + half * half_count
                    pieces = [(ref, i) for ref in parts for i in range(ref.shape[0])]
                    where = slice(start, start + half_count)
                    keyed.append(marked([ref[i, 0, head] for ref, i in pieces], where))
                    valued += [ref[i, 1, head] for ref, i in pieces]
            return jnp.concatenate(keyed, axis=0), jnp.concatenate(valued, axis=0)

        if near:
            state = begin(asked, *zip(*map(ready, those, columns)))
        else:
            state = (
                [stats_in[head, 0:1, :] for head in those],
                [stats_in[head, 1:2, :] for head in those],
                [gathered_in[head] for head in those],
            )
            if few:
                state = update(asked, *zip(*map(ready, those, columns)), state)
        if not few:
            for half, (part,) in far:
                start = span + half * half_count

                def step(number, state, start=start, part=part):
                    base = number * GROUP
                    width = GROUP * FAR_ROWS
                    where = pl.ds(pl.multiple_of(start + number * width, width), width)
                    found = [
                        [
                            marked([part[base + i, 0, head] for i in range(GROUP)], where)
                            for head in those
                        ],
                        [
                            jnp.concatenate([part[base + i, 1, head] for i in range(GROUP)], axis=0)
                            for head in those
                        ],
                    ]
                    return update(asked, *found, state)

                state = lax.fori_loop(0, part.shape[0] // GROUP, step, state)
        for head, each, peak, total, gathered in zip(those, columns, *state):
            if finish:
                keep, send = refs
                context = (gathered / total).T.astype(BF16)
                keep[:, each] = context[:BLOCK]
                send[:, each] = context[BLOCK:]
            else:
                gathered_out, stats_out = refs
                gathered_out[head] = gathered
                stats_out[head, 0:1, :] = peak
                stats_out[head, 1:2, :] = total
        return 0

    if group == heads:
        some_heads(0, 0)
    else:
        lax.fori_loop(0, heads // group, some_heads, 0)


def attend(masks, few, first_row, queries, halves, near=None, begun=None, finish=True):
    rows, width = queries.shape
    heads = width // HEAD_SIZE
    operands = [*masks, queries]
    operands += [*near[0], *near[1]] if near else list(begun)
    columns = masks[0].shape[0] if near else 0
    for _, parts in halves:
        operands += parts
    far_bytes = sum(2 * part.size for _, parts in halves for part in parts)
    columns += far_bytes // (4 * width)
    if finish:
        out_shape = [shape((BLOCK, width))] * 2
    else:
        out_shape = [shape((heads, HEAD_SIZE, rows), F32), shape((heads, 8, rows), F32)]
    return pl.pallas_call(
        functools.partial(
            attend_kernel,
            first_row,
            near is not None,
            [(half, len(parts)) for half, parts in halves],
            few,
            finish,
        ),
        in_specs=[IN_VMEM] * len(operands),
        out_specs=[IN_VMEM] * 2,
        out_shape=out_shape,
        compiler_params=params(far_bytes),
        cost_estimate=cost(
            4 * rows * columns * width, 4 * rows * width, heads * rows * columns
        ),
    )(*operands)


def mix_kernel(rows_0, rows_1, weight_0, weight_1, out):
    tile = min(512, out.shape[1])
    for index in range(out.shape[1] // tile):
        part = slice(index * tile, (index + 1) * tile)
        total = dot(rows_0[...], weight_0[:, part]) + dot(rows_1[...], weight_1[:, part])
        out[:, part] = total.astype(out.dtype)


def mix(rows_0, rows_1, weight_0, weight_1, dtype):
    rows, depth = rows_0.shape
    width = weight_0.shape[1]
    return pl.pallas_call(
        mix_kernel,
        in_specs=[IN_VMEM] * 4,
        out_specs=IN_VMEM,
        out_shape=shape((rows, width), dtype),
        compiler_params=params(),
        cost_estimate=cost(4 * rows * depth * width, 4 * rows * width),
    )(rows_0, rows_1, weight_0, weight_1)


def shards(seqs, subs, normed, w_query, w_key, w_value, w_out, pattern, slide_lengths):
    slides = slide_lengths.shape[0]
    axes = [lax.axis_index(name).astype(jnp.int32)[None] for name in ("seq", "sub")]
    few = seqs == GROUP

    def swap(array, bit, axis="sub"):
        count = subs if axis == "sub" else seqs
        return lax.ppermute(array, axis, [(i, i ^ bit) for i in range(count)])

    def after(array, *others):
        return lax.optimization_barrier((array, *others))[0]

    def first_round(kept):
        return [swap(kept, bit, "seq") for bit in Z_BITS]

    def second_round(kept, along_z):
        column = jnp.stack([kept, *along_z])
        return [column, swap(column, Y_BIT, "seq")]

    across = swap(normed, 2)
    beside = swap(normed, 1)
    mine, wk, wv, keys_0, values_0 = first(normed, w_key, w_value)
    keys_1, values_1, kept_a = second(beside, wk, wv, keys_0, values_0, pattern)
    place = jnp.concatenate([after(slide_lengths, kept_a), *axes])
    masks = list(make_masks(place, slides, subs, seqs, few))
    wo_beside = swap(w_out, 1)
    if few:
        along_z = first_round(kept_a)
        *along_z, masks[0] = lax.optimization_barrier((*along_z, masks[0]))
        half_a = 0, second_round(kept_a, along_z)
        across = after(across, half_a[1][0], wo_beside)
    else:
        half_a = 0, [lax.all_gather(kept_a, "seq", axis=0)]
    wo_beside = pltpu.with_memory_space_constraint(wo_beside, pltpu.VMEM)
    beyond = swap(across, 1)
    keys_2, values_2 = keys_and_values(across, wk, wv)
    keys_3, values_3, kept_b = second(after(beyond, keys_2), wk, wv, keys_2, values_2, pattern)
    query_a, query_b, wo = query([mine, beside, across, beyond], w_query, w_out)
    near = [keys_0, keys_1, keys_2, keys_3], [values_0, values_1, values_2, values_3]
    call = functools.partial(attend, masks, few)
    if few:
        along_z = first_round(kept_b)
        *along_z, query_b, half_a[1][1] = lax.optimization_barrier(
            (*along_z, query_b, half_a[1][1])
        )
        half_b = 1, second_round(kept_b, along_z)
        asked = after(query_b, half_b[1][0])
        begun = call(2 * BLOCK, asked, [half_a], near=near, finish=False)
    else:
        half_b = 1, [lax.all_gather(kept_b, "seq", axis=0)]
        begun = call(2 * BLOCK, query_b, [half_a], near=near, finish=False)
    keep_b, send_b = call(2 * BLOCK, query_b, [half_b], begun=begun)
    other_b = swap(send_b, 1)
    leaving = mix(keep_b, other_b, wo, wo_beside, BF16)
    arriving = swap(leaving, 2)
    query_a = after(query_a, leaving)
    keep_a, send_a = call(0, query_a, [half_a, half_b], near=near)
    other_a = swap(send_a, 1)
    own = mix(keep_a, other_a, wo, wo_beside, F32)
    return (own + arriving.astype(F32)).astype(BF16)


def solution(mesh):
    placed = (
        P(("seq", "sub"), None),
        P(None, "sub"),
        P(None, "sub"),
        P(None, "sub"),
        P("sub", None),
        P("sub", None),
        P(),
    )
    return jax.shard_map(
        functools.partial(shards, mesh.shape["seq"], mesh.shape["sub"]),
        mesh=mesh,
        in_specs=placed,
        out_specs=P(("seq", "sub"), None),
        check_vma=False,
    )
```

```python
import functools
import math

import jax
import jax.numpy as jnp
from jax import lax
from jax.experimental import pallas as pl
from jax.experimental.pallas import tpu as pltpu
from jax.sharding import PartitionSpec as P

HEAD_SIZE = 128
BLOCK = 128
DILATED_KEPT = 16
BLOCKS_HALF = 2
FAR_ROWS = BLOCKS_HALF * DILATED_KEPT
GROUP = 8
HIDDEN = -1e30
SCALE = math.log2(math.e) / math.sqrt(HEAD_SIZE)
BF16 = jnp.bfloat16
F32 = jnp.float32
IN_VMEM = pl.BlockSpec(memory_space=pltpu.VMEM)
IN_HBM = pl.BlockSpec(memory_space=pltpu.HBM)
IN_SMEM = pl.BlockSpec(memory_space=pltpu.SMEM)
Y_BIT = 1
Z_BITS = (4, 6, 2)


def dot(a, b):
    return jnp.dot(a, b, preferred_element_type=F32)


def dot_t(a, b):
    return lax.dot_general(a, b, (((1,), (1,)), ((), ())), preferred_element_type=F32)


def params(extra=0):
    return pltpu.CompilerParams(vmem_limit_bytes=16 * 2**20 + extra)


def cost(flops, bytes_accessed, transcendentals=0):
    return pl.CostEstimate(
        flops=flops // 100,
        bytes_accessed=bytes_accessed // 100,
        transcendentals=transcendentals // 100,
    )


def shape(dims, dtype=BF16):
    return jax.ShapeDtypeStruct(tuple(dims), dtype)


def keep_in_hbm(array):
    return pltpu.with_memory_space_constraint(array, pltpu.HBM)


def halves_of(width):
    tile = min(256, width)
    return [slice(i * tile, (i + 1) * tile) for i in range(width // tile)]


def pick_dilated(pattern, blocks, kept):
    positions = lax.broadcasted_iota(jnp.int32, (BLOCK, BLOCK), 0)
    for head in range(kept.shape[1]):
        row = pattern[head : head + 1, :]
        chosen = (positions == row).astype(F32).T[:DILATED_KEPT].astype(BF16)
        for index, block in enumerate(blocks):
            picked = dot(chosen, jnp.concatenate(block(head), axis=1)).astype(BF16)
            spot = slice(index * DILATED_KEPT, (index + 1) * DILATED_KEPT)
            kept[0, head, spot, :] = picked[:, :HEAD_SIZE]
            kept[1, head, spot, :] = picked[:, HEAD_SIZE:]


def head_of(ref, head, rows=slice(None)):
    return ref[rows, head * HEAD_SIZE : (head + 1) * HEAD_SIZE]


def first_kernel(rows_hbm, wk_hbm, wv_hbm, rows, wk, wv, keys, values, sems):
    parts = halves_of(wk.shape[1])
    whole = pltpu.make_async_copy(rows_hbm, rows, sems.at[0])
    whole.start()
    copies = []
    for index, part in enumerate(parts):
        for side, (source, target) in enumerate(((wk_hbm, wk), (wv_hbm, wv))):
            copy = pltpu.make_async_copy(
                source.at[:, part], target.at[:, part], sems.at[1 + 2 * index + side]
            )
            copy.start()
            copies.append((copy, target, part, (keys, values)[side]))
    whole.wait()
    for copy, weight, part, out in copies:
        copy.wait()
        out[:, part] = dot(rows[...], weight[:, part]).astype(BF16)


def first(rows, w_key, w_value):
    count, depth = rows.shape
    width = w_key.shape[1]
    return pl.pallas_call(
        first_kernel,
        in_specs=[IN_HBM] * 3,
        out_specs=[IN_VMEM] * 5,
        out_shape=[
            pltpu.VMEM(rows.shape, BF16),
            pltpu.VMEM(w_key.shape, BF16),
            pltpu.VMEM(w_value.shape, BF16),
            shape((count, width)),
            shape((count, width)),
        ],
        scratch_shapes=[pltpu.SemaphoreType.DMA((1 + 2 * len(halves_of(width)),))],
        compiler_params=params(),
        cost_estimate=cost(4 * count * depth * width, 4 * depth * width),
    )(keep_in_hbm(rows), keep_in_hbm(w_key), keep_in_hbm(w_value))


def second_kernel(rows, wk, wv, keys_0, values_0, pattern, keys, values, kept):
    for part in halves_of(wk.shape[1]):
        keys[:, part] = dot(rows[...], wk[:, part]).astype(BF16)
        values[:, part] = dot(rows[...], wv[:, part]).astype(BF16)
    blocks = [
        lambda head: (head_of(keys_0, head), head_of(values_0, head)),
        lambda head: (head_of(keys, head), head_of(values, head)),
    ]
    pick_dilated(pattern, blocks, kept)


def second(rows, wk, wv, keys_0, values_0, pattern):
    count, depth = rows.shape
    width = wk.shape[1]
    kept = (2, width // HEAD_SIZE, FAR_ROWS, HEAD_SIZE)
    return pl.pallas_call(
        second_kernel,
        in_specs=[IN_VMEM] * 6,
        out_specs=[IN_VMEM] * 3,
        out_shape=[shape((count, width))] * 2 + [shape(kept)],
        compiler_params=params(),
        cost_estimate=cost(4 * count * depth * width, 2 * count * depth),
    )(rows, wk, wv, keys_0, values_0, pattern)


def query_kernel(*refs):
    rows, (wq_hbm, w_hbm, kept), outs, (wq, sems) = refs[:4], refs[4:7], refs[7:11], refs[11:]
    w = outs[2]
    parts = halves_of(wq.shape[1])
    copies = [
        pltpu.make_async_copy(wq_hbm.at[:, part], wq.at[:, part], sems.at[index])
        for index, part in enumerate(parts)
    ]
    copies.append(pltpu.make_async_copy(w_hbm, w, sems.at[len(parts)]))
    for copy in copies:
        copy.start()
    for part, copy in zip(parts, copies):
        copy.wait()
        for pair, out in ((rows[:2], outs[0]), (rows[2:], outs[1])):
            both = jnp.concatenate([ref[...] for ref in pair], axis=0)
            out[:, part] = dot(both, wq[:, part]).astype(BF16)
    outs[3][...] = kept[...]
    copies[-1].wait()


def query(rows, w_query, w_out, kept):
    count, depth = rows[0].shape
    width = w_query.shape[1]
    return pl.pallas_call(
        query_kernel,
        in_specs=[IN_VMEM] * 4 + [IN_HBM] * 2 + [IN_VMEM],
        out_specs=[IN_VMEM] * 4,
        out_shape=[shape((2 * count, width))] * 2
        + [pltpu.VMEM(w_out.shape, BF16), shape(kept.shape)],
        scratch_shapes=[
            pltpu.VMEM(w_query.shape, BF16),
            pltpu.SemaphoreType.DMA((1 + len(halves_of(width)),)),
        ],
        compiler_params=params(),
        cost_estimate=cost(8 * count * depth * width, 4 * depth * width),
    )(*rows, keep_in_hbm(w_query), keep_in_hbm(w_out), kept)


def across_kernel(rows, wk, wv, keys, values):
    for part in halves_of(wk.shape[1]):
        keys[:, part] = dot(rows[...], wk[:, part]).astype(BF16)
        values[:, part] = dot(rows[...], wv[:, part]).astype(BF16)


def keys_and_values(rows, wk, wv):
    count, depth = rows.shape
    width = wk.shape[1]
    return pl.pallas_call(
        across_kernel,
        in_specs=[IN_VMEM] * 3,
        out_specs=[IN_VMEM] * 2,
        out_shape=[shape((count, width))] * 2,
        compiler_params=params(),
        cost_estimate=cost(4 * count * depth * width, 2 * count * depth),
    )(rows, wk, wv)


def slide_of(place, slides, block):
    end, total = jnp.int32(0), jnp.zeros_like(block)
    for index in range(slides):
        end = end + place[index]
        total = total + (block >= end).astype(jnp.int32)
    return total


def mask_kernel(slides, subs, spans, few, place, asking, asked):
    span, sub = place[slides], place[slides + 1]
    slide = [slide_of(place, slides, span * subs + (sub ^ r)) for r in range(subs)]
    lane = lax.broadcasted_iota(jnp.int32, (BLOCK, HEAD_SIZE), 1)
    for r in range(subs):
        rows = slice(r * BLOCK, (r + 1) * BLOCK)
        apart = (lane <= slides) & (lane != slide[r])
        asking[rows, :] = jnp.where(apart, HIDDEN, 0.0).astype(BF16)
        asked[rows, :] = jnp.where(lane == slide[r], 1.0, 0.0).astype(BF16)
    count = min(spans, GROUP) * FAR_ROWS
    row = lax.broadcasted_iota(jnp.int32, (count, HEAD_SIZE), 0)
    lane = lax.broadcasted_iota(jnp.int32, (count, HEAD_SIZE), 1)
    upper = (row // DILATED_KEPT) % BLOCKS_HALF
    for half in range(subs // BLOCKS_HALF):
        place_0, place_1 = sub ^ (half * BLOCKS_HALF), sub ^ (half * BLOCKS_HALF + 1)
        for group in range(spans * FAR_ROWS // count):
            far = row // FAR_ROWS
            if few:
                order = [bit | y for y in (0, Y_BIT) for bit in (0, *Z_BITS)]
                place_of = jnp.zeros_like(far)
                for index, bits in enumerate(order):
                    place_of = jnp.where(far == index, bits, place_of)
                far = place_of ^ span
            else:
                far = far + group * GROUP
            theirs = slide_of(place, slides, far * subs + jnp.where(upper == 0, place_0, place_1))
            marked = (lane == theirs) | ((lane == slides) & (far == span))
            start = subs * BLOCK + (half * spans * FAR_ROWS + group * count)
            asked[start : start + count, :] = jnp.where(marked, 1.0, 0.0).astype(BF16)


def make_masks(place, slides, subs, spans, few):
    keys = subs * BLOCK + subs // BLOCKS_HALF * spans * FAR_ROWS
    return pl.pallas_call(
        functools.partial(mask_kernel, slides, subs, spans, few),
        in_specs=[IN_SMEM],
        out_specs=[IN_VMEM] * 2,
        out_shape=[shape((subs * BLOCK, HEAD_SIZE)), shape((keys, HEAD_SIZE))],
        compiler_params=params(),
        cost_estimate=cost(64 * keys * HEAD_SIZE, 2 * keys * HEAD_SIZE),
    )(place)


def scores_of(keys, queries):
    return dot_t(keys, queries)


def gather(values, weight):
    return lax.dot_general(
        values, weight.astype(BF16), (((0,), (0,)), ((), ())), preferred_element_type=F32
    )


def begin(queries, keys, values):
    scores = [scores_of(k, q) for k, q in zip(keys, queries)]
    peak = [jnp.max(each, axis=0, keepdims=True) for each in scores]
    weight = [jnp.exp2((each - top) * SCALE) for each, top in zip(scores, peak)]
    total = [jnp.sum(each, axis=0, keepdims=True) for each in weight]
    return peak, total, [gather(v, each) for v, each in zip(values, weight)]


def update(queries, keys, values, state):
    scores = [scores_of(k, q) for k, q in zip(keys, queries)]
    higher = [
        jnp.maximum(top, jnp.max(each, axis=0, keepdims=True))
        for top, each in zip(state[0], scores)
    ]
    shrink = [jnp.exp2((top - new) * SCALE) for top, new in zip(state[0], higher)]
    weight = [jnp.exp2((each - new) * SCALE) for each, new in zip(scores, higher)]
    total = [
        old * less + jnp.sum(each, axis=0, keepdims=True)
        for old, less, each in zip(state[1], shrink, weight)
    ]
    added = [gather(v, each) for v, each in zip(values, weight)]
    return higher, total, [old * less + new for old, less, new in zip(state[2], shrink, added)]


def attend_kernel(first_row, near, halves, few, finish, asking, asked_of, *refs):
    refs = list(refs)
    queries = refs.pop(0)
    if near:
        keys, values = refs[0:4], refs[4:8]
        del refs[:8]
    else:
        gathered_in, stats_in = refs[0:2]
        del refs[:2]
    far = []
    for half, size in halves:
        far.append((half, refs[:size]))
        del refs[:size]
    rows = queries.shape[0]
    span = asking.shape[0]
    half_count = (asked_of.shape[0] - span) // BLOCKS_HALF

    heads = queries.shape[1] // HEAD_SIZE
    group = heads if few and not near else 1

    def some_heads(turn, _):
        those = [turn * group + i for i in range(group)]
        columns = [
            pl.ds(pl.multiple_of(head * HEAD_SIZE, HEAD_SIZE), HEAD_SIZE)
            if group < heads
            else slice(head * HEAD_SIZE, (head + 1) * HEAD_SIZE)
            for head in those
        ]
        row_marks = asking[first_row : first_row + rows, :]
        asked = [jnp.concatenate([queries[:, each], row_marks], axis=1) for each in columns]

        def marked(parts, where):
            return jnp.concatenate([jnp.concatenate(parts, axis=0), asked_of[where, :]], axis=1)

        def ready(head, each):
            keyed, valued = [], []
            if near:
                keyed.append(marked([ref[:, each] for ref in keys], slice(0, span)))
                valued += [ref[:, each] for ref in values]
            if few:
                for half, parts in far:
                    start = span + half * half_count
                    pieces = [(ref, i) for ref in parts for i in range(ref.shape[0])]
                    where = slice(start, start + half_count)
                    keyed.append(marked([ref[i, 0, head] for ref, i in pieces], where))
                    valued += [ref[i, 1, head] for ref, i in pieces]
            return jnp.concatenate(keyed, axis=0), jnp.concatenate(valued, axis=0)

        if near:
            state = begin(asked, *zip(*map(ready, those, columns)))
        else:
            state = (
                [stats_in[head, 0:1, :] for head in those],
                [stats_in[head, 1:2, :] for head in those],
                [gathered_in[head] for head in those],
            )
            if few:
                state = update(asked, *zip(*map(ready, those, columns)), state)
        if not few:
            for half, (part,) in far:
                start = span + half * half_count

                def step(number, state, start=start, part=part):
                    base = number * GROUP
                    width = GROUP * FAR_ROWS
                    where = pl.ds(pl.multiple_of(start + number * width, width), width)
                    found = [
                        [
                            marked([part[base + i, 0, head] for i in range(GROUP)], where)
                            for head in those
                        ],
                        [
                            jnp.concatenate([part[base + i, 1, head] for i in range(GROUP)], axis=0)
                            for head in those
                        ],
                    ]
                    return update(asked, *found, state)

                state = lax.fori_loop(0, part.shape[0] // GROUP, step, state)
        for head, each, peak, total, gathered in zip(those, columns, *state):
            if finish:
                keep, send = refs
                context = (gathered / total).T.astype(BF16)
                keep[:, each] = context[:BLOCK]
                send[:, each] = context[BLOCK:]
            else:
                gathered_out, stats_out = refs
                gathered_out[head] = gathered
                stats_out[head, 0:1, :] = peak
                stats_out[head, 1:2, :] = total
        return 0

    if group == heads:
        some_heads(0, 0)
    else:
        lax.fori_loop(0, heads // group, some_heads, 0)


def attend(masks, few, first_row, queries, halves, near=None, begun=None, finish=True):
    rows, width = queries.shape
    heads = width // HEAD_SIZE
    operands = [*masks, queries]
    operands += [*near[0], *near[1]] if near else list(begun)
    columns = masks[0].shape[0] if near else 0
    for _, parts in halves:
        operands += parts
    far_bytes = sum(2 * part.size for _, parts in halves for part in parts)
    columns += far_bytes // (4 * width)
    if finish:
        out_shape = [shape((BLOCK, width))] * 2
    else:
        out_shape = [shape((heads, HEAD_SIZE, rows), F32), shape((heads, 8, rows), F32)]
    return pl.pallas_call(
        functools.partial(
            attend_kernel,
            first_row,
            near is not None,
            [(half, len(parts)) for half, parts in halves],
            few,
            finish,
        ),
        in_specs=[IN_VMEM] * len(operands),
        out_specs=[IN_VMEM] * 2,
        out_shape=out_shape,
        compiler_params=params(far_bytes),
        cost_estimate=cost(
            4 * rows * columns * width, 4 * rows * width, heads * rows * columns
        ),
    )(*operands)


def mix_kernel(rows_0, rows_1, weight_0, weight_1, out):
    tile = min(512, out.shape[1])
    for index in range(out.shape[1] // tile):
        part = slice(index * tile, (index + 1) * tile)
        total = dot(rows_0[...], weight_0[:, part]) + dot(rows_1[...], weight_1[:, part])
        out[:, part] = total.astype(out.dtype)


def mix(rows_0, rows_1, weight_0, weight_1, dtype):
    rows, depth = rows_0.shape
    width = weight_0.shape[1]
    return pl.pallas_call(
        mix_kernel,
        in_specs=[IN_VMEM] * 4,
        out_specs=IN_VMEM,
        out_shape=shape((rows, width), dtype),
        compiler_params=params(),
        cost_estimate=cost(4 * rows * depth * width, 4 * rows * width),
    )(rows_0, rows_1, weight_0, weight_1)


def shards(seqs, subs, normed, w_query, w_key, w_value, w_out, pattern, slide_lengths):
    slides = slide_lengths.shape[0]
    axes = [lax.axis_index(name).astype(jnp.int32)[None] for name in ("seq", "sub")]
    few = seqs == GROUP

    def swap(array, bit, axis="sub"):
        count = subs if axis == "sub" else seqs
        return lax.ppermute(array, axis, [(i, i ^ bit) for i in range(count)])

    def after(array, *others):
        return lax.optimization_barrier((array, *others))[0]

    def first_round(kept):
        return [swap(kept, bit, "seq") for bit in Z_BITS]

    def second_round(pieces):
        column = jnp.stack(pieces)
        return [column, swap(column, Y_BIT, "seq")]

    across = swap(normed, 2)
    beside = swap(normed, 1)
    mine, wk, wv, keys_0, values_0 = first(normed, w_key, w_value)
    keys_1, values_1, kept_a = second(beside, wk, wv, keys_0, values_0, pattern)
    place = jnp.concatenate([after(slide_lengths, kept_a), *axes])
    masks = list(make_masks(place, slides, subs, seqs, few))
    wo_beside = swap(w_out, 1)
    if few:
        along_z = first_round(kept_a)
        *along_z, masks[0] = lax.optimization_barrier((*along_z, masks[0]))
        half_a = 0, second_round([kept_a, *along_z])
        across = after(across, masks[0], wo_beside)
    else:
        half_a = 0, [lax.all_gather(kept_a, "seq", axis=0)]
    wo_beside = pltpu.with_memory_space_constraint(wo_beside, pltpu.VMEM)
    beyond = swap(across, 1)
    if few:
        beyond = after(beyond, half_a[1][0])
    keys_2, values_2 = keys_and_values(across, wk, wv)
    keys_3, values_3, kept_b = second(after(beyond, keys_2), wk, wv, keys_2, values_2, pattern)
    rows = [mine, beside, across, beyond]
    query_a, query_b, wo, kept_again = query(rows, w_query, w_out, kept_b)
    near = [keys_0, keys_1, keys_2, keys_3], [values_0, values_1, values_2, values_3]
    call = functools.partial(attend, masks, few)
    if few:
        along_z = first_round(kept_b)
        along_y = swap(kept_again, Y_BIT, "seq")
        *along_z, along_y, query_b, half_a[1][1] = lax.optimization_barrier(
            (*along_z, along_y, query_b, half_a[1][1])
        )
        column, other = second_round(along_z)
        half_b = 1, [kept_b[None], column, along_y[None], other]
        asked = after(query_b, column)
        begun = call(2 * BLOCK, asked, [half_a], near=near, finish=False)
    else:
        half_b = 1, [lax.all_gather(kept_b, "seq", axis=0)]
        begun = call(2 * BLOCK, query_b, [half_a], near=near, finish=False)
    keep_b, send_b = call(2 * BLOCK, query_b, [half_b], begun=begun)
    other_b = swap(send_b, 1)
    leaving = mix(keep_b, other_b, wo, wo_beside, BF16)
    arriving = swap(leaving, 2)
    query_a = after(query_a, leaving)
    keep_a, send_a = call(0, query_a, [half_a, half_b], near=near)
    other_a = swap(send_a, 1)
    own = mix(keep_a, other_a, wo, wo_beside, F32)
    return (own + arriving.astype(F32)).astype(BF16)


def solution(mesh):
    placed = (
        P(("seq", "sub"), None),
        P(None, "sub"),
        P(None, "sub"),
        P(None, "sub"),
        P("sub", None),
        P("sub", None),
        P(),
    )
    return jax.shard_map(
        functools.partial(shards, mesh.shape["seq"], mesh.shape["sub"]),
        mesh=mesh,
        in_specs=placed,
        out_specs=P(("seq", "sub"), None),
        check_vma=False,
    )
```

```python
import functools
import math

import jax
import jax.numpy as jnp
from jax import lax
from jax.experimental import pallas as pl
from jax.experimental.pallas import tpu as pltpu
from jax.sharding import PartitionSpec as P

HEAD_SIZE = 128
BLOCK = 128
DILATED_KEPT = 16
BLOCKS_HALF = 2
FAR_ROWS = BLOCKS_HALF * DILATED_KEPT
GROUP = 8
HIDDEN = -1e30
SCALE = math.log2(math.e) / math.sqrt(HEAD_SIZE)
BF16 = jnp.bfloat16
F32 = jnp.float32
IN_VMEM = pl.BlockSpec(memory_space=pltpu.VMEM)
IN_HBM = pl.BlockSpec(memory_space=pltpu.HBM)
IN_SMEM = pl.BlockSpec(memory_space=pltpu.SMEM)
Y_BIT = 1
Z_BITS = (4, 6, 2)


def dot(a, b):
    return jnp.dot(a, b, preferred_element_type=F32)


def dot_t(a, b):
    return lax.dot_general(a, b, (((1,), (1,)), ((), ())), preferred_element_type=F32)


def params(extra=0):
    return pltpu.CompilerParams(vmem_limit_bytes=16 * 2**20 + extra)


def cost(flops, bytes_accessed, transcendentals=0):
    return pl.CostEstimate(
        flops=flops // 100,
        bytes_accessed=bytes_accessed // 100,
        transcendentals=transcendentals // 100,
    )


def shape(dims, dtype=BF16):
    return jax.ShapeDtypeStruct(tuple(dims), dtype)


def keep_in_hbm(array):
    return pltpu.with_memory_space_constraint(array, pltpu.HBM)


def halves_of(width):
    tile = min(256, width)
    return [slice(i * tile, (i + 1) * tile) for i in range(width // tile)]


def pick_dilated(pattern, blocks, kept):
    positions = lax.broadcasted_iota(jnp.int32, (BLOCK, BLOCK), 0)
    for head in range(kept.shape[1]):
        row = pattern[head : head + 1, :]
        chosen = (positions == row).astype(F32).T[:DILATED_KEPT].astype(BF16)
        for index, block in enumerate(blocks):
            picked = dot(chosen, jnp.concatenate(block(head), axis=1)).astype(BF16)
            spot = slice(index * DILATED_KEPT, (index + 1) * DILATED_KEPT)
            kept[0, head, spot, :] = picked[:, :HEAD_SIZE]
            kept[1, head, spot, :] = picked[:, HEAD_SIZE:]


def head_of(ref, head, rows=slice(None)):
    return ref[rows, head * HEAD_SIZE : (head + 1) * HEAD_SIZE]


def first_kernel(rows_hbm, wk_hbm, wv_hbm, rows, wk, wv, keys, values, sems):
    parts = halves_of(wk.shape[1])
    whole = pltpu.make_async_copy(rows_hbm, rows, sems.at[0])
    whole.start()
    copies = []
    for index, part in enumerate(parts):
        for side, (source, target) in enumerate(((wk_hbm, wk), (wv_hbm, wv))):
            copy = pltpu.make_async_copy(
                source.at[:, part], target.at[:, part], sems.at[1 + 2 * index + side]
            )
            copy.start()
            copies.append((copy, target, part, (keys, values)[side]))
    whole.wait()
    for copy, weight, part, out in copies:
        copy.wait()
        out[:, part] = dot(rows[...], weight[:, part]).astype(BF16)


def first(rows, w_key, w_value):
    count, depth = rows.shape
    width = w_key.shape[1]
    return pl.pallas_call(
        first_kernel,
        in_specs=[IN_HBM] * 3,
        out_specs=[IN_VMEM] * 5,
        out_shape=[
            pltpu.VMEM(rows.shape, BF16),
            pltpu.VMEM(w_key.shape, BF16),
            pltpu.VMEM(w_value.shape, BF16),
            shape((count, width)),
            shape((count, width)),
        ],
        scratch_shapes=[pltpu.SemaphoreType.DMA((1 + 2 * len(halves_of(width)),))],
        compiler_params=params(),
        cost_estimate=cost(4 * count * depth * width, 4 * depth * width),
    )(keep_in_hbm(rows), keep_in_hbm(w_key), keep_in_hbm(w_value))


def second_kernel(rows, wk, wv, keys_0, values_0, pattern, keys, values, kept):
    for part in halves_of(wk.shape[1]):
        keys[:, part] = dot(rows[...], wk[:, part]).astype(BF16)
        values[:, part] = dot(rows[...], wv[:, part]).astype(BF16)
    blocks = [
        lambda head: (head_of(keys_0, head), head_of(values_0, head)),
        lambda head: (head_of(keys, head), head_of(values, head)),
    ]
    pick_dilated(pattern, blocks, kept)


def second(rows, wk, wv, keys_0, values_0, pattern):
    count, depth = rows.shape
    width = wk.shape[1]
    kept = (2, width // HEAD_SIZE, FAR_ROWS, HEAD_SIZE)
    return pl.pallas_call(
        second_kernel,
        in_specs=[IN_VMEM] * 6,
        out_specs=[IN_VMEM] * 3,
        out_shape=[shape((count, width))] * 2 + [shape(kept)],
        compiler_params=params(),
        cost_estimate=cost(4 * count * depth * width, 2 * count * depth),
    )(rows, wk, wv, keys_0, values_0, pattern)


def query_kernel(rows_0, rows_1, wq_hbm, kept, queries, wq, passed, sems):
    parts = halves_of(wq.shape[1])
    copies = [
        pltpu.make_async_copy(wq_hbm.at[:, part], wq.at[:, part], sems.at[index])
        for index, part in enumerate(parts)
    ]
    for copy in copies:
        copy.start()
    passed[...] = kept[...]
    rows = jnp.concatenate([rows_0[...], rows_1[...]], axis=0)
    for part, copy in zip(parts, copies):
        copy.wait()
        queries[:, part] = dot(rows, wq[:, part]).astype(BF16)


def query(rows_0, rows_1, w_query, kept):
    count, depth = rows_0.shape
    width = w_query.shape[1]
    return pl.pallas_call(
        query_kernel,
        in_specs=[IN_VMEM] * 2 + [IN_HBM, IN_VMEM],
        out_specs=[IN_VMEM] * 3,
        out_shape=[
            shape((2 * count, width)),
            pltpu.VMEM(w_query.shape, BF16),
            shape(kept.shape),
        ],
        scratch_shapes=[pltpu.SemaphoreType.DMA((len(halves_of(width)),))],
        compiler_params=params(),
        cost_estimate=cost(4 * count * depth * width, 2 * depth * width),
    )(rows_0, rows_1, keep_in_hbm(w_query), kept)


def last_query_kernel(rows_0, rows_1, wq, w_hbm, queries, w, sem):
    copy = pltpu.make_async_copy(w_hbm, w, sem)
    copy.start()
    rows = jnp.concatenate([rows_0[...], rows_1[...]], axis=0)
    for part in halves_of(wq.shape[1]):
        queries[:, part] = dot(rows, wq[:, part]).astype(BF16)
    copy.wait()


def last_query(rows_0, rows_1, wq, w_out):
    count, depth = rows_0.shape
    width = wq.shape[1]
    return pl.pallas_call(
        last_query_kernel,
        in_specs=[IN_VMEM] * 3 + [IN_HBM],
        out_specs=[IN_VMEM] * 2,
        out_shape=[shape((2 * count, width)), pltpu.VMEM(w_out.shape, BF16)],
        scratch_shapes=[pltpu.SemaphoreType.DMA],
        compiler_params=params(),
        cost_estimate=cost(4 * count * depth * width, 2 * depth * width),
    )(rows_0, rows_1, wq, keep_in_hbm(w_out))


def across_kernel(rows, wk, wv, keys, values):
    for part in halves_of(wk.shape[1]):
        keys[:, part] = dot(rows[...], wk[:, part]).astype(BF16)
        values[:, part] = dot(rows[...], wv[:, part]).astype(BF16)


def keys_and_values(rows, wk, wv):
    count, depth = rows.shape
    width = wk.shape[1]
    return pl.pallas_call(
        across_kernel,
        in_specs=[IN_VMEM] * 3,
        out_specs=[IN_VMEM] * 2,
        out_shape=[shape((count, width))] * 2,
        compiler_params=params(),
        cost_estimate=cost(4 * count * depth * width, 2 * count * depth),
    )(rows, wk, wv)


def slide_of(place, slides, block):
    end, total = jnp.int32(0), jnp.zeros_like(block)
    for index in range(slides):
        end = end + place[index]
        total = total + (block >= end).astype(jnp.int32)
    return total


def mask_kernel(slides, subs, spans, few, place, asking, asked):
    span, sub = place[slides], place[slides + 1]
    slide = [slide_of(place, slides, span * subs + (sub ^ r)) for r in range(subs)]
    lane = lax.broadcasted_iota(jnp.int32, (BLOCK, HEAD_SIZE), 1)
    for r in range(subs):
        rows = slice(r * BLOCK, (r + 1) * BLOCK)
        apart = (lane <= slides) & (lane != slide[r])
        asking[rows, :] = jnp.where(apart, HIDDEN, 0.0).astype(BF16)
        asked[rows, :] = jnp.where(lane == slide[r], 1.0, 0.0).astype(BF16)
    count = min(spans, GROUP) * FAR_ROWS
    row = lax.broadcasted_iota(jnp.int32, (count, HEAD_SIZE), 0)
    lane = lax.broadcasted_iota(jnp.int32, (count, HEAD_SIZE), 1)
    upper = (row // DILATED_KEPT) % BLOCKS_HALF
    for half in range(subs // BLOCKS_HALF):
        place_0, place_1 = sub ^ (half * BLOCKS_HALF), sub ^ (half * BLOCKS_HALF + 1)
        for group in range(spans * FAR_ROWS // count):
            far = row // FAR_ROWS
            if few:
                order = [bit | y for y in (0, Y_BIT) for bit in (0, *Z_BITS)]
                place_of = jnp.zeros_like(far)
                for index, bits in enumerate(order):
                    place_of = jnp.where(far == index, bits, place_of)
                far = place_of ^ span
            else:
                far = far + group * GROUP
            theirs = slide_of(place, slides, far * subs + jnp.where(upper == 0, place_0, place_1))
            marked = (lane == theirs) | ((lane == slides) & (far == span))
            start = subs * BLOCK + (half * spans * FAR_ROWS + group * count)
            asked[start : start + count, :] = jnp.where(marked, 1.0, 0.0).astype(BF16)


def make_masks(place, slides, subs, spans, few):
    keys = subs * BLOCK + subs // BLOCKS_HALF * spans * FAR_ROWS
    return pl.pallas_call(
        functools.partial(mask_kernel, slides, subs, spans, few),
        in_specs=[IN_SMEM],
        out_specs=[IN_VMEM] * 2,
        out_shape=[shape((subs * BLOCK, HEAD_SIZE)), shape((keys, HEAD_SIZE))],
        compiler_params=params(),
        cost_estimate=cost(64 * keys * HEAD_SIZE, 2 * keys * HEAD_SIZE),
    )(place)


def scores_of(keys, queries):
    return dot_t(keys, queries)


def gather(values, weight):
    return lax.dot_general(
        values, weight.astype(BF16), (((0,), (0,)), ((), ())), preferred_element_type=F32
    )


def begin(queries, keys, values):
    scores = [scores_of(k, q) for k, q in zip(keys, queries)]
    peak = [jnp.max(each, axis=0, keepdims=True) for each in scores]
    weight = [jnp.exp2((each - top) * SCALE) for each, top in zip(scores, peak)]
    total = [jnp.sum(each, axis=0, keepdims=True) for each in weight]
    return peak, total, [gather(v, each) for v, each in zip(values, weight)]


def update(queries, keys, values, state):
    scores = [scores_of(k, q) for k, q in zip(keys, queries)]
    higher = [
        jnp.maximum(top, jnp.max(each, axis=0, keepdims=True))
        for top, each in zip(state[0], scores)
    ]
    shrink = [jnp.exp2((top - new) * SCALE) for top, new in zip(state[0], higher)]
    weight = [jnp.exp2((each - new) * SCALE) for each, new in zip(scores, higher)]
    total = [
        old * less + jnp.sum(each, axis=0, keepdims=True)
        for old, less, each in zip(state[1], shrink, weight)
    ]
    added = [gather(v, each) for v, each in zip(values, weight)]
    return higher, total, [old * less + new for old, less, new in zip(state[2], shrink, added)]


def attend_kernel(first_row, near, halves, few, finish, asking, asked_of, *refs):
    refs = list(refs)
    queries = refs.pop(0)
    if near:
        keys, values = refs[0:4], refs[4:8]
        del refs[:8]
    else:
        gathered_in, stats_in = refs[0:2]
        del refs[:2]
    far = []
    for half, size in halves:
        far.append((half, refs[:size]))
        del refs[:size]
    rows = queries.shape[0]
    span = asking.shape[0]
    half_count = (asked_of.shape[0] - span) // BLOCKS_HALF

    heads = queries.shape[1] // HEAD_SIZE
    group = 1 if not few else min(2, heads) if near else heads

    def some_heads(turn, _):
        those = [turn * group + i for i in range(group)]
        columns = [
            pl.ds(pl.multiple_of(head * HEAD_SIZE, HEAD_SIZE), HEAD_SIZE)
            if group < heads
            else slice(head * HEAD_SIZE, (head + 1) * HEAD_SIZE)
            for head in those
        ]
        row_marks = asking[first_row : first_row + rows, :]
        asked = [jnp.concatenate([queries[:, each], row_marks], axis=1) for each in columns]

        def marked(parts, where):
            return jnp.concatenate([jnp.concatenate(parts, axis=0), asked_of[where, :]], axis=1)

        def ready(head, each):
            keyed, valued = [], []
            if near:
                keyed.append(marked([ref[:, each] for ref in keys], slice(0, span)))
                valued += [ref[:, each] for ref in values]
            if few:
                for half, parts in far:
                    start = span + half * half_count
                    pieces = [(ref, i) for ref in parts for i in range(ref.shape[0])]
                    where = slice(start, start + half_count)
                    keyed.append(marked([ref[i, 0, head] for ref, i in pieces], where))
                    valued += [ref[i, 1, head] for ref, i in pieces]
            return jnp.concatenate(keyed, axis=0), jnp.concatenate(valued, axis=0)

        if near:
            state = begin(asked, *zip(*map(ready, those, columns)))
        else:
            state = (
                [stats_in[head, 0:1, :] for head in those],
                [stats_in[head, 1:2, :] for head in those],
                [gathered_in[head] for head in those],
            )
            if few:
                state = update(asked, *zip(*map(ready, those, columns)), state)
        if not few:
            for half, (part,) in far:
                start = span + half * half_count

                def step(number, state, start=start, part=part):
                    base = number * GROUP
                    width = GROUP * FAR_ROWS
                    where = pl.ds(pl.multiple_of(start + number * width, width), width)
                    found = [
                        [
                            marked([part[base + i, 0, head] for i in range(GROUP)], where)
                            for head in those
                        ],
                        [
                            jnp.concatenate([part[base + i, 1, head] for i in range(GROUP)], axis=0)
                            for head in those
                        ],
                    ]
                    return update(asked, *found, state)

                state = lax.fori_loop(0, part.shape[0] // GROUP, step, state)
        for head, each, peak, total, gathered in zip(those, columns, *state):
            if finish:
                keep, send = refs
                context = (gathered / total).T.astype(BF16)
                keep[:, each] = context[:BLOCK]
                send[:, each] = context[BLOCK:]
            else:
                gathered_out, stats_out = refs
                gathered_out[head] = gathered
                stats_out[head, 0:1, :] = peak
                stats_out[head, 1:2, :] = total
        return 0

    if group == heads:
        some_heads(0, 0)
    else:
        lax.fori_loop(0, heads // group, some_heads, 0)


def attend(masks, few, first_row, queries, halves, near=None, begun=None, finish=True):
    rows, width = queries.shape
    heads = width // HEAD_SIZE
    operands = [*masks, queries]
    operands += [*near[0], *near[1]] if near else list(begun)
    columns = masks[0].shape[0] if near else 0
    for _, parts in halves:
        operands += parts
    far_bytes = sum(2 * part.size for _, parts in halves for part in parts)
    columns += far_bytes // (4 * width)
    if finish:
        out_shape = [shape((BLOCK, width))] * 2
    else:
        out_shape = [shape((heads, HEAD_SIZE, rows), F32), shape((heads, 8, rows), F32)]
    return pl.pallas_call(
        functools.partial(
            attend_kernel,
            first_row,
            near is not None,
            [(half, len(parts)) for half, parts in halves],
            few,
            finish,
        ),
        in_specs=[IN_VMEM] * len(operands),
        out_specs=[IN_VMEM] * 2,
        out_shape=out_shape,
        compiler_params=params(far_bytes),
        cost_estimate=cost(
            4 * rows * columns * width, 4 * rows * width, heads * rows * columns
        ),
    )(*operands)


def mix_kernel(rows_0, rows_1, weight_0, weight_1, out):
    tile = min(512, out.shape[1])
    for index in range(out.shape[1] // tile):
        part = slice(index * tile, (index + 1) * tile)
        total = dot(rows_0[...], weight_0[:, part]) + dot(rows_1[...], weight_1[:, part])
        out[:, part] = total.astype(out.dtype)


def mix(rows_0, rows_1, weight_0, weight_1, dtype):
    rows, depth = rows_0.shape
    width = weight_0.shape[1]
    return pl.pallas_call(
        mix_kernel,
        in_specs=[IN_VMEM] * 4,
        out_specs=IN_VMEM,
        out_shape=shape((rows, width), dtype),
        compiler_params=params(),
        cost_estimate=cost(4 * rows * depth * width, 4 * rows * width),
    )(rows_0, rows_1, weight_0, weight_1)


def shards(seqs, subs, normed, w_query, w_key, w_value, w_out, pattern, slide_lengths):
    slides = slide_lengths.shape[0]
    axes = [lax.axis_index(name).astype(jnp.int32)[None] for name in ("seq", "sub")]
    few = seqs == GROUP

    def swap(array, bit, axis="sub"):
        count = subs if axis == "sub" else seqs
        return lax.ppermute(array, axis, [(i, i ^ bit) for i in range(count)])

    def after(array, *others):
        return lax.optimization_barrier((array, *others))[0]

    def first_round(kept):
        return [swap(kept, bit, "seq") for bit in Z_BITS]

    def second_round(pieces):
        column = jnp.stack(pieces)
        return [column, swap(column, Y_BIT, "seq")]

    across = swap(normed, 2)
    beside = swap(normed, 1)
    mine, wk, wv, keys_0, values_0 = first(normed, w_key, w_value)
    keys_1, values_1, kept_a = second(beside, wk, wv, keys_0, values_0, pattern)
    place = jnp.concatenate([after(slide_lengths, kept_a), *axes])
    masks = list(make_masks(place, slides, subs, seqs, few))
    wo_beside = swap(w_out, 1)
    if few:
        along_z = first_round(kept_a)
        *along_z, masks[0] = lax.optimization_barrier((*along_z, masks[0]))
        half_a = 0, second_round([kept_a, *along_z])
        across = after(across, masks[0], wo_beside)
    else:
        half_a = 0, [lax.all_gather(kept_a, "seq", axis=0)]
    wo_beside = pltpu.with_memory_space_constraint(wo_beside, pltpu.VMEM)
    beyond = swap(across, 1)
    if few:
        beyond = after(beyond, half_a[1][0])
    keys_2, values_2 = keys_and_values(across, wk, wv)
    keys_3, values_3, kept_b = second(after(beyond, keys_2), wk, wv, keys_2, values_2, pattern)
    query_b, wq, kept_again = query(across, beyond, w_query, kept_b)
    near = [keys_0, keys_1, keys_2, keys_3], [values_0, values_1, values_2, values_3]
    call = functools.partial(attend, masks, few)
    if few:
        along_z = first_round(kept_b)
        along_y = swap(kept_again, Y_BIT, "seq")
        *along_z, along_y, query_b, half_a[1][1] = lax.optimization_barrier(
            (*along_z, along_y, query_b, half_a[1][1])
        )
        column, other = second_round(along_z)
        half_b = 1, [kept_b[None], column, along_y[None], other]
        asked = after(query_b, column)
        mine = after(mine, column)
        begun = call(2 * BLOCK, asked, [half_a], near=near, finish=False)
    else:
        half_b = 1, [lax.all_gather(kept_b, "seq", axis=0)]
        begun = call(2 * BLOCK, query_b, [half_a], near=near, finish=False)
    query_a, wo = last_query(mine, beside, wq, w_out)
    query_b = after(query_b, query_a)
    keep_b, send_b = call(2 * BLOCK, query_b, [half_b], begun=begun)
    other_b = swap(send_b, 1)
    leaving = mix(keep_b, other_b, wo, wo_beside, BF16)
    arriving = swap(leaving, 2)
    query_a = after(query_a, leaving)
    keep_a, send_a = call(0, query_a, [half_a, half_b], near=near)
    other_a = swap(send_a, 1)
    own = mix(keep_a, other_a, wo, wo_beside, F32)
    return (own + arriving.astype(F32)).astype(BF16)


def solution(mesh):
    placed = (
        P(("seq", "sub"), None),
        P(None, "sub"),
        P(None, "sub"),
        P(None, "sub"),
        P("sub", None),
        P("sub", None),
        P(),
    )
    return jax.shard_map(
        functools.partial(shards, mesh.shape["seq"], mesh.shape["sub"]),
        mesh=mesh,
        in_specs=placed,
        out_specs=P(("seq", "sub"), None),
        check_vma=False,
    )
```

```python
import functools
import math

import jax
import jax.numpy as jnp
from jax import lax
from jax.experimental import pallas as pl
from jax.experimental.pallas import tpu as pltpu
from jax.sharding import PartitionSpec as P

HEAD_SIZE = 128
BLOCK = 128
DILATED_KEPT = 16
BLOCKS_HALF = 2
FAR_ROWS = BLOCKS_HALF * DILATED_KEPT
GROUP = 8
STREAMS = 8
HIDDEN = -1e30
SCALE = math.log2(math.e) / math.sqrt(HEAD_SIZE)
BF16 = jnp.bfloat16
F32 = jnp.float32
IN_VMEM = pl.BlockSpec(memory_space=pltpu.VMEM)
IN_HBM = pl.BlockSpec(memory_space=pltpu.HBM)
IN_SMEM = pl.BlockSpec(memory_space=pltpu.SMEM)
Y_BIT = 1
Z_BITS = (4, 6, 2)


def dot(a, b):
    return jnp.dot(a, b, preferred_element_type=F32)


def dot_t(a, b):
    return lax.dot_general(a, b, (((1,), (1,)), ((), ())), preferred_element_type=F32)


def params(extra=0):
    return pltpu.CompilerParams(vmem_limit_bytes=16 * 2**20 + extra)


def cost(flops, bytes_accessed, transcendentals=0):
    return pl.CostEstimate(
        flops=flops // 100,
        bytes_accessed=bytes_accessed // 100,
        transcendentals=transcendentals // 100,
    )


def shape(dims, dtype=BF16):
    return jax.ShapeDtypeStruct(tuple(dims), dtype)


def keep_in_hbm(array):
    return pltpu.with_memory_space_constraint(array, pltpu.HBM)


def start_copies(source, target, sems, base):
    rows = source.shape[0] // STREAMS
    copies = []
    for index in range(STREAMS):
        where = slice(index * rows, (index + 1) * rows)
        copy = pltpu.make_async_copy(source.at[where, :], target.at[where, :], sems.at[base + index])
        copy.start()
        copies.append(copy)
    return copies


def halves_of(width):
    tile = min(256, width)
    return [slice(i * tile, (i + 1) * tile) for i in range(width // tile)]


def pick_dilated(pattern, blocks, kept):
    positions = lax.broadcasted_iota(jnp.int32, (BLOCK, BLOCK), 0)
    for head in range(kept.shape[1]):
        row = pattern[head : head + 1, :]
        chosen = (positions == row).astype(F32).T[:DILATED_KEPT].astype(BF16)
        for index, block in enumerate(blocks):
            picked = dot(chosen, jnp.concatenate(block(head), axis=1)).astype(BF16)
            spot = slice(index * DILATED_KEPT, (index + 1) * DILATED_KEPT)
            kept[0, head, spot, :] = picked[:, :HEAD_SIZE]
            kept[1, head, spot, :] = picked[:, HEAD_SIZE:]


def head_of(ref, head, rows=slice(None)):
    return ref[rows, head * HEAD_SIZE : (head + 1) * HEAD_SIZE]


def first_kernel(rows_hbm, wk_hbm, wv_hbm, rows, wk, wv, keys, values, sems):
    whole = pltpu.make_async_copy(rows_hbm, rows, sems.at[0])
    whole.start()
    key_copies = start_copies(wk_hbm, wk, sems, 1)
    value_copies = start_copies(wv_hbm, wv, sems, 1 + STREAMS)
    whole.wait()
    for copies, weight, out in ((key_copies, wk, keys), (value_copies, wv, values)):
        for copy in copies:
            copy.wait()
        for part in halves_of(wk.shape[1]):
            out[:, part] = dot(rows[...], weight[:, part]).astype(BF16)


def first(rows, w_key, w_value):
    count, depth = rows.shape
    width = w_key.shape[1]
    return pl.pallas_call(
        first_kernel,
        in_specs=[IN_HBM] * 3,
        out_specs=[IN_VMEM] * 5,
        out_shape=[
            pltpu.VMEM(rows.shape, BF16),
            pltpu.VMEM(w_key.shape, BF16),
            pltpu.VMEM(w_value.shape, BF16),
            shape((count, width)),
            shape((count, width)),
        ],
        scratch_shapes=[pltpu.SemaphoreType.DMA((1 + 2 * STREAMS,))],
        compiler_params=params(),
        cost_estimate=cost(4 * count * depth * width, 4 * depth * width),
    )(keep_in_hbm(rows), keep_in_hbm(w_key), keep_in_hbm(w_value))


def second_kernel(rows, wk, wv, keys_0, values_0, pattern, keys, values, kept):
    for part in halves_of(wk.shape[1]):
        keys[:, part] = dot(rows[...], wk[:, part]).astype(BF16)
        values[:, part] = dot(rows[...], wv[:, part]).astype(BF16)
    blocks = [
        lambda head: (head_of(keys_0, head), head_of(values_0, head)),
        lambda head: (head_of(keys, head), head_of(values, head)),
    ]
    pick_dilated(pattern, blocks, kept)


def second(rows, wk, wv, keys_0, values_0, pattern):
    count, depth = rows.shape
    width = wk.shape[1]
    kept = (2, width // HEAD_SIZE, FAR_ROWS, HEAD_SIZE)
    return pl.pallas_call(
        second_kernel,
        in_specs=[IN_VMEM] * 6,
        out_specs=[IN_VMEM] * 3,
        out_shape=[shape((count, width))] * 2 + [shape(kept)],
        compiler_params=params(),
        cost_estimate=cost(4 * count * depth * width, 2 * count * depth),
    )(rows, wk, wv, keys_0, values_0, pattern)


def query_kernel(rows_0, rows_1, wq_hbm, kept, queries, wq, passed, sems):
    copies = start_copies(wq_hbm, wq, sems, 0)
    passed[...] = kept[...]
    rows = jnp.concatenate([rows_0[...], rows_1[...]], axis=0)
    for copy in copies:
        copy.wait()
    for part in halves_of(wq.shape[1]):
        queries[:, part] = dot(rows, wq[:, part]).astype(BF16)


def query(rows_0, rows_1, w_query, kept):
    count, depth = rows_0.shape
    width = w_query.shape[1]
    return pl.pallas_call(
        query_kernel,
        in_specs=[IN_VMEM] * 2 + [IN_HBM, IN_VMEM],
        out_specs=[IN_VMEM] * 3,
        out_shape=[
            shape((2 * count, width)),
            pltpu.VMEM(w_query.shape, BF16),
            shape(kept.shape),
        ],
        scratch_shapes=[pltpu.SemaphoreType.DMA((STREAMS,))],
        compiler_params=params(),
        cost_estimate=cost(4 * count * depth * width, 2 * depth * width),
    )(rows_0, rows_1, keep_in_hbm(w_query), kept)


def last_query_kernel(rows_0, rows_1, wq, w_hbm, queries, w, sems):
    copies = start_copies(w_hbm, w, sems, 0)
    rows = jnp.concatenate([rows_0[...], rows_1[...]], axis=0)
    for part in halves_of(wq.shape[1]):
        queries[:, part] = dot(rows, wq[:, part]).astype(BF16)
    for copy in copies:
        copy.wait()


def last_query(rows_0, rows_1, wq, w_out):
    count, depth = rows_0.shape
    width = wq.shape[1]
    return pl.pallas_call(
        last_query_kernel,
        in_specs=[IN_VMEM] * 3 + [IN_HBM],
        out_specs=[IN_VMEM] * 2,
        out_shape=[shape((2 * count, width)), pltpu.VMEM(w_out.shape, BF16)],
        scratch_shapes=[pltpu.SemaphoreType.DMA((STREAMS,))],
        compiler_params=params(),
        cost_estimate=cost(4 * count * depth * width, 2 * depth * width),
    )(rows_0, rows_1, wq, keep_in_hbm(w_out))


def across_kernel(rows, wk, wv, keys, values):
    for part in halves_of(wk.shape[1]):
        keys[:, part] = dot(rows[...], wk[:, part]).astype(BF16)
        values[:, part] = dot(rows[...], wv[:, part]).astype(BF16)


def keys_and_values(rows, wk, wv):
    count, depth = rows.shape
    width = wk.shape[1]
    return pl.pallas_call(
        across_kernel,
        in_specs=[IN_VMEM] * 3,
        out_specs=[IN_VMEM] * 2,
        out_shape=[shape((count, width))] * 2,
        compiler_params=params(),
        cost_estimate=cost(4 * count * depth * width, 2 * count * depth),
    )(rows, wk, wv)


def slide_of(place, slides, block):
    end, total = jnp.int32(0), jnp.zeros_like(block)
    for index in range(slides):
        end = end + place[index]
        total = total + (block >= end).astype(jnp.int32)
    return total


def mask_kernel(slides, subs, spans, few, place, asking, asked):
    span, sub = place[slides], place[slides + 1]
    slide = [slide_of(place, slides, span * subs + (sub ^ r)) for r in range(subs)]
    lane = lax.broadcasted_iota(jnp.int32, (BLOCK, HEAD_SIZE), 1)
    for r in range(subs):
        rows = slice(r * BLOCK, (r + 1) * BLOCK)
        apart = (lane <= slides) & (lane != slide[r])
        asking[rows, :] = jnp.where(apart, HIDDEN, 0.0).astype(BF16)
        asked[rows, :] = jnp.where(lane == slide[r], 1.0, 0.0).astype(BF16)
    count = min(spans, GROUP) * FAR_ROWS
    row = lax.broadcasted_iota(jnp.int32, (count, HEAD_SIZE), 0)
    lane = lax.broadcasted_iota(jnp.int32, (count, HEAD_SIZE), 1)
    upper = (row // DILATED_KEPT) % BLOCKS_HALF
    for half in range(subs // BLOCKS_HALF):
        place_0, place_1 = sub ^ (half * BLOCKS_HALF), sub ^ (half * BLOCKS_HALF + 1)
        for group in range(spans * FAR_ROWS // count):
            far = row // FAR_ROWS
            if few:
                order = [bit | y for y in (0, Y_BIT) for bit in (0, *Z_BITS)]
                place_of = jnp.zeros_like(far)
                for index, bits in enumerate(order):
                    place_of = jnp.where(far == index, bits, place_of)
                far = place_of ^ span
            else:
                far = far + group * GROUP
            theirs = slide_of(place, slides, far * subs + jnp.where(upper == 0, place_0, place_1))
            marked = (lane == theirs) | ((lane == slides) & (far == span))
            start = subs * BLOCK + (half * spans * FAR_ROWS + group * count)
            asked[start : start + count, :] = jnp.where(marked, 1.0, 0.0).astype(BF16)


def make_masks(place, slides, subs, spans, few):
    keys = subs * BLOCK + subs // BLOCKS_HALF * spans * FAR_ROWS
    return pl.pallas_call(
        functools.partial(mask_kernel, slides, subs, spans, few),
        in_specs=[IN_SMEM],
        out_specs=[IN_VMEM] * 2,
        out_shape=[shape((subs * BLOCK, HEAD_SIZE)), shape((keys, HEAD_SIZE))],
        compiler_params=params(),
        cost_estimate=cost(64 * keys * HEAD_SIZE, 2 * keys * HEAD_SIZE),
    )(place)


def scores_of(keys, queries):
    return dot_t(keys, queries)


def gather(values, weight):
    return lax.dot_general(
        values, weight.astype(BF16), (((0,), (0,)), ((), ())), preferred_element_type=F32
    )


def begin(queries, keys, values):
    scores = [scores_of(k, q) for k, q in zip(keys, queries)]
    peak = [jnp.max(each, axis=0, keepdims=True) for each in scores]
    weight = [jnp.exp2((each - top) * SCALE) for each, top in zip(scores, peak)]
    total = [jnp.sum(each, axis=0, keepdims=True) for each in weight]
    return peak, total, [gather(v, each) for v, each in zip(values, weight)]


def update(queries, keys, values, state):
    scores = [scores_of(k, q) for k, q in zip(keys, queries)]
    higher = [
        jnp.maximum(top, jnp.max(each, axis=0, keepdims=True))
        for top, each in zip(state[0], scores)
    ]
    shrink = [jnp.exp2((top - new) * SCALE) for top, new in zip(state[0], higher)]
    weight = [jnp.exp2((each - new) * SCALE) for each, new in zip(scores, higher)]
    total = [
        old * less + jnp.sum(each, axis=0, keepdims=True)
        for old, less, each in zip(state[1], shrink, weight)
    ]
    added = [gather(v, each) for v, each in zip(values, weight)]
    return higher, total, [old * less + new for old, less, new in zip(state[2], shrink, added)]


def attend_kernel(first_row, near, halves, few, finish, asking, asked_of, *refs):
    refs = list(refs)
    queries = refs.pop(0)
    if near:
        keys, values = refs[0:4], refs[4:8]
        del refs[:8]
    else:
        gathered_in, stats_in = refs[0:2]
        del refs[:2]
    far = []
    for half, size in halves:
        far.append((half, refs[:size]))
        del refs[:size]
    rows = queries.shape[0]
    span = asking.shape[0]
    half_count = (asked_of.shape[0] - span) // BLOCKS_HALF

    heads = queries.shape[1] // HEAD_SIZE
    group = 1 if not few else min(2, heads) if near else heads

    def some_heads(turn, _):
        those = [turn * group + i for i in range(group)]
        columns = [
            pl.ds(pl.multiple_of(head * HEAD_SIZE, HEAD_SIZE), HEAD_SIZE)
            if group < heads
            else slice(head * HEAD_SIZE, (head + 1) * HEAD_SIZE)
            for head in those
        ]
        row_marks = asking[first_row : first_row + rows, :]
        asked = [jnp.concatenate([queries[:, each], row_marks], axis=1) for each in columns]

        def marked(parts, where):
            return jnp.concatenate([jnp.concatenate(parts, axis=0), asked_of[where, :]], axis=1)

        def ready(head, each):
            keyed, valued = [], []
            if near:
                keyed.append(marked([ref[:, each] for ref in keys], slice(0, span)))
                valued += [ref[:, each] for ref in values]
            if few:
                for half, parts in far:
                    start = span + half * half_count
                    pieces = [(ref, i) for ref in parts for i in range(ref.shape[0])]
                    where = slice(start, start + half_count)
                    keyed.append(marked([ref[i, 0, head] for ref, i in pieces], where))
                    valued += [ref[i, 1, head] for ref, i in pieces]
            return jnp.concatenate(keyed, axis=0), jnp.concatenate(valued, axis=0)

        if near:
            state = begin(asked, *zip(*map(ready, those, columns)))
        else:
            state = (
                [stats_in[head, 0:1, :] for head in those],
                [stats_in[head, 1:2, :] for head in those],
                [gathered_in[head] for head in those],
            )
            if few:
                state = update(asked, *zip(*map(ready, those, columns)), state)
        if not few:
            for half, (part,) in far:
                start = span + half * half_count

                def step(number, state, start=start, part=part):
                    base = number * GROUP
                    width = GROUP * FAR_ROWS
                    where = pl.ds(pl.multiple_of(start + number * width, width), width)
                    found = [
                        [
                            marked([part[base + i, 0, head] for i in range(GROUP)], where)
                            for head in those
                        ],
                        [
                            jnp.concatenate([part[base + i, 1, head] for i in range(GROUP)], axis=0)
                            for head in those
                        ],
                    ]
                    return update(asked, *found, state)

                state = lax.fori_loop(0, part.shape[0] // GROUP, step, state)
        for head, each, peak, total, gathered in zip(those, columns, *state):
            if finish:
                keep, send = refs
                context = (gathered / total).T.astype(BF16)
                keep[:, each] = context[:BLOCK]
                send[:, each] = context[BLOCK:]
            else:
                gathered_out, stats_out = refs
                gathered_out[head] = gathered
                stats_out[head, 0:1, :] = peak
                stats_out[head, 1:2, :] = total
        return 0

    if group == heads:
        some_heads(0, 0)
    else:
        lax.fori_loop(0, heads // group, some_heads, 0)


def attend(masks, few, first_row, queries, halves, near=None, begun=None, finish=True):
    rows, width = queries.shape
    heads = width // HEAD_SIZE
    operands = [*masks, queries]
    operands += [*near[0], *near[1]] if near else list(begun)
    columns = masks[0].shape[0] if near else 0
    for _, parts in halves:
        operands += parts
    far_bytes = sum(2 * part.size for _, parts in halves for part in parts)
    columns += far_bytes // (4 * width)
    if finish:
        out_shape = [shape((BLOCK, width))] * 2
    else:
        out_shape = [shape((heads, HEAD_SIZE, rows), F32), shape((heads, 8, rows), F32)]
    return pl.pallas_call(
        functools.partial(
            attend_kernel,
            first_row,
            near is not None,
            [(half, len(parts)) for half, parts in halves],
            few,
            finish,
        ),
        in_specs=[IN_VMEM] * len(operands),
        out_specs=[IN_VMEM] * 2,
        out_shape=out_shape,
        compiler_params=params(far_bytes),
        cost_estimate=cost(
            4 * rows * columns * width, 4 * rows * width, heads * rows * columns
        ),
    )(*operands)


def mix_kernel(rows_0, rows_1, weight_0, weight_1, out):
    tile = min(512, out.shape[1])
    for index in range(out.shape[1] // tile):
        part = slice(index * tile, (index + 1) * tile)
        total = dot(rows_0[...], weight_0[:, part]) + dot(rows_1[...], weight_1[:, part])
        out[:, part] = total.astype(out.dtype)


def mix(rows_0, rows_1, weight_0, weight_1, dtype):
    rows, depth = rows_0.shape
    width = weight_0.shape[1]
    return pl.pallas_call(
        mix_kernel,
        in_specs=[IN_VMEM] * 4,
        out_specs=IN_VMEM,
        out_shape=shape((rows, width), dtype),
        compiler_params=params(),
        cost_estimate=cost(4 * rows * depth * width, 4 * rows * width),
    )(rows_0, rows_1, weight_0, weight_1)


def shards(seqs, subs, normed, w_query, w_key, w_value, w_out, pattern, slide_lengths):
    slides = slide_lengths.shape[0]
    axes = [lax.axis_index(name).astype(jnp.int32)[None] for name in ("seq", "sub")]
    few = seqs == GROUP

    def swap(array, bit, axis="sub"):
        count = subs if axis == "sub" else seqs
        return lax.ppermute(array, axis, [(i, i ^ bit) for i in range(count)])

    def after(array, *others):
        return lax.optimization_barrier((array, *others))[0]

    def first_round(kept):
        return [swap(kept, bit, "seq") for bit in Z_BITS]

    def second_round(pieces):
        column = jnp.stack(pieces)
        return [column, swap(column, Y_BIT, "seq")]

    across = swap(normed, 2)
    beside = swap(normed, 1)
    mine, wk, wv, keys_0, values_0 = first(normed, w_key, w_value)
    keys_1, values_1, kept_a = second(beside, wk, wv, keys_0, values_0, pattern)
    place = jnp.concatenate([after(slide_lengths, kept_a), *axes])
    masks = list(make_masks(place, slides, subs, seqs, few))
    wo_beside = swap(w_out, 1)
    if few:
        along_z = first_round(kept_a)
        *along_z, masks[0] = lax.optimization_barrier((*along_z, masks[0]))
        half_a = 0, second_round([kept_a, *along_z])
        across = after(across, masks[0], wo_beside)
    else:
        half_a = 0, [lax.all_gather(kept_a, "seq", axis=0)]
    wo_beside = pltpu.with_memory_space_constraint(wo_beside, pltpu.VMEM)
    beyond = swap(across, 1)
    if few:
        beyond = after(beyond, half_a[1][0])
    keys_2, values_2 = keys_and_values(across, wk, wv)
    keys_3, values_3, kept_b = second(after(beyond, keys_2), wk, wv, keys_2, values_2, pattern)
    query_b, wq, kept_again = query(across, beyond, w_query, kept_b)
    near = [keys_0, keys_1, keys_2, keys_3], [values_0, values_1, values_2, values_3]
    call = functools.partial(attend, masks, few)
    if few:
        along_z = first_round(kept_b)
        along_y = swap(kept_again, Y_BIT, "seq")
        *along_z, along_y, query_b, half_a[1][1] = lax.optimization_barrier(
            (*along_z, along_y, query_b, half_a[1][1])
        )
        column, other = second_round(along_z)
        half_b = 1, [kept_b[None], column, along_y[None], other]
        asked = after(query_b, column)
        mine = after(mine, column)
        begun = call(2 * BLOCK, asked, [half_a], near=near, finish=False)
    else:
        half_b = 1, [lax.all_gather(kept_b, "seq", axis=0)]
        begun = call(2 * BLOCK, query_b, [half_a], near=near, finish=False)
    query_a, wo = last_query(mine, beside, wq, w_out)
    query_b = after(query_b, query_a)
    keep_b, send_b = call(2 * BLOCK, query_b, [half_b], begun=begun)
    other_b = swap(send_b, 1)
    leaving = mix(keep_b, other_b, wo, wo_beside, BF16)
    arriving = swap(leaving, 2)
    query_a = after(query_a, leaving)
    keep_a, send_a = call(0, query_a, [half_a, half_b], near=near)
    other_a = swap(send_a, 1)
    own = mix(keep_a, other_a, wo, wo_beside, F32)
    return (own + arriving.astype(F32)).astype(BF16)


def solution(mesh):
    placed = (
        P(("seq", "sub"), None),
        P(None, "sub"),
        P(None, "sub"),
        P(None, "sub"),
        P("sub", None),
        P("sub", None),
        P(),
    )
    return jax.shard_map(
        functools.partial(shards, mesh.shape["seq"], mesh.shape["sub"]),
        mesh=mesh,
        in_specs=placed,
        out_specs=P(("seq", "sub"), None),
        check_vma=False,
    )
```

```python
import functools
import math

import jax
import jax.numpy as jnp
from jax import lax
from jax.experimental import pallas as pl
from jax.experimental.pallas import tpu as pltpu
from jax.sharding import PartitionSpec as P

HEAD_SIZE = 128
BLOCK = 128
DILATED_KEPT = 16
BLOCKS_HALF = 2
FAR_ROWS = BLOCKS_HALF * DILATED_KEPT
GROUP = 8
STREAMS = 8
HIDDEN = -1e30
SCALE = math.log2(math.e) / math.sqrt(HEAD_SIZE)
BF16 = jnp.bfloat16
F32 = jnp.float32
IN_VMEM = pl.BlockSpec(memory_space=pltpu.VMEM)
IN_HBM = pl.BlockSpec(memory_space=pltpu.HBM)
IN_SMEM = pl.BlockSpec(memory_space=pltpu.SMEM)
Y_BIT = 1
Z_BITS = (4, 6, 2)


def dot(a, b):
    return jnp.dot(a, b, preferred_element_type=F32)


def dot_t(a, b):
    return lax.dot_general(a, b, (((1,), (1,)), ((), ())), preferred_element_type=F32)


def params(extra=0):
    return pltpu.CompilerParams(vmem_limit_bytes=16 * 2**20 + extra)


def cost(flops, bytes_accessed, transcendentals=0):
    return pl.CostEstimate(
        flops=flops // 100,
        bytes_accessed=bytes_accessed // 100,
        transcendentals=transcendentals // 100,
    )


def shape(dims, dtype=BF16):
    return jax.ShapeDtypeStruct(tuple(dims), dtype)


def keep_in_hbm(array):
    return pltpu.with_memory_space_constraint(array, pltpu.HBM)


def start_copies(source, target, sems, base):
    rows = source.shape[0] // STREAMS
    copies = []
    for index in range(STREAMS):
        where = slice(index * rows, (index + 1) * rows)
        copy = pltpu.make_async_copy(source.at[where, :], target.at[where, :], sems.at[base + index])
        copy.start()
        copies.append(copy)
    return copies


def halves_of(width):
    tile = min(256, width)
    return [slice(i * tile, (i + 1) * tile) for i in range(width // tile)]


def pick_dilated(pattern, blocks, kept):
    positions = lax.broadcasted_iota(jnp.int32, (BLOCK, BLOCK), 0)
    for head in range(kept.shape[1]):
        row = pattern[head : head + 1, :]
        chosen = (positions == row).astype(F32).T[:DILATED_KEPT].astype(BF16)
        for index, block in enumerate(blocks):
            picked = dot(chosen, jnp.concatenate(block(head), axis=1)).astype(BF16)
            spot = slice(index * DILATED_KEPT, (index + 1) * DILATED_KEPT)
            kept[0, head, spot, :] = picked[:, :HEAD_SIZE]
            kept[1, head, spot, :] = picked[:, HEAD_SIZE:]


def head_of(ref, head, rows=slice(None)):
    return ref[rows, head * HEAD_SIZE : (head + 1) * HEAD_SIZE]


def first_kernel(rows_hbm, wk_hbm, wv_hbm, rows, wk, wv, keys, values, sems):
    whole = pltpu.make_async_copy(rows_hbm, rows, sems.at[0])
    whole.start()
    key_copies = start_copies(wk_hbm, wk, sems, 1)
    value_copies = start_copies(wv_hbm, wv, sems, 1 + STREAMS)
    whole.wait()
    for copies, weight, out in ((key_copies, wk, keys), (value_copies, wv, values)):
        for copy in copies:
            copy.wait()
        for part in halves_of(wk.shape[1]):
            out[:, part] = dot(rows[...], weight[:, part]).astype(BF16)


def first(rows, w_key, w_value):
    count, depth = rows.shape
    width = w_key.shape[1]
    return pl.pallas_call(
        first_kernel,
        in_specs=[IN_HBM] * 3,
        out_specs=[IN_VMEM] * 5,
        out_shape=[
            pltpu.VMEM(rows.shape, BF16),
            pltpu.VMEM(w_key.shape, BF16),
            pltpu.VMEM(w_value.shape, BF16),
            shape((count, width)),
            shape((count, width)),
        ],
        scratch_shapes=[pltpu.SemaphoreType.DMA((1 + 2 * STREAMS,))],
        compiler_params=params(),
        cost_estimate=cost(4 * count * depth * width, 4 * depth * width),
    )(keep_in_hbm(rows), keep_in_hbm(w_key), keep_in_hbm(w_value))


def second_kernel(rows, wk, wv, keys_0, values_0, pattern, keys, values, kept):
    for part in halves_of(wk.shape[1]):
        keys[:, part] = dot(rows[...], wk[:, part]).astype(BF16)
        values[:, part] = dot(rows[...], wv[:, part]).astype(BF16)
    blocks = [
        lambda head: (head_of(keys_0, head), head_of(values_0, head)),
        lambda head: (head_of(keys, head), head_of(values, head)),
    ]
    pick_dilated(pattern, blocks, kept)


def second(rows, wk, wv, keys_0, values_0, pattern):
    count, depth = rows.shape
    width = wk.shape[1]
    kept = (2, width // HEAD_SIZE, FAR_ROWS, HEAD_SIZE)
    return pl.pallas_call(
        second_kernel,
        in_specs=[IN_VMEM] * 6,
        out_specs=[IN_VMEM] * 3,
        out_shape=[shape((count, width))] * 2 + [shape(kept)],
        compiler_params=params(),
        cost_estimate=cost(4 * count * depth * width, 2 * count * depth),
    )(rows, wk, wv, keys_0, values_0, pattern)


def query_kernel(*refs):
    rows, (wq_hbm, w_hbm), outs, (wq, sems) = refs[:4], refs[4:6], refs[6:9], refs[9:]
    copies = start_copies(wq_hbm, wq, sems, 0)
    more = start_copies(w_hbm, outs[2], sems, STREAMS)
    for copy in copies:
        copy.wait()
    for pair, out in ((rows[2:], outs[1]), (rows[:2], outs[0])):
        both = jnp.concatenate([ref[...] for ref in pair], axis=0)
        for part in halves_of(wq.shape[1]):
            out[:, part] = dot(both, wq[:, part]).astype(BF16)
    for copy in more:
        copy.wait()


def query(rows, w_query, w_out):
    count, depth = rows[0].shape
    width = w_query.shape[1]
    return pl.pallas_call(
        query_kernel,
        in_specs=[IN_VMEM] * 4 + [IN_HBM] * 2,
        out_specs=[IN_VMEM] * 3,
        out_shape=[shape((2 * count, width))] * 2 + [pltpu.VMEM(w_out.shape, BF16)],
        scratch_shapes=[
            pltpu.VMEM(w_query.shape, BF16),
            pltpu.SemaphoreType.DMA((2 * STREAMS,)),
        ],
        compiler_params=params(),
        cost_estimate=cost(8 * count * depth * width, 4 * depth * width),
    )(*rows, keep_in_hbm(w_query), keep_in_hbm(w_out))


def again_kernel(source, out):
    out[...] = source[...]


def again(kept):
    return pl.pallas_call(
        again_kernel,
        in_specs=[IN_VMEM],
        out_specs=IN_VMEM,
        out_shape=shape(kept.shape),
        compiler_params=params(),
        cost_estimate=cost(0, 4 * kept.size),
    )(kept)


def across_kernel(rows, wk, wv, keys, values):
    for part in halves_of(wk.shape[1]):
        keys[:, part] = dot(rows[...], wk[:, part]).astype(BF16)
        values[:, part] = dot(rows[...], wv[:, part]).astype(BF16)


def keys_and_values(rows, wk, wv):
    count, depth = rows.shape
    width = wk.shape[1]
    return pl.pallas_call(
        across_kernel,
        in_specs=[IN_VMEM] * 3,
        out_specs=[IN_VMEM] * 2,
        out_shape=[shape((count, width))] * 2,
        compiler_params=params(),
        cost_estimate=cost(4 * count * depth * width, 2 * count * depth),
    )(rows, wk, wv)


def slide_of(place, slides, block):
    end, total = jnp.int32(0), jnp.zeros_like(block)
    for index in range(slides):
        end = end + place[index]
        total = total + (block >= end).astype(jnp.int32)
    return total


def mask_kernel(slides, subs, spans, few, place, asking, asked):
    span, sub = place[slides], place[slides + 1]
    slide = [slide_of(place, slides, span * subs + (sub ^ r)) for r in range(subs)]
    lane = lax.broadcasted_iota(jnp.int32, (BLOCK, HEAD_SIZE), 1)
    for r in range(subs):
        rows = slice(r * BLOCK, (r + 1) * BLOCK)
        apart = (lane <= slides) & (lane != slide[r])
        asking[rows, :] = jnp.where(apart, HIDDEN, 0.0).astype(BF16)
        asked[rows, :] = jnp.where(lane == slide[r], 1.0, 0.0).astype(BF16)
    count = min(spans, GROUP) * FAR_ROWS
    row = lax.broadcasted_iota(jnp.int32, (count, HEAD_SIZE), 0)
    lane = lax.broadcasted_iota(jnp.int32, (count, HEAD_SIZE), 1)
    upper = (row // DILATED_KEPT) % BLOCKS_HALF
    for half in range(subs // BLOCKS_HALF):
        place_0, place_1 = sub ^ (half * BLOCKS_HALF), sub ^ (half * BLOCKS_HALF + 1)
        for group in range(spans * FAR_ROWS // count):
            far = row // FAR_ROWS
            if few:
                order = [bit | y for y in (0, Y_BIT) for bit in (0, *Z_BITS)]
                place_of = jnp.zeros_like(far)
                for index, bits in enumerate(order):
                    place_of = jnp.where(far == index, bits, place_of)
                far = place_of ^ span
            else:
                far = far + group * GROUP
            theirs = slide_of(place, slides, far * subs + jnp.where(upper == 0, place_0, place_1))
            marked = (lane == theirs) | ((lane == slides) & (far == span))
            start = subs * BLOCK + (half * spans * FAR_ROWS + group * count)
            asked[start : start + count, :] = jnp.where(marked, 1.0, 0.0).astype(BF16)


def make_masks(place, slides, subs, spans, few):
    keys = subs * BLOCK + subs // BLOCKS_HALF * spans * FAR_ROWS
    return pl.pallas_call(
        functools.partial(mask_kernel, slides, subs, spans, few),
        in_specs=[IN_SMEM],
        out_specs=[IN_VMEM] * 2,
        out_shape=[shape((subs * BLOCK, HEAD_SIZE)), shape((keys, HEAD_SIZE))],
        compiler_params=params(),
        cost_estimate=cost(64 * keys * HEAD_SIZE, 2 * keys * HEAD_SIZE),
    )(place)


def scores_of(keys, queries):
    return dot_t(keys, queries)


def gather(values, weight):
    return lax.dot_general(
        values, weight.astype(BF16), (((0,), (0,)), ((), ())), preferred_element_type=F32
    )


def begin(queries, keys, values):
    scores = [scores_of(k, q) for k, q in zip(keys, queries)]
    peak = [jnp.max(each, axis=0, keepdims=True) for each in scores]
    weight = [jnp.exp2((each - top) * SCALE) for each, top in zip(scores, peak)]
    total = [jnp.sum(each, axis=0, keepdims=True) for each in weight]
    return peak, total, [gather(v, each) for v, each in zip(values, weight)]


def update(queries, keys, values, state):
    scores = [scores_of(k, q) for k, q in zip(keys, queries)]
    higher = [
        jnp.maximum(top, jnp.max(each, axis=0, keepdims=True))
        for top, each in zip(state[0], scores)
    ]
    shrink = [jnp.exp2((top - new) * SCALE) for top, new in zip(state[0], higher)]
    weight = [jnp.exp2((each - new) * SCALE) for each, new in zip(scores, higher)]
    total = [
        old * less + jnp.sum(each, axis=0, keepdims=True)
        for old, less, each in zip(state[1], shrink, weight)
    ]
    added = [gather(v, each) for v, each in zip(values, weight)]
    return higher, total, [old * less + new for old, less, new in zip(state[2], shrink, added)]


def attend_kernel(first_row, near, halves, few, finish, asking, asked_of, *refs):
    refs = list(refs)
    queries = refs.pop(0)
    if near:
        keys, values = refs[0:4], refs[4:8]
        del refs[:8]
    else:
        gathered_in, stats_in = refs[0:2]
        del refs[:2]
    far = []
    for half, size in halves:
        far.append((half, refs[:size]))
        del refs[:size]
    rows = queries.shape[0]
    span = asking.shape[0]
    half_count = (asked_of.shape[0] - span) // BLOCKS_HALF

    heads = queries.shape[1] // HEAD_SIZE
    group = 1 if not few else min(2, heads) if near else heads

    def some_heads(turn, _):
        those = [turn * group + i for i in range(group)]
        columns = [
            pl.ds(pl.multiple_of(head * HEAD_SIZE, HEAD_SIZE), HEAD_SIZE)
            if group < heads
            else slice(head * HEAD_SIZE, (head + 1) * HEAD_SIZE)
            for head in those
        ]
        row_marks = asking[first_row : first_row + rows, :]
        asked = [jnp.concatenate([queries[:, each], row_marks], axis=1) for each in columns]

        def marked(parts, where):
            return jnp.concatenate([jnp.concatenate(parts, axis=0), asked_of[where, :]], axis=1)

        def ready(head, each):
            keyed, valued = [], []
            if near:
                keyed.append(marked([ref[:, each] for ref in keys], slice(0, span)))
                valued += [ref[:, each] for ref in values]
            if few:
                for half, parts in far:
                    start = span + half * half_count
                    pieces = [(ref, i) for ref in parts for i in range(ref.shape[0])]
                    where = slice(start, start + half_count)
                    keyed.append(marked([ref[i, 0, head] for ref, i in pieces], where))
                    valued += [ref[i, 1, head] for ref, i in pieces]
            return jnp.concatenate(keyed, axis=0), jnp.concatenate(valued, axis=0)

        if near:
            state = begin(asked, *zip(*map(ready, those, columns)))
        else:
            state = (
                [stats_in[head, 0:1, :] for head in those],
                [stats_in[head, 1:2, :] for head in those],
                [gathered_in[head] for head in those],
            )
            if few:
                state = update(asked, *zip(*map(ready, those, columns)), state)
        if not few:
            for half, (part,) in far:
                start = span + half * half_count

                def step(number, state, start=start, part=part):
                    base = number * GROUP
                    width = GROUP * FAR_ROWS
                    where = pl.ds(pl.multiple_of(start + number * width, width), width)
                    found = [
                        [
                            marked([part[base + i, 0, head] for i in range(GROUP)], where)
                            for head in those
                        ],
                        [
                            jnp.concatenate([part[base + i, 1, head] for i in range(GROUP)], axis=0)
                            for head in those
                        ],
                    ]
                    return update(asked, *found, state)

                state = lax.fori_loop(0, part.shape[0] // GROUP, step, state)
        for head, each, peak, total, gathered in zip(those, columns, *state):
            if finish:
                keep, send = refs
                context = (gathered / total).T.astype(BF16)
                keep[:, each] = context[:BLOCK]
                send[:, each] = context[BLOCK:]
            else:
                gathered_out, stats_out = refs
                gathered_out[head] = gathered
                stats_out[head, 0:1, :] = peak
                stats_out[head, 1:2, :] = total
        return 0

    if group == heads:
        some_heads(0, 0)
    else:
        lax.fori_loop(0, heads // group, some_heads, 0)


def attend(masks, few, first_row, queries, halves, near=None, begun=None, finish=True):
    rows, width = queries.shape
    heads = width // HEAD_SIZE
    operands = [*masks, queries]
    operands += [*near[0], *near[1]] if near else list(begun)
    columns = masks[0].shape[0] if near else 0
    for _, parts in halves:
        operands += parts
    far_bytes = sum(2 * part.size for _, parts in halves for part in parts)
    columns += far_bytes // (4 * width)
    if finish:
        out_shape = [shape((BLOCK, width))] * 2
    else:
        out_shape = [shape((heads, HEAD_SIZE, rows), F32), shape((heads, 8, rows), F32)]
    return pl.pallas_call(
        functools.partial(
            attend_kernel,
            first_row,
            near is not None,
            [(half, len(parts)) for half, parts in halves],
            few,
            finish,
        ),
        in_specs=[IN_VMEM] * len(operands),
        out_specs=[IN_VMEM] * 2,
        out_shape=out_shape,
        compiler_params=params(far_bytes),
        cost_estimate=cost(
            4 * rows * columns * width, 4 * rows * width, heads * rows * columns
        ),
    )(*operands)


def mix_kernel(rows_0, rows_1, weight_0, weight_1, out):
    tile = min(512, out.shape[1])
    for index in range(out.shape[1] // tile):
        part = slice(index * tile, (index + 1) * tile)
        total = dot(rows_0[...], weight_0[:, part]) + dot(rows_1[...], weight_1[:, part])
        out[:, part] = total.astype(out.dtype)


def mix(rows_0, rows_1, weight_0, weight_1, dtype):
    rows, depth = rows_0.shape
    width = weight_0.shape[1]
    return pl.pallas_call(
        mix_kernel,
        in_specs=[IN_VMEM] * 4,
        out_specs=IN_VMEM,
        out_shape=shape((rows, width), dtype),
        compiler_params=params(),
        cost_estimate=cost(4 * rows * depth * width, 4 * rows * width),
    )(rows_0, rows_1, weight_0, weight_1)


def shards(seqs, subs, normed, w_query, w_key, w_value, w_out, pattern, slide_lengths):
    slides = slide_lengths.shape[0]
    axes = [lax.axis_index(name).astype(jnp.int32)[None] for name in ("seq", "sub")]
    few = seqs == GROUP

    def swap(array, bit, axis="sub"):
        count = subs if axis == "sub" else seqs
        return lax.ppermute(array, axis, [(i, i ^ bit) for i in range(count)])

    def after(array, *others):
        return lax.optimization_barrier((array, *others))[0]

    def first_round(kept):
        return [swap(kept, bit, "seq") for bit in Z_BITS]

    def second_round(pieces):
        column = jnp.stack(pieces)
        return [column, swap(column, Y_BIT, "seq")]

    across = swap(normed, 2)
    beside = swap(normed, 1)
    mine, wk, wv, keys_0, values_0 = first(normed, w_key, w_value)
    keys_1, values_1, kept_a = second(beside, wk, wv, keys_0, values_0, pattern)
    place = jnp.concatenate([after(slide_lengths, kept_a), *axes])
    masks = list(make_masks(place, slides, subs, seqs, few))
    wo_beside = swap(w_out, 1)
    if few:
        along_z = first_round(kept_a)
        *along_z, masks[0] = lax.optimization_barrier((*along_z, masks[0]))
        half_a = 0, second_round([kept_a, *along_z])
        across = after(across, masks[0], wo_beside)
    else:
        half_a = 0, [lax.all_gather(kept_a, "seq", axis=0)]
    wo_beside = pltpu.with_memory_space_constraint(wo_beside, pltpu.VMEM)
    beyond = swap(across, 1)
    if few:
        beyond = after(beyond, half_a[1][0])
    keys_2, values_2 = keys_and_values(across, wk, wv)
    keys_3, values_3, kept_b = second(after(beyond, keys_2), wk, wv, keys_2, values_2, pattern)
    near = [keys_0, keys_1, keys_2, keys_3], [values_0, values_1, values_2, values_3]
    call = functools.partial(attend, masks, few)
    if few:
        along_z = first_round(kept_b)
        along_y = swap(again(kept_b), Y_BIT, "seq")
        *along_z, along_y, half_a[1][1] = lax.optimization_barrier(
            (*along_z, along_y, half_a[1][1])
        )
        column, other = second_round(along_z)
        half_b = 1, [kept_b[None], column, along_y[None], other]
        mine = after(mine, column)
    else:
        half_b = 1, [lax.all_gather(kept_b, "seq", axis=0)]
    query_a, query_b, wo = query([mine, beside, across, beyond], w_query, w_out)
    begun = call(2 * BLOCK, query_b, [half_a], near=near, finish=False)
    keep_b, send_b = call(2 * BLOCK, query_b, [half_b], begun=begun)
    other_b = swap(send_b, 1)
    leaving = mix(keep_b, other_b, wo, wo_beside, BF16)
    arriving = swap(leaving, 2)
    query_a = after(query_a, leaving)
    keep_a, send_a = call(0, query_a, [half_a, half_b], near=near)
    other_a = swap(send_a, 1)
    own = mix(keep_a, other_a, wo, wo_beside, F32)
    return (own + arriving.astype(F32)).astype(BF16)


def solution(mesh):
    placed = (
        P(("seq", "sub"), None),
        P(None, "sub"),
        P(None, "sub"),
        P(None, "sub"),
        P("sub", None),
        P("sub", None),
        P(),
    )
    return jax.shard_map(
        functools.partial(shards, mesh.shape["seq"], mesh.shape["sub"]),
        mesh=mesh,
        in_specs=placed,
        out_specs=P(("seq", "sub"), None),
        check_vma=False,
    )
```

```python
import functools
import math

import jax
import jax.numpy as jnp
from jax import lax
from jax.experimental import pallas as pl
from jax.experimental.pallas import tpu as pltpu
from jax.sharding import PartitionSpec as P

HEAD_SIZE = 128
BLOCK = 128
DILATED_KEPT = 16
BLOCKS_HALF = 2
FAR_ROWS = BLOCKS_HALF * DILATED_KEPT
GROUP = 8
STREAMS = 8
HIDDEN = -1e30
SCALE = math.log2(math.e) / math.sqrt(HEAD_SIZE)
BF16 = jnp.bfloat16
F32 = jnp.float32
IN_VMEM = pl.BlockSpec(memory_space=pltpu.VMEM)
IN_HBM = pl.BlockSpec(memory_space=pltpu.HBM)
IN_SMEM = pl.BlockSpec(memory_space=pltpu.SMEM)
Y_BIT = 1
Z_BITS = (4, 6, 2)


def dot(a, b):
    return jnp.dot(a, b, preferred_element_type=F32)


def dot_t(a, b):
    return lax.dot_general(a, b, (((1,), (1,)), ((), ())), preferred_element_type=F32)


def params(extra=0):
    return pltpu.CompilerParams(vmem_limit_bytes=16 * 2**20 + extra)


def cost(flops, bytes_accessed, transcendentals=0):
    return pl.CostEstimate(
        flops=flops // 100,
        bytes_accessed=bytes_accessed // 100,
        transcendentals=transcendentals // 100,
    )


def shape(dims, dtype=BF16):
    return jax.ShapeDtypeStruct(tuple(dims), dtype)


def keep_in_hbm(array):
    return pltpu.with_memory_space_constraint(array, pltpu.HBM)


def start_copies(source, target, sems, base):
    rows = source.shape[0] // STREAMS
    copies = []
    for index in range(STREAMS):
        where = slice(index * rows, (index + 1) * rows)
        copy = pltpu.make_async_copy(source.at[where, :], target.at[where, :], sems.at[base + index])
        copy.start()
        copies.append(copy)
    return copies


def halves_of(width):
    tile = min(256, width)
    return [slice(i * tile, (i + 1) * tile) for i in range(width // tile)]


def pick_dilated(pattern, blocks, kept):
    positions = lax.broadcasted_iota(jnp.int32, (BLOCK, BLOCK), 0)
    for head in range(kept.shape[1]):
        row = pattern[head : head + 1, :]
        chosen = (positions == row).astype(F32).T[:DILATED_KEPT].astype(BF16)
        for index, block in enumerate(blocks):
            picked = dot(chosen, jnp.concatenate(block(head), axis=1)).astype(BF16)
            spot = slice(index * DILATED_KEPT, (index + 1) * DILATED_KEPT)
            kept[0, head, spot, :] = picked[:, :HEAD_SIZE]
            kept[1, head, spot, :] = picked[:, HEAD_SIZE:]


def head_of(ref, head, rows=slice(None)):
    return ref[rows, head * HEAD_SIZE : (head + 1) * HEAD_SIZE]


def first_kernel(rows_hbm, wk_hbm, wv_hbm, rows, wk, wv, keys, values, sems):
    whole = pltpu.make_async_copy(rows_hbm, rows, sems.at[0])
    whole.start()
    key_copies = start_copies(wk_hbm, wk, sems, 1)
    value_copies = start_copies(wv_hbm, wv, sems, 1 + STREAMS)
    whole.wait()
    for copies, weight, out in ((key_copies, wk, keys), (value_copies, wv, values)):
        for copy in copies:
            copy.wait()
        for part in halves_of(wk.shape[1]):
            out[:, part] = dot(rows[...], weight[:, part]).astype(BF16)


def first(rows, w_key, w_value):
    count, depth = rows.shape
    width = w_key.shape[1]
    return pl.pallas_call(
        first_kernel,
        in_specs=[IN_HBM] * 3,
        out_specs=[IN_VMEM] * 5,
        out_shape=[
            pltpu.VMEM(rows.shape, BF16),
            pltpu.VMEM(w_key.shape, BF16),
            pltpu.VMEM(w_value.shape, BF16),
            shape((count, width)),
            shape((count, width)),
        ],
        scratch_shapes=[pltpu.SemaphoreType.DMA((1 + 2 * STREAMS,))],
        compiler_params=params(),
        cost_estimate=cost(4 * count * depth * width, 4 * depth * width),
    )(keep_in_hbm(rows), keep_in_hbm(w_key), keep_in_hbm(w_value))


def second_kernel(rows, wk, wv, keys_0, values_0, pattern, keys, values, kept):
    for part in halves_of(wk.shape[1]):
        keys[:, part] = dot(rows[...], wk[:, part]).astype(BF16)
        values[:, part] = dot(rows[...], wv[:, part]).astype(BF16)
    blocks = [
        lambda head: (head_of(keys_0, head), head_of(values_0, head)),
        lambda head: (head_of(keys, head), head_of(values, head)),
    ]
    pick_dilated(pattern, blocks, kept)


def second(rows, wk, wv, keys_0, values_0, pattern):
    count, depth = rows.shape
    width = wk.shape[1]
    kept = (2, width // HEAD_SIZE, FAR_ROWS, HEAD_SIZE)
    return pl.pallas_call(
        second_kernel,
        in_specs=[IN_VMEM] * 6,
        out_specs=[IN_VMEM] * 3,
        out_shape=[shape((count, width))] * 2 + [shape(kept)],
        compiler_params=params(),
        cost_estimate=cost(4 * count * depth * width, 2 * count * depth),
    )(rows, wk, wv, keys_0, values_0, pattern)


def query_kernel(*refs):
    rows, (wq_hbm, w_hbm), outs, (wq, sems) = refs[:4], refs[4:6], refs[6:9], refs[9:]
    copies = start_copies(wq_hbm, wq, sems, 0)
    more = start_copies(w_hbm, outs[2], sems, STREAMS)
    for copy in copies:
        copy.wait()
    for pair, out in ((rows[2:], outs[1]), (rows[:2], outs[0])):
        both = jnp.concatenate([ref[...] for ref in pair], axis=0)
        for part in halves_of(wq.shape[1]):
            out[:, part] = dot(both, wq[:, part]).astype(BF16)
    for copy in more:
        copy.wait()


def query(rows, w_query, w_out):
    count, depth = rows[0].shape
    width = w_query.shape[1]
    return pl.pallas_call(
        query_kernel,
        in_specs=[IN_VMEM] * 4 + [IN_HBM] * 2,
        out_specs=[IN_VMEM] * 3,
        out_shape=[shape((2 * count, width))] * 2 + [pltpu.VMEM(w_out.shape, BF16)],
        scratch_shapes=[
            pltpu.VMEM(w_query.shape, BF16),
            pltpu.SemaphoreType.DMA((2 * STREAMS,)),
        ],
        compiler_params=params(),
        cost_estimate=cost(8 * count * depth * width, 4 * depth * width),
    )(*rows, keep_in_hbm(w_query), keep_in_hbm(w_out))


def again_kernel(source, out):
    out[...] = source[...]


def again(kept):
    return pl.pallas_call(
        again_kernel,
        in_specs=[IN_VMEM],
        out_specs=IN_VMEM,
        out_shape=shape(kept.shape),
        compiler_params=params(),
        cost_estimate=cost(0, 4 * kept.size),
    )(kept)


def across_kernel(rows, wk, wv, keys, values):
    for part in halves_of(wk.shape[1]):
        keys[:, part] = dot(rows[...], wk[:, part]).astype(BF16)
        values[:, part] = dot(rows[...], wv[:, part]).astype(BF16)


def keys_and_values(rows, wk, wv):
    count, depth = rows.shape
    width = wk.shape[1]
    return pl.pallas_call(
        across_kernel,
        in_specs=[IN_VMEM] * 3,
        out_specs=[IN_VMEM] * 2,
        out_shape=[shape((count, width))] * 2,
        compiler_params=params(),
        cost_estimate=cost(4 * count * depth * width, 2 * count * depth),
    )(rows, wk, wv)


def slide_of(place, slides, block):
    end, total = jnp.int32(0), jnp.zeros_like(block)
    for index in range(slides):
        end = end + place[index]
        total = total + (block >= end).astype(jnp.int32)
    return total


def mask_kernel(slides, subs, spans, few, place, asking, asked):
    span, sub = place[slides], place[slides + 1]
    slide = [slide_of(place, slides, span * subs + (sub ^ r)) for r in range(subs)]
    lane = lax.broadcasted_iota(jnp.int32, (BLOCK, HEAD_SIZE), 1)
    for r in range(subs):
        rows = slice(r * BLOCK, (r + 1) * BLOCK)
        apart = (lane <= slides) & (lane != slide[r])
        asking[rows, :] = jnp.where(apart, HIDDEN, 0.0).astype(BF16)
        asked[rows, :] = jnp.where(lane == slide[r], 1.0, 0.0).astype(BF16)
    count = min(spans, GROUP) * FAR_ROWS
    row = lax.broadcasted_iota(jnp.int32, (count, HEAD_SIZE), 0)
    lane = lax.broadcasted_iota(jnp.int32, (count, HEAD_SIZE), 1)
    upper = (row // DILATED_KEPT) % BLOCKS_HALF
    for half in range(subs // BLOCKS_HALF):
        place_0, place_1 = sub ^ (half * BLOCKS_HALF), sub ^ (half * BLOCKS_HALF + 1)
        for group in range(spans * FAR_ROWS // count):
            far = row // FAR_ROWS
            if few:
                order = [bit | y for y in (0, Y_BIT) for bit in (0, *Z_BITS)]
                place_of = jnp.zeros_like(far)
                for index, bits in enumerate(order):
                    place_of = jnp.where(far == index, bits, place_of)
                far = place_of ^ span
            else:
                far = far + group * GROUP
            theirs = slide_of(place, slides, far * subs + jnp.where(upper == 0, place_0, place_1))
            marked = (lane == theirs) | ((lane == slides) & (far == span))
            start = subs * BLOCK + (half * spans * FAR_ROWS + group * count)
            asked[start : start + count, :] = jnp.where(marked, 1.0, 0.0).astype(BF16)


def make_masks(place, slides, subs, spans, few):
    keys = subs * BLOCK + subs // BLOCKS_HALF * spans * FAR_ROWS
    return pl.pallas_call(
        functools.partial(mask_kernel, slides, subs, spans, few),
        in_specs=[IN_SMEM],
        out_specs=[IN_VMEM] * 2,
        out_shape=[shape((subs * BLOCK, HEAD_SIZE)), shape((keys, HEAD_SIZE))],
        compiler_params=params(),
        cost_estimate=cost(64 * keys * HEAD_SIZE, 2 * keys * HEAD_SIZE),
    )(place)


def scores_of(keys, queries):
    return dot_t(keys, queries)


def gather(values, weight):
    return lax.dot_general(
        values, weight.astype(BF16), (((0,), (0,)), ((), ())), preferred_element_type=F32
    )


def begin(queries, keys, values):
    scores = [scores_of(k, q) for k, q in zip(keys, queries)]
    peak = [jnp.max(each, axis=0, keepdims=True) for each in scores]
    weight = [jnp.exp2((each - top) * SCALE) for each, top in zip(scores, peak)]
    total = [jnp.sum(each, axis=0, keepdims=True) for each in weight]
    return peak, total, [gather(v, each) for v, each in zip(values, weight)]


def update(queries, keys, values, state):
    scores = [scores_of(k, q) for k, q in zip(keys, queries)]
    higher = [
        jnp.maximum(top, jnp.max(each, axis=0, keepdims=True))
        for top, each in zip(state[0], scores)
    ]
    shrink = [jnp.exp2((top - new) * SCALE) for top, new in zip(state[0], higher)]
    weight = [jnp.exp2((each - new) * SCALE) for each, new in zip(scores, higher)]
    total = [
        old * less + jnp.sum(each, axis=0, keepdims=True)
        for old, less, each in zip(state[1], shrink, weight)
    ]
    added = [gather(v, each) for v, each in zip(values, weight)]
    return higher, total, [old * less + new for old, less, new in zip(state[2], shrink, added)]


def attend_kernel(first_row, near, halves, few, finish, asking, asked_of, *refs):
    refs = list(refs)
    queries = refs.pop(0)
    if near:
        keys, values = refs[0:4], refs[4:8]
        del refs[:8]
    else:
        gathered_in, stats_in = refs[0:2]
        del refs[:2]
    far = []
    for half, size in halves:
        far.append((half, refs[:size]))
        del refs[:size]
    rows = queries.shape[0]
    span = asking.shape[0]
    half_count = (asked_of.shape[0] - span) // BLOCKS_HALF

    heads = queries.shape[1] // HEAD_SIZE
    group = 1 if not few else min(2, heads) if near else heads

    def some_heads(turn, _):
        those = [turn * group + i for i in range(group)]
        columns = [
            pl.ds(pl.multiple_of(head * HEAD_SIZE, HEAD_SIZE), HEAD_SIZE)
            if group < heads
            else slice(head * HEAD_SIZE, (head + 1) * HEAD_SIZE)
            for head in those
        ]
        row_marks = asking[first_row : first_row + rows, :]
        asked = [jnp.concatenate([queries[:, each], row_marks], axis=1) for each in columns]

        def marked(parts, where):
            return jnp.concatenate([jnp.concatenate(parts, axis=0), asked_of[where, :]], axis=1)

        def ready(head, each):
            keyed, valued = [], []
            if near:
                keyed.append(marked([ref[:, each] for ref in keys], slice(0, span)))
                valued += [ref[:, each] for ref in values]
            if few:
                for half, parts in far:
                    start = span + half * half_count
                    pieces = [(ref, i) for ref in parts for i in range(ref.shape[0])]
                    where = slice(start, start + half_count)
                    keyed.append(marked([ref[i, 0, head] for ref, i in pieces], where))
                    valued += [ref[i, 1, head] for ref, i in pieces]
            return jnp.concatenate(keyed, axis=0), jnp.concatenate(valued, axis=0)

        if near:
            state = begin(asked, *zip(*map(ready, those, columns)))
        else:
            state = (
                [stats_in[head, 0:1, :] for head in those],
                [stats_in[head, 1:2, :] for head in those],
                [gathered_in[head] for head in those],
            )
            if few:
                state = update(asked, *zip(*map(ready, those, columns)), state)
        if not few:
            for half, (part,) in far:
                start = span + half * half_count

                def step(number, state, start=start, part=part):
                    base = number * GROUP
                    width = GROUP * FAR_ROWS
                    where = pl.ds(pl.multiple_of(start + number * width, width), width)
                    found = [
                        [
                            marked([part[base + i, 0, head] for i in range(GROUP)], where)
                            for head in those
                        ],
                        [
                            jnp.concatenate([part[base + i, 1, head] for i in range(GROUP)], axis=0)
                            for head in those
                        ],
                    ]
                    return update(asked, *found, state)

                state = lax.fori_loop(0, part.shape[0] // GROUP, step, state)
        for head, each, peak, total, gathered in zip(those, columns, *state):
            if finish:
                keep, send = refs
                context = (gathered / total).T.astype(BF16)
                keep[:, each] = context[:BLOCK]
                send[:, each] = context[BLOCK:]
            else:
                gathered_out, stats_out = refs
                gathered_out[head] = gathered
                stats_out[head, 0:1, :] = peak
                stats_out[head, 1:2, :] = total
        return 0

    if group == heads:
        some_heads(0, 0)
    else:
        lax.fori_loop(0, heads // group, some_heads, 0)


def attend(masks, few, first_row, queries, halves, near=None, begun=None, finish=True):
    rows, width = queries.shape
    heads = width // HEAD_SIZE
    operands = [*masks, queries]
    operands += [*near[0], *near[1]] if near else list(begun)
    columns = masks[0].shape[0] if near else 0
    for _, parts in halves:
        operands += parts
    far_bytes = sum(2 * part.size for _, parts in halves for part in parts)
    columns += far_bytes // (4 * width)
    if finish:
        out_shape = [shape((BLOCK, width))] * 2
    else:
        out_shape = [shape((heads, HEAD_SIZE, rows), F32), shape((heads, 8, rows), F32)]
    return pl.pallas_call(
        functools.partial(
            attend_kernel,
            first_row,
            near is not None,
            [(half, len(parts)) for half, parts in halves],
            few,
            finish,
        ),
        in_specs=[IN_VMEM] * len(operands),
        out_specs=[IN_VMEM] * 2,
        out_shape=out_shape,
        compiler_params=params(far_bytes),
        cost_estimate=cost(
            4 * rows * columns * width, 4 * rows * width, heads * rows * columns
        ),
    )(*operands)


def mix_kernel(rows_0, rows_1, weight_0, weight_1, out):
    tile = min(512, out.shape[1])
    for index in range(out.shape[1] // tile):
        part = slice(index * tile, (index + 1) * tile)
        total = dot(rows_0[...], weight_0[:, part]) + dot(rows_1[...], weight_1[:, part])
        out[:, part] = total.astype(out.dtype)


def mix(rows_0, rows_1, weight_0, weight_1, dtype):
    rows, depth = rows_0.shape
    width = weight_0.shape[1]
    return pl.pallas_call(
        mix_kernel,
        in_specs=[IN_VMEM] * 4,
        out_specs=IN_VMEM,
        out_shape=shape((rows, width), dtype),
        compiler_params=params(),
        cost_estimate=cost(4 * rows * depth * width, 4 * rows * width),
    )(rows_0, rows_1, weight_0, weight_1)


def shards(seqs, subs, normed, w_query, w_key, w_value, w_out, pattern, slide_lengths):
    slides = slide_lengths.shape[0]
    axes = [lax.axis_index(name).astype(jnp.int32)[None] for name in ("seq", "sub")]
    few = seqs == GROUP

    def swap(array, bit, axis="sub"):
        count = subs if axis == "sub" else seqs
        return lax.ppermute(array, axis, [(i, i ^ bit) for i in range(count)])

    def after(array, *others):
        return lax.optimization_barrier((array, *others))[0]

    def first_round(kept):
        return [swap(kept, bit, "seq") for bit in Z_BITS]

    def second_round(pieces):
        column = jnp.stack(pieces)
        return [column, swap(column, Y_BIT, "seq")]

    across = swap(normed, 2)
    beside = swap(normed, 1)
    mine, wk, wv, keys_0, values_0 = first(normed, w_key, w_value)
    keys_1, values_1, kept_a = second(beside, wk, wv, keys_0, values_0, pattern)
    place = jnp.concatenate([after(slide_lengths, kept_a), *axes])
    masks = list(make_masks(place, slides, subs, seqs, few))
    wo_beside = swap(w_out, 1)
    if few:
        along_z = first_round(kept_a)
        *along_z, masks[0] = lax.optimization_barrier((*along_z, masks[0]))
        half_a = 0, second_round([kept_a, *along_z])
        across = after(across, masks[0], wo_beside)
    else:
        half_a = 0, [lax.all_gather(kept_a, "seq", axis=0)]
    wo_beside = pltpu.with_memory_space_constraint(wo_beside, pltpu.VMEM)
    beyond = swap(across, 1)
    if few:
        beyond = after(beyond, half_a[1][0])
    keys_2, values_2 = keys_and_values(across, wk, wv)
    keys_3, values_3, kept_b = second(after(beyond, keys_2), wk, wv, keys_2, values_2, pattern)
    sent_later = again(kept_b)
    query_a, query_b, wo = query([after(mine, sent_later), beside, across, beyond], w_query, w_out)
    near = [keys_0, keys_1, keys_2, keys_3], [values_0, values_1, values_2, values_3]
    call = functools.partial(attend, masks, few)
    if few:
        along_z = first_round(kept_b)
        along_y = swap(sent_later, Y_BIT, "seq")
        *along_z, along_y, query_b, half_a[1][1] = lax.optimization_barrier(
            (*along_z, along_y, query_b, half_a[1][1])
        )
        column, other = second_round(along_z)
        half_b = 1, [kept_b[None], column, along_y[None], other]
        asked = after(query_b, column)
    else:
        half_b = 1, [lax.all_gather(kept_b, "seq", axis=0)]
        asked = query_b
    begun = call(2 * BLOCK, asked, [half_a], near=near, finish=False)
    keep_b, send_b = call(2 * BLOCK, query_b, [half_b], begun=begun)
    other_b = swap(send_b, 1)
    leaving = mix(keep_b, other_b, wo, wo_beside, BF16)
    arriving = swap(leaving, 2)
    query_a = after(query_a, leaving)
    keep_a, send_a = call(0, query_a, [half_a, half_b], near=near)
    other_a = swap(send_a, 1)
    own = mix(keep_a, other_a, wo, wo_beside, F32)
    return (own + arriving.astype(F32)).astype(BF16)


def solution(mesh):
    placed = (
        P(("seq", "sub"), None),
        P(None, "sub"),
        P(None, "sub"),
        P(None, "sub"),
        P("sub", None),
        P("sub", None),
        P(),
    )
    return jax.shard_map(
        functools.partial(shards, mesh.shape["seq"], mesh.shape["sub"]),
        mesh=mesh,
        in_specs=placed,
        out_specs=P(("seq", "sub"), None),
        check_vma=False,
    )
```

```python
import functools
import math

import jax
import jax.numpy as jnp
from jax import lax
from jax.experimental import pallas as pl
from jax.experimental.pallas import tpu as pltpu
from jax.sharding import PartitionSpec as P

HEAD_SIZE = 128
BLOCK = 128
DILATED_KEPT = 16
BLOCKS_HALF = 2
FAR_ROWS = BLOCKS_HALF * DILATED_KEPT
GROUP = 8
STREAMS = 8
PARTS = 4
HIDDEN = -1e30
SCALE = math.log2(math.e) / math.sqrt(HEAD_SIZE)
BF16 = jnp.bfloat16
F32 = jnp.float32
IN_VMEM = pl.BlockSpec(memory_space=pltpu.VMEM)
IN_HBM = pl.BlockSpec(memory_space=pltpu.HBM)
IN_SMEM = pl.BlockSpec(memory_space=pltpu.SMEM)
Y_BIT = 1
Z_BITS = (4, 6, 2)


def dot(a, b):
    return jnp.dot(a, b, preferred_element_type=F32)


def dot_t(a, b):
    return lax.dot_general(a, b, (((1,), (1,)), ((), ())), preferred_element_type=F32)


def params(extra=0):
    return pltpu.CompilerParams(vmem_limit_bytes=16 * 2**20 + extra)


def cost(flops, bytes_accessed, transcendentals=0):
    return pl.CostEstimate(
        flops=flops // 100,
        bytes_accessed=bytes_accessed // 100,
        transcendentals=transcendentals // 100,
    )


def shape(dims, dtype=BF16):
    return jax.ShapeDtypeStruct(tuple(dims), dtype)


def keep_in_hbm(array):
    return pltpu.with_memory_space_constraint(array, pltpu.HBM)


def start_copies(source, target, sems, base):
    rows = source.shape[0] // STREAMS
    copies = []
    for index in range(STREAMS):
        where = slice(index * rows, (index + 1) * rows)
        copy = pltpu.make_async_copy(source.at[where, :], target.at[where, :], sems.at[base + index])
        copy.start()
        copies.append(copy)
    return copies


def halves_of(width):
    tile = min(256, width)
    return [slice(i * tile, (i + 1) * tile) for i in range(width // tile)]


def pick_dilated(pattern, blocks, kept):
    positions = lax.broadcasted_iota(jnp.int32, (BLOCK, BLOCK), 0)
    for head in range(kept.shape[1]):
        row = pattern[head : head + 1, :]
        chosen = (positions == row).astype(F32).T[:DILATED_KEPT].astype(BF16)
        for index, block in enumerate(blocks):
            picked = dot(chosen, jnp.concatenate(block(head), axis=1)).astype(BF16)
            spot = slice(index * DILATED_KEPT, (index + 1) * DILATED_KEPT)
            kept[0, head, spot, :] = picked[:, :HEAD_SIZE]
            kept[1, head, spot, :] = picked[:, HEAD_SIZE:]


def head_of(ref, head, rows=slice(None)):
    return ref[rows, head * HEAD_SIZE : (head + 1) * HEAD_SIZE]


def first_kernel(rows_hbm, wk_hbm, wv_hbm, rows, wk, wv, keys, values, sems):
    whole = pltpu.make_async_copy(rows_hbm, rows, sems.at[0])
    whole.start()
    key_copies = start_copies(wk_hbm, wk, sems, 1)
    value_copies = start_copies(wv_hbm, wv, sems, 1 + STREAMS)
    whole.wait()
    for copies, weight, out in ((key_copies, wk, keys), (value_copies, wv, values)):
        for copy in copies:
            copy.wait()
        for part in halves_of(wk.shape[1]):
            out[:, part] = dot(rows[...], weight[:, part]).astype(BF16)


def first(rows, w_key, w_value):
    count, depth = rows.shape
    width = w_key.shape[1]
    return pl.pallas_call(
        first_kernel,
        in_specs=[IN_HBM] * 3,
        out_specs=[IN_VMEM] * 5,
        out_shape=[
            pltpu.VMEM(rows.shape, BF16),
            pltpu.VMEM(w_key.shape, BF16),
            pltpu.VMEM(w_value.shape, BF16),
            shape((count, width)),
            shape((count, width)),
        ],
        scratch_shapes=[pltpu.SemaphoreType.DMA((1 + 2 * STREAMS,))],
        compiler_params=params(),
        cost_estimate=cost(4 * count * depth * width, 4 * depth * width),
    )(keep_in_hbm(rows), keep_in_hbm(w_key), keep_in_hbm(w_value))


def second_kernel(rows, wk, wv, keys_0, values_0, pattern, keys, values, kept):
    for part in halves_of(wk.shape[1]):
        keys[:, part] = dot(rows[...], wk[:, part]).astype(BF16)
        values[:, part] = dot(rows[...], wv[:, part]).astype(BF16)
    blocks = [
        lambda head: (head_of(keys_0, head), head_of(values_0, head)),
        lambda head: (head_of(keys, head), head_of(values, head)),
    ]
    pick_dilated(pattern, blocks, kept)


def second(rows, wk, wv, keys_0, values_0, pattern):
    count, depth = rows.shape
    width = wk.shape[1]
    kept = (2, width // HEAD_SIZE, FAR_ROWS, HEAD_SIZE)
    return pl.pallas_call(
        second_kernel,
        in_specs=[IN_VMEM] * 6,
        out_specs=[IN_VMEM] * 3,
        out_shape=[shape((count, width))] * 2 + [shape(kept)],
        compiler_params=params(),
        cost_estimate=cost(4 * count * depth * width, 2 * count * depth),
    )(rows, wk, wv, keys_0, values_0, pattern)


def query_kernel(*refs):
    rows, (wq_hbm, w_hbm), outs, (wq, sems) = refs[:4], refs[4:6], refs[6:9], refs[9:]
    copies = start_copies(wq_hbm, wq, sems, 0)
    more = start_copies(w_hbm, outs[2], sems, STREAMS)
    for copy in copies:
        copy.wait()
    for pair, out in ((rows[2:], outs[1]), (rows[:2], outs[0])):
        both = jnp.concatenate([ref[...] for ref in pair], axis=0)
        for part in halves_of(wq.shape[1]):
            out[:, part] = dot(both, wq[:, part]).astype(BF16)
    for copy in more:
        copy.wait()


def query(rows, w_query, w_out):
    count, depth = rows[0].shape
    width = w_query.shape[1]
    return pl.pallas_call(
        query_kernel,
        in_specs=[IN_VMEM] * 4 + [IN_HBM] * 2,
        out_specs=[IN_VMEM] * 3,
        out_shape=[shape((2 * count, width))] * 2 + [pltpu.VMEM(w_out.shape, BF16)],
        scratch_shapes=[
            pltpu.VMEM(w_query.shape, BF16),
            pltpu.SemaphoreType.DMA((2 * STREAMS,)),
        ],
        compiler_params=params(),
        cost_estimate=cost(8 * count * depth * width, 4 * depth * width),
    )(*rows, keep_in_hbm(w_query), keep_in_hbm(w_out))


def again_kernel(source, out):
    out[...] = source[...]


def again(kept):
    return pl.pallas_call(
        again_kernel,
        in_specs=[IN_VMEM],
        out_specs=IN_VMEM,
        out_shape=shape(kept.shape),
        compiler_params=params(),
        cost_estimate=cost(0, 4 * kept.size),
    )(kept)


def across_kernel(rows, wk, wv, keys, values):
    for part in halves_of(wk.shape[1]):
        keys[:, part] = dot(rows[...], wk[:, part]).astype(BF16)
        values[:, part] = dot(rows[...], wv[:, part]).astype(BF16)


def keys_and_values(rows, wk, wv):
    count, depth = rows.shape
    width = wk.shape[1]
    return pl.pallas_call(
        across_kernel,
        in_specs=[IN_VMEM] * 3,
        out_specs=[IN_VMEM] * 2,
        out_shape=[shape((count, width))] * 2,
        compiler_params=params(),
        cost_estimate=cost(4 * count * depth * width, 2 * count * depth),
    )(rows, wk, wv)


def slide_of(place, slides, block):
    end, total = jnp.int32(0), jnp.zeros_like(block)
    for index in range(slides):
        end = end + place[index]
        total = total + (block >= end).astype(jnp.int32)
    return total


def mask_kernel(slides, subs, spans, few, place, asking, asked):
    span, sub = place[slides], place[slides + 1]
    slide = [slide_of(place, slides, span * subs + (sub ^ r)) for r in range(subs)]
    lane = lax.broadcasted_iota(jnp.int32, (BLOCK, HEAD_SIZE), 1)
    for r in range(subs):
        rows = slice(r * BLOCK, (r + 1) * BLOCK)
        apart = (lane <= slides) & (lane != slide[r])
        asking[rows, :] = jnp.where(apart, HIDDEN, 0.0).astype(BF16)
        asked[rows, :] = jnp.where(lane == slide[r], 1.0, 0.0).astype(BF16)
    count = min(spans, GROUP) * FAR_ROWS
    row = lax.broadcasted_iota(jnp.int32, (count, HEAD_SIZE), 0)
    lane = lax.broadcasted_iota(jnp.int32, (count, HEAD_SIZE), 1)
    upper = (row // DILATED_KEPT) % BLOCKS_HALF
    for half in range(subs // BLOCKS_HALF):
        place_0, place_1 = sub ^ (half * BLOCKS_HALF), sub ^ (half * BLOCKS_HALF + 1)
        for group in range(spans * FAR_ROWS // count):
            far = row // FAR_ROWS
            if few:
                order = [bit | y for y in (0, Y_BIT) for bit in (0, *Z_BITS)]
                place_of = jnp.zeros_like(far)
                for index, bits in enumerate(order):
                    place_of = jnp.where(far == index, bits, place_of)
                far = place_of ^ span
            else:
                far = far + group * GROUP
            theirs = slide_of(place, slides, far * subs + jnp.where(upper == 0, place_0, place_1))
            marked = (lane == theirs) | ((lane == slides) & (far == span))
            start = subs * BLOCK + (half * spans * FAR_ROWS + group * count)
            asked[start : start + count, :] = jnp.where(marked, 1.0, 0.0).astype(BF16)


def make_masks(place, slides, subs, spans, few):
    keys = subs * BLOCK + subs // BLOCKS_HALF * spans * FAR_ROWS
    return pl.pallas_call(
        functools.partial(mask_kernel, slides, subs, spans, few),
        in_specs=[IN_SMEM],
        out_specs=[IN_VMEM] * 2,
        out_shape=[shape((subs * BLOCK, HEAD_SIZE)), shape((keys, HEAD_SIZE))],
        compiler_params=params(),
        cost_estimate=cost(64 * keys * HEAD_SIZE, 2 * keys * HEAD_SIZE),
    )(place)


def scores_of(keys, queries):
    return dot_t(keys, queries)


def gather(values, weight):
    return lax.dot_general(
        values, weight.astype(BF16), (((0,), (0,)), ((), ())), preferred_element_type=F32
    )


def begin(queries, keys, values):
    scores = [scores_of(k, q) for k, q in zip(keys, queries)]
    peak = [jnp.max(each, axis=0, keepdims=True) for each in scores]
    weight = [jnp.exp2((each - top) * SCALE) for each, top in zip(scores, peak)]
    total = [jnp.sum(each, axis=0, keepdims=True) for each in weight]
    return peak, total, [gather(v, each) for v, each in zip(values, weight)]


def update(queries, keys, values, state):
    scores = [scores_of(k, q) for k, q in zip(keys, queries)]
    higher = [
        jnp.maximum(top, jnp.max(each, axis=0, keepdims=True))
        for top, each in zip(state[0], scores)
    ]
    shrink = [jnp.exp2((top - new) * SCALE) for top, new in zip(state[0], higher)]
    weight = [jnp.exp2((each - new) * SCALE) for each, new in zip(scores, higher)]
    total = [
        old * less + jnp.sum(each, axis=0, keepdims=True)
        for old, less, each in zip(state[1], shrink, weight)
    ]
    added = [gather(v, each) for v, each in zip(values, weight)]
    return higher, total, [old * less + new for old, less, new in zip(state[2], shrink, added)]


def attend_kernel(first_row, near, halves, few, finish, asking, asked_of, *refs):
    refs = list(refs)
    queries = refs.pop(0)
    if near:
        keys, values = refs[0:4], refs[4:8]
        del refs[:8]
    else:
        gathered_in, stats_in = refs[0:2]
        del refs[:2]
    far = []
    for half, size in halves:
        far.append((half, refs[:size]))
        del refs[:size]
    rows = queries.shape[0]
    span = asking.shape[0]
    half_count = (asked_of.shape[0] - span) // BLOCKS_HALF

    heads = queries.shape[1] // HEAD_SIZE
    group = 1 if not few else min(2, heads) if near else heads

    def some_heads(turn, _):
        those = [turn * group + i for i in range(group)]
        columns = [
            pl.ds(pl.multiple_of(head * HEAD_SIZE, HEAD_SIZE), HEAD_SIZE)
            if group < heads
            else slice(head * HEAD_SIZE, (head + 1) * HEAD_SIZE)
            for head in those
        ]
        row_marks = asking[first_row : first_row + rows, :]
        asked = [jnp.concatenate([queries[:, each], row_marks], axis=1) for each in columns]

        def marked(parts, where):
            return jnp.concatenate([jnp.concatenate(parts, axis=0), asked_of[where, :]], axis=1)

        def ready(head, each):
            keyed, valued = [], []
            if near:
                keyed.append(marked([ref[:, each] for ref in keys], slice(0, span)))
                valued += [ref[:, each] for ref in values]
            if few:
                for half, parts in far:
                    start = span + half * half_count
                    pieces = [(ref, i) for ref in parts for i in range(ref.shape[0])]
                    where = slice(start, start + half_count)
                    keyed.append(marked([ref[i, 0, head] for ref, i in pieces], where))
                    valued += [ref[i, 1, head] for ref, i in pieces]
            return jnp.concatenate(keyed, axis=0), jnp.concatenate(valued, axis=0)

        if near:
            state = begin(asked, *zip(*map(ready, those, columns)))
        else:
            state = (
                [stats_in[head, 0:1, :] for head in those],
                [stats_in[head, 1:2, :] for head in those],
                [gathered_in[head] for head in those],
            )
            if few:
                state = update(asked, *zip(*map(ready, those, columns)), state)
        if not few:
            for half, (part,) in far:
                start = span + half * half_count

                def step(number, state, start=start, part=part):
                    base = number * GROUP
                    width = GROUP * FAR_ROWS
                    where = pl.ds(pl.multiple_of(start + number * width, width), width)
                    found = [
                        [
                            marked([part[base + i, 0, head] for i in range(GROUP)], where)
                            for head in those
                        ],
                        [
                            jnp.concatenate([part[base + i, 1, head] for i in range(GROUP)], axis=0)
                            for head in those
                        ],
                    ]
                    return update(asked, *found, state)

                state = lax.fori_loop(0, part.shape[0] // GROUP, step, state)
        for head, each, peak, total, gathered in zip(those, columns, *state):
            if finish:
                keep, send = refs
                context = (gathered / total).T.astype(BF16)
                keep[:, each] = context[:BLOCK]
                send[:, each] = context[BLOCK:]
            else:
                gathered_out, stats_out = refs
                gathered_out[head] = gathered
                stats_out[head, 0:1, :] = peak
                stats_out[head, 1:2, :] = total
        return 0

    if group == heads:
        some_heads(0, 0)
    else:
        lax.fori_loop(0, heads // group, some_heads, 0)


def attend(masks, few, first_row, queries, halves, near=None, begun=None, finish=True):
    rows, width = queries.shape
    heads = width // HEAD_SIZE
    operands = [*masks, queries]
    operands += [*near[0], *near[1]] if near else list(begun)
    columns = masks[0].shape[0] if near else 0
    for _, parts in halves:
        operands += parts
    far_bytes = sum(2 * part.size for _, parts in halves for part in parts)
    columns += far_bytes // (4 * width)
    if finish:
        out_shape = [shape((BLOCK, width))] * 2
    else:
        out_shape = [shape((heads, HEAD_SIZE, rows), F32), shape((heads, 8, rows), F32)]
    return pl.pallas_call(
        functools.partial(
            attend_kernel,
            first_row,
            near is not None,
            [(half, len(parts)) for half, parts in halves],
            few,
            finish,
        ),
        in_specs=[IN_VMEM] * len(operands),
        out_specs=[IN_VMEM] * 2,
        out_shape=out_shape,
        compiler_params=params(far_bytes),
        cost_estimate=cost(
            4 * rows * columns * width, 4 * rows * width, heads * rows * columns
        ),
    )(*operands)


def mix_kernel(more, rows, weight, *refs):
    out = refs[-1]
    tile = min(512, out.shape[1])
    for index in range(out.shape[1] // tile):
        part = slice(index * tile, (index + 1) * tile)
        total = dot(rows[...], weight[:, part])
        if more:
            total = total + refs[0][:, part]
        out[:, part] = total.astype(out.dtype)


def mix(rows, weight, dtype, begun=None):
    count, depth = rows.shape
    width = weight.shape[1]
    operands = [rows, weight] + ([begun] if begun is not None else [])
    return pl.pallas_call(
        functools.partial(mix_kernel, begun is not None),
        in_specs=[IN_VMEM] * len(operands),
        out_specs=IN_VMEM,
        out_shape=shape((count, width), dtype),
        compiler_params=params(),
        cost_estimate=cost(2 * count * depth * width, 4 * count * width),
    )(*operands)


def add_kernel(own, arriving, out, held, sems):
    rows = held.shape[0] // PARTS
    copies = []
    for index in range(PARTS):
        where = slice(index * rows, (index + 1) * rows)
        held[where, :] = (own[where, :] + arriving[where, :].astype(F32)).astype(BF16)
        copy = pltpu.make_async_copy(held.at[where, :], out.at[where, :], sems.at[index])
        copy.start()
        copies.append(copy)
    for copy in copies:
        copy.wait()


def add(own, arriving):
    return pl.pallas_call(
        add_kernel,
        in_specs=[IN_VMEM] * 2,
        out_specs=IN_HBM,
        out_shape=shape(arriving.shape),
        scratch_shapes=[pltpu.VMEM(arriving.shape, BF16), pltpu.SemaphoreType.DMA((PARTS,))],
        compiler_params=params(),
        cost_estimate=cost(own.size, 8 * own.size),
    )(own, arriving)


def shards(seqs, subs, normed, w_query, w_key, w_value, w_out, pattern, slide_lengths):
    slides = slide_lengths.shape[0]
    axes = [lax.axis_index(name).astype(jnp.int32)[None] for name in ("seq", "sub")]
    few = seqs == GROUP

    def swap(array, bit, axis="sub"):
        count = subs if axis == "sub" else seqs
        return lax.ppermute(array, axis, [(i, i ^ bit) for i in range(count)])

    def after(array, *others):
        return lax.optimization_barrier((array, *others))[0]

    def first_round(kept):
        return [swap(kept, bit, "seq") for bit in Z_BITS]

    def second_round(pieces):
        column = jnp.stack(pieces)
        return [column, swap(column, Y_BIT, "seq")]

    across = swap(normed, 2)
    beside = swap(normed, 1)
    mine, wk, wv, keys_0, values_0 = first(normed, w_key, w_value)
    keys_1, values_1, kept_a = second(beside, wk, wv, keys_0, values_0, pattern)
    place = jnp.concatenate([after(slide_lengths, kept_a), *axes])
    masks = list(make_masks(place, slides, subs, seqs, few))
    wo_beside = swap(w_out, 1)
    if few:
        along_z = first_round(kept_a)
        *along_z, masks[0] = lax.optimization_barrier((*along_z, masks[0]))
        half_a = 0, second_round([kept_a, *along_z])
        across = after(across, masks[0], wo_beside)
    else:
        half_a = 0, [lax.all_gather(kept_a, "seq", axis=0)]
    wo_beside = pltpu.with_memory_space_constraint(wo_beside, pltpu.VMEM)
    beyond = swap(across, 1)
    if few:
        beyond = after(beyond, half_a[1][0])
    keys_2, values_2 = keys_and_values(across, wk, wv)
    keys_3, values_3, kept_b = second(after(beyond, keys_2), wk, wv, keys_2, values_2, pattern)
    near = [keys_0, keys_1, keys_2, keys_3], [values_0, values_1, values_2, values_3]
    call = functools.partial(attend, masks, few)
    if few:
        along_z = first_round(kept_b)
        along_y = swap(again(kept_b), Y_BIT, "seq")
        *along_z, along_y, half_a[1][1] = lax.optimization_barrier(
            (*along_z, along_y, half_a[1][1])
        )
        column, other = second_round(along_z)
        half_b = 1, [kept_b[None], column, along_y[None], other]
        mine = after(mine, column)
    else:
        half_b = 1, [lax.all_gather(kept_b, "seq", axis=0)]
    query_a, query_b, wo = query([mine, beside, across, beyond], w_query, w_out)
    begun = call(2 * BLOCK, query_b, [half_a], near=near, finish=False)
    keep_b, send_b = call(2 * BLOCK, query_b, [half_b], begun=begun)
    other_b = swap(send_b, 1)
    leaving = mix(other_b, wo_beside, BF16, mix(keep_b, wo, F32))
    arriving = swap(leaving, 2)
    query_a = after(query_a, leaving)
    keep_a, send_a = call(0, query_a, [half_a, half_b], near=near)
    other_a = swap(send_a, 1)
    own = mix(other_a, wo_beside, F32, mix(keep_a, wo, F32))
    return add(own, arriving)


def solution(mesh):
    placed = (
        P(("seq", "sub"), None),
        P(None, "sub"),
        P(None, "sub"),
        P(None, "sub"),
        P("sub", None),
        P("sub", None),
        P(),
    )
    return jax.shard_map(
        functools.partial(shards, mesh.shape["seq"], mesh.shape["sub"]),
        mesh=mesh,
        in_specs=placed,
        out_specs=P(("seq", "sub"), None),
        check_vma=False,
    )
```

```python
import functools
import math

import jax
import jax.numpy as jnp
from jax import lax
from jax.experimental import pallas as pl
from jax.experimental.pallas import tpu as pltpu
from jax.sharding import PartitionSpec as P

HEAD_SIZE = 128
BLOCK = 128
DILATED_KEPT = 16
BLOCKS_HALF = 2
FAR_ROWS = BLOCKS_HALF * DILATED_KEPT
GROUP = 8
STREAMS = 8
PARTS = 4
HIDDEN = -1e30
SCALE = math.log2(math.e) / math.sqrt(HEAD_SIZE)
BF16 = jnp.bfloat16
F32 = jnp.float32
IN_VMEM = pl.BlockSpec(memory_space=pltpu.VMEM)
IN_HBM = pl.BlockSpec(memory_space=pltpu.HBM)
IN_SMEM = pl.BlockSpec(memory_space=pltpu.SMEM)
Y_BIT = 1
Z_BITS = (4, 6, 2)


def dot(a, b):
    return jnp.dot(a, b, preferred_element_type=F32)


def dot_t(a, b):
    return lax.dot_general(a, b, (((1,), (1,)), ((), ())), preferred_element_type=F32)


def params(extra=0):
    return pltpu.CompilerParams(vmem_limit_bytes=16 * 2**20 + extra)


def cost(flops, bytes_accessed, transcendentals=0):
    return pl.CostEstimate(
        flops=flops // 100,
        bytes_accessed=bytes_accessed // 100,
        transcendentals=transcendentals // 100,
    )


def shape(dims, dtype=BF16):
    return jax.ShapeDtypeStruct(tuple(dims), dtype)


def keep_in_hbm(array):
    return pltpu.with_memory_space_constraint(array, pltpu.HBM)


def start_copies(source, target, sems, base):
    rows = source.shape[0] // STREAMS
    copies = []
    for index in range(STREAMS):
        where = slice(index * rows, (index + 1) * rows)
        copy = pltpu.make_async_copy(source.at[where, :], target.at[where, :], sems.at[base + index])
        copy.start()
        copies.append(copy)
    return copies


def halves_of(width):
    tile = min(256, width)
    return [slice(i * tile, (i + 1) * tile) for i in range(width // tile)]


def pick_dilated(pattern, blocks, kept):
    positions = lax.broadcasted_iota(jnp.int32, (BLOCK, BLOCK), 0)
    for head in range(kept.shape[1]):
        row = pattern[head : head + 1, :]
        chosen = (positions == row).astype(F32).T[:DILATED_KEPT].astype(BF16)
        for index, block in enumerate(blocks):
            picked = dot(chosen, jnp.concatenate(block(head), axis=1)).astype(BF16)
            spot = slice(index * DILATED_KEPT, (index + 1) * DILATED_KEPT)
            kept[0, head, spot, :] = picked[:, :HEAD_SIZE]
            kept[1, head, spot, :] = picked[:, HEAD_SIZE:]


def head_of(ref, head, rows=slice(None)):
    return ref[rows, head * HEAD_SIZE : (head + 1) * HEAD_SIZE]


def first_kernel(rows_hbm, wk_hbm, wv_hbm, rows, wk, wv, keys, values, sems):
    whole = pltpu.make_async_copy(rows_hbm, rows, sems.at[0])
    whole.start()
    key_copies = start_copies(wk_hbm, wk, sems, 1)
    value_copies = start_copies(wv_hbm, wv, sems, 1 + STREAMS)
    whole.wait()
    for copies, weight, out in ((key_copies, wk, keys), (value_copies, wv, values)):
        for copy in copies:
            copy.wait()
        for part in halves_of(wk.shape[1]):
            out[:, part] = dot(rows[...], weight[:, part]).astype(BF16)


def first(rows, w_key, w_value):
    count, depth = rows.shape
    width = w_key.shape[1]
    return pl.pallas_call(
        first_kernel,
        in_specs=[IN_HBM] * 3,
        out_specs=[IN_VMEM] * 5,
        out_shape=[
            pltpu.VMEM(rows.shape, BF16),
            pltpu.VMEM(w_key.shape, BF16),
            pltpu.VMEM(w_value.shape, BF16),
            shape((count, width)),
            shape((count, width)),
        ],
        scratch_shapes=[pltpu.SemaphoreType.DMA((1 + 2 * STREAMS,))],
        compiler_params=params(),
        cost_estimate=cost(4 * count * depth * width, 4 * depth * width),
    )(keep_in_hbm(rows), keep_in_hbm(w_key), keep_in_hbm(w_value))


def second_kernel(rows, wk, wv, keys_0, values_0, pattern, keys, values, kept):
    for part in halves_of(wk.shape[1]):
        keys[:, part] = dot(rows[...], wk[:, part]).astype(BF16)
        values[:, part] = dot(rows[...], wv[:, part]).astype(BF16)
    blocks = [
        lambda head: (head_of(keys_0, head), head_of(values_0, head)),
        lambda head: (head_of(keys, head), head_of(values, head)),
    ]
    pick_dilated(pattern, blocks, kept)


def second(rows, wk, wv, keys_0, values_0, pattern):
    count, depth = rows.shape
    width = wk.shape[1]
    kept = (2, width // HEAD_SIZE, FAR_ROWS, HEAD_SIZE)
    return pl.pallas_call(
        second_kernel,
        in_specs=[IN_VMEM] * 6,
        out_specs=[IN_VMEM] * 3,
        out_shape=[shape((count, width))] * 2 + [shape(kept)],
        compiler_params=params(),
        cost_estimate=cost(4 * count * depth * width, 2 * count * depth),
    )(rows, wk, wv, keys_0, values_0, pattern)


def query_kernel(*refs):
    rows, (wq_hbm, w_hbm), outs, (wq, sems) = refs[:4], refs[4:6], refs[6:9], refs[9:]
    copies = start_copies(wq_hbm, wq, sems, 0)
    more = start_copies(w_hbm, outs[2], sems, STREAMS)
    for copy in copies:
        copy.wait()
    for pair, out in ((rows[2:], outs[1]), (rows[:2], outs[0])):
        both = jnp.concatenate([ref[...] for ref in pair], axis=0)
        for part in halves_of(wq.shape[1]):
            out[:, part] = dot(both, wq[:, part]).astype(BF16)
    for copy in more:
        copy.wait()


def query(rows, w_query, w_out):
    count, depth = rows[0].shape
    width = w_query.shape[1]
    return pl.pallas_call(
        query_kernel,
        in_specs=[IN_VMEM] * 4 + [IN_HBM] * 2,
        out_specs=[IN_VMEM] * 3,
        out_shape=[shape((2 * count, width))] * 2 + [pltpu.VMEM(w_out.shape, BF16)],
        scratch_shapes=[
            pltpu.VMEM(w_query.shape, BF16),
            pltpu.SemaphoreType.DMA((2 * STREAMS,)),
        ],
        compiler_params=params(),
        cost_estimate=cost(8 * count * depth * width, 4 * depth * width),
    )(*rows, keep_in_hbm(w_query), keep_in_hbm(w_out))


def again_kernel(source, out):
    out[...] = source[...]


def again(kept):
    return pl.pallas_call(
        again_kernel,
        in_specs=[IN_VMEM],
        out_specs=IN_VMEM,
        out_shape=shape(kept.shape),
        compiler_params=params(),
        cost_estimate=cost(0, 4 * kept.size),
    )(kept)


def across_kernel(rows, wk, wv, keys, values):
    for part in halves_of(wk.shape[1]):
        keys[:, part] = dot(rows[...], wk[:, part]).astype(BF16)
        values[:, part] = dot(rows[...], wv[:, part]).astype(BF16)


def keys_and_values(rows, wk, wv):
    count, depth = rows.shape
    width = wk.shape[1]
    return pl.pallas_call(
        across_kernel,
        in_specs=[IN_VMEM] * 3,
        out_specs=[IN_VMEM] * 2,
        out_shape=[shape((count, width))] * 2,
        compiler_params=params(),
        cost_estimate=cost(4 * count * depth * width, 2 * count * depth),
    )(rows, wk, wv)


def slide_of(place, slides, block):
    end, total = jnp.int32(0), jnp.zeros_like(block)
    for index in range(slides):
        end = end + place[index]
        total = total + (block >= end).astype(jnp.int32)
    return total


def mask_kernel(slides, subs, spans, few, place, asking, asked):
    span, sub = place[slides], place[slides + 1]
    slide = [slide_of(place, slides, span * subs + (sub ^ r)) for r in range(subs)]
    lane = lax.broadcasted_iota(jnp.int32, (BLOCK, HEAD_SIZE), 1)
    for r in range(subs):
        rows = slice(r * BLOCK, (r + 1) * BLOCK)
        apart = (lane <= slides) & (lane != slide[r])
        asking[rows, :] = jnp.where(apart, HIDDEN, 0.0).astype(BF16)
        asked[rows, :] = jnp.where(lane == slide[r], 1.0, 0.0).astype(BF16)
    count = min(spans, GROUP) * FAR_ROWS
    row = lax.broadcasted_iota(jnp.int32, (count, HEAD_SIZE), 0)
    lane = lax.broadcasted_iota(jnp.int32, (count, HEAD_SIZE), 1)
    upper = (row // DILATED_KEPT) % BLOCKS_HALF
    for half in range(subs // BLOCKS_HALF):
        place_0, place_1 = sub ^ (half * BLOCKS_HALF), sub ^ (half * BLOCKS_HALF + 1)
        for group in range(spans * FAR_ROWS // count):
            far = row // FAR_ROWS
            if few:
                order = [bit | y for y in (0, Y_BIT) for bit in (0, *Z_BITS)]
                place_of = jnp.zeros_like(far)
                for index, bits in enumerate(order):
                    place_of = jnp.where(far == index, bits, place_of)
                far = place_of ^ span
            else:
                far = far + group * GROUP
            theirs = slide_of(place, slides, far * subs + jnp.where(upper == 0, place_0, place_1))
            marked = (lane == theirs) | ((lane == slides) & (far == span))
            start = subs * BLOCK + (half * spans * FAR_ROWS + group * count)
            asked[start : start + count, :] = jnp.where(marked, 1.0, 0.0).astype(BF16)


def make_masks(place, slides, subs, spans, few):
    keys = subs * BLOCK + subs // BLOCKS_HALF * spans * FAR_ROWS
    return pl.pallas_call(
        functools.partial(mask_kernel, slides, subs, spans, few),
        in_specs=[IN_SMEM],
        out_specs=[IN_VMEM] * 2,
        out_shape=[shape((subs * BLOCK, HEAD_SIZE)), shape((keys, HEAD_SIZE))],
        compiler_params=params(),
        cost_estimate=cost(64 * keys * HEAD_SIZE, 2 * keys * HEAD_SIZE),
    )(place)


def scores_of(keys, queries):
    return dot_t(keys, queries)


def gather(values, weight):
    return lax.dot_general(
        values, weight.astype(BF16), (((0,), (0,)), ((), ())), preferred_element_type=F32
    )


def begin(queries, keys, values):
    scores = [scores_of(k, q) for k, q in zip(keys, queries)]
    peak = [jnp.max(each, axis=0, keepdims=True) for each in scores]
    weight = [jnp.exp2((each - top) * SCALE) for each, top in zip(scores, peak)]
    total = [jnp.sum(each, axis=0, keepdims=True) for each in weight]
    return peak, total, [gather(v, each) for v, each in zip(values, weight)]


def update(queries, keys, values, state):
    scores = [scores_of(k, q) for k, q in zip(keys, queries)]
    higher = [
        jnp.maximum(top, jnp.max(each, axis=0, keepdims=True))
        for top, each in zip(state[0], scores)
    ]
    shrink = [jnp.exp2((top - new) * SCALE) for top, new in zip(state[0], higher)]
    weight = [jnp.exp2((each - new) * SCALE) for each, new in zip(scores, higher)]
    total = [
        old * less + jnp.sum(each, axis=0, keepdims=True)
        for old, less, each in zip(state[1], shrink, weight)
    ]
    added = [gather(v, each) for v, each in zip(values, weight)]
    return higher, total, [old * less + new for old, less, new in zip(state[2], shrink, added)]


def attend_kernel(first_row, near, halves, few, finish, asking, asked_of, *refs):
    refs = list(refs)
    queries = refs.pop(0)
    if near:
        keys, values = refs[0:4], refs[4:8]
        del refs[:8]
    else:
        gathered_in, stats_in = refs[0:2]
        del refs[:2]
    far = []
    for half, size in halves:
        far.append((half, refs[:size]))
        del refs[:size]
    rows = queries.shape[0]
    span = asking.shape[0]
    half_count = (asked_of.shape[0] - span) // BLOCKS_HALF

    heads = queries.shape[1] // HEAD_SIZE
    group = 1 if not few else min(2, heads) if near else heads

    def some_heads(turn, _):
        those = [turn * group + i for i in range(group)]
        columns = [
            pl.ds(pl.multiple_of(head * HEAD_SIZE, HEAD_SIZE), HEAD_SIZE)
            if group < heads
            else slice(head * HEAD_SIZE, (head + 1) * HEAD_SIZE)
            for head in those
        ]
        row_marks = asking[first_row : first_row + rows, :]
        asked = [jnp.concatenate([queries[:, each], row_marks], axis=1) for each in columns]

        def marked(parts, where):
            return jnp.concatenate([jnp.concatenate(parts, axis=0), asked_of[where, :]], axis=1)

        def ready(head, each):
            keyed, valued = [], []
            if near:
                keyed.append(marked([ref[:, each] for ref in keys], slice(0, span)))
                valued += [ref[:, each] for ref in values]
            if few:
                for half, parts in far:
                    start = span + half * half_count
                    pieces = [(ref, i) for ref in parts for i in range(ref.shape[0])]
                    where = slice(start, start + half_count)
                    keyed.append(marked([ref[i, 0, head] for ref, i in pieces], where))
                    valued += [ref[i, 1, head] for ref, i in pieces]
            return jnp.concatenate(keyed, axis=0), jnp.concatenate(valued, axis=0)

        if near:
            state = begin(asked, *zip(*map(ready, those, columns)))
        else:
            state = (
                [stats_in[head, 0:1, :] for head in those],
                [stats_in[head, 1:2, :] for head in those],
                [gathered_in[head] for head in those],
            )
            if few:
                state = update(asked, *zip(*map(ready, those, columns)), state)
        if not few:
            for half, (part,) in far:
                start = span + half * half_count

                def step(number, state, start=start, part=part):
                    base = number * GROUP
                    width = GROUP * FAR_ROWS
                    where = pl.ds(pl.multiple_of(start + number * width, width), width)
                    found = [
                        [
                            marked([part[base + i, 0, head] for i in range(GROUP)], where)
                            for head in those
                        ],
                        [
                            jnp.concatenate([part[base + i, 1, head] for i in range(GROUP)], axis=0)
                            for head in those
                        ],
                    ]
                    return update(asked, *found, state)

                state = lax.fori_loop(0, part.shape[0] // GROUP, step, state)
        for head, each, peak, total, gathered in zip(those, columns, *state):
            if finish:
                keep, send = refs
                context = (gathered / total).T.astype(BF16)
                keep[:, each] = context[:BLOCK]
                send[:, each] = context[BLOCK:]
            else:
                gathered_out, stats_out = refs
                gathered_out[head] = gathered
                stats_out[head, 0:1, :] = peak
                stats_out[head, 1:2, :] = total
        return 0

    if group == heads:
        some_heads(0, 0)
    else:
        lax.fori_loop(0, heads // group, some_heads, 0)


def attend(masks, few, first_row, queries, halves, near=None, begun=None, finish=True):
    rows, width = queries.shape
    heads = width // HEAD_SIZE
    operands = [*masks, queries]
    operands += [*near[0], *near[1]] if near else list(begun)
    columns = masks[0].shape[0] if near else 0
    for _, parts in halves:
        operands += parts
    far_bytes = sum(2 * part.size for _, parts in halves for part in parts)
    columns += far_bytes // (4 * width)
    if finish:
        out_shape = [shape((BLOCK, width))] * 2
    else:
        out_shape = [shape((heads, HEAD_SIZE, rows), F32), shape((heads, 8, rows), F32)]
    return pl.pallas_call(
        functools.partial(
            attend_kernel,
            first_row,
            near is not None,
            [(half, len(parts)) for half, parts in halves],
            few,
            finish,
        ),
        in_specs=[IN_VMEM] * len(operands),
        out_specs=[IN_VMEM] * 2,
        out_shape=out_shape,
        compiler_params=params(far_bytes),
        cost_estimate=cost(
            4 * rows * columns * width, 4 * rows * width, heads * rows * columns
        ),
    )(*operands)


def mix_kernel(more, rows, weight, *refs):
    out = refs[-1]
    tile = min(512, out.shape[1])
    for index in range(out.shape[1] // tile):
        part = slice(index * tile, (index + 1) * tile)
        total = dot(rows[...], weight[:, part])
        if more:
            total = total + refs[0][:, part]
        out[:, part] = total.astype(out.dtype)


def mix(rows, weight, dtype, begun=None):
    count, depth = rows.shape
    width = weight.shape[1]
    operands = [rows, weight] + ([begun] if begun is not None else [])
    return pl.pallas_call(
        functools.partial(mix_kernel, begun is not None),
        in_specs=[IN_VMEM] * len(operands),
        out_specs=IN_VMEM,
        out_shape=shape((count, width), dtype),
        compiler_params=params(),
        cost_estimate=cost(2 * count * depth * width, 4 * count * width),
    )(*operands)


def add_kernel(own, arriving, out, held, sems):
    rows = held.shape[0] // PARTS
    copies = []
    for index in range(PARTS):
        where = slice(index * rows, (index + 1) * rows)
        held[where, :] = (own[where, :] + arriving[where, :].astype(F32)).astype(BF16)
        copy = pltpu.make_async_copy(held.at[where, :], out.at[where, :], sems.at[index])
        copy.start()
        copies.append(copy)
    for copy in copies:
        copy.wait()


def add(own, arriving):
    return pl.pallas_call(
        add_kernel,
        in_specs=[IN_VMEM] * 2,
        out_specs=IN_HBM,
        out_shape=shape(arriving.shape),
        scratch_shapes=[pltpu.VMEM(arriving.shape, BF16), pltpu.SemaphoreType.DMA((PARTS,))],
        compiler_params=params(),
        cost_estimate=cost(own.size, 8 * own.size),
    )(own, arriving)


def shards(seqs, subs, normed, w_query, w_key, w_value, w_out, pattern, slide_lengths):
    slides = slide_lengths.shape[0]
    axes = [lax.axis_index(name).astype(jnp.int32)[None] for name in ("seq", "sub")]
    few = seqs == GROUP

    def swap(array, bit, axis="sub"):
        count = subs if axis == "sub" else seqs
        return lax.ppermute(array, axis, [(i, i ^ bit) for i in range(count)])

    def after(array, *others):
        return lax.optimization_barrier((array, *others))[0]

    def first_round(kept):
        return [swap(kept, bit, "seq") for bit in Z_BITS]

    def second_round(pieces):
        column = jnp.stack(pieces)
        return [column, swap(column, Y_BIT, "seq")]

    across = swap(normed, 2)
    beside = swap(normed, 1)
    mine, wk, wv, keys_0, values_0 = first(normed, w_key, w_value)
    keys_1, values_1, kept_a = second(beside, wk, wv, keys_0, values_0, pattern)
    place = jnp.concatenate([after(slide_lengths, kept_a), *axes])
    masks = list(make_masks(place, slides, subs, seqs, few))
    wo_beside = swap(w_out, 1)
    if few:
        along_z = first_round(kept_a)
        *along_z, masks[0] = lax.optimization_barrier((*along_z, masks[0]))
        half_a = 0, second_round([kept_a, *along_z])
        across = after(across, masks[0], wo_beside)
    else:
        half_a = 0, [lax.all_gather(kept_a, "seq", axis=0)]
    wo_beside = pltpu.with_memory_space_constraint(wo_beside, pltpu.VMEM)
    beyond = swap(across, 1)
    if few:
        beyond = after(beyond, half_a[1][0])
    keys_2, values_2 = keys_and_values(across, wk, wv)
    keys_3, values_3, kept_b = second(after(beyond, keys_2), wk, wv, keys_2, values_2, pattern)
    sent_later = again(kept_b)
    query_a, query_b, wo = query([after(mine, sent_later), beside, across, beyond], w_query, w_out)
    near = [keys_0, keys_1, keys_2, keys_3], [values_0, values_1, values_2, values_3]
    call = functools.partial(attend, masks, few)
    if few:
        along_z = first_round(kept_b)
        along_y = swap(sent_later, Y_BIT, "seq")
        diagonal = swap(sent_later, Z_BITS[-1] | Y_BIT, "seq")
        *along_z, along_y, diagonal, query_b, half_a[1][1] = lax.optimization_barrier(
            (*along_z, along_y, diagonal, query_b, half_a[1][1])
        )
        column, other = second_round(along_z[:-1])
        nearest = along_z[-1][None]
        half_b = 1, [kept_b[None], column, nearest, along_y[None], other, diagonal[None]]
        asked = after(query_b, column)
    else:
        half_b = 1, [lax.all_gather(kept_b, "seq", axis=0)]
        asked = query_b
    begun = call(2 * BLOCK, asked, [half_a], near=near, finish=False)
    keep_b, send_b = call(2 * BLOCK, query_b, [half_b], begun=begun)
    other_b = swap(send_b, 1)
    leaving = mix(other_b, wo_beside, BF16, mix(keep_b, wo, F32))
    arriving = swap(leaving, 2)
    query_a = after(query_a, leaving)
    keep_a, send_a = call(0, query_a, [half_a, half_b], near=near)
    other_a = swap(send_a, 1)
    own = mix(other_a, wo_beside, F32, mix(keep_a, wo, F32))
    return add(own, arriving)


def solution(mesh):
    placed = (
        P(("seq", "sub"), None),
        P(None, "sub"),
        P(None, "sub"),
        P(None, "sub"),
        P("sub", None),
        P("sub", None),
        P(),
    )
    return jax.shard_map(
        functools.partial(shards, mesh.shape["seq"], mesh.shape["sub"]),
        mesh=mesh,
        in_specs=placed,
        out_specs=P(("seq", "sub"), None),
        check_vma=False,
    )
```

```python
import functools
import math

import jax
import jax.numpy as jnp
from jax import lax
from jax.experimental import pallas as pl
from jax.experimental.pallas import tpu as pltpu
from jax.sharding import PartitionSpec as P

HEAD_SIZE = 128
BLOCK = 128
DILATED_KEPT = 16
BLOCKS_HALF = 2
FAR_ROWS = BLOCKS_HALF * DILATED_KEPT
GROUP = 8
STREAMS = 8
PARTS = 4
HIDDEN = -1e30
SCALE = math.log2(math.e) / math.sqrt(HEAD_SIZE)
BF16 = jnp.bfloat16
F32 = jnp.float32
IN_VMEM = pl.BlockSpec(memory_space=pltpu.VMEM)
IN_HBM = pl.BlockSpec(memory_space=pltpu.HBM)
IN_SMEM = pl.BlockSpec(memory_space=pltpu.SMEM)
Y_BIT = 1
Z_BITS = (4, 6, 2)


def dot(a, b):
    return jnp.dot(a, b, preferred_element_type=F32)


def dot_t(a, b):
    return lax.dot_general(a, b, (((1,), (1,)), ((), ())), preferred_element_type=F32)


def params(extra=0):
    return pltpu.CompilerParams(vmem_limit_bytes=16 * 2**20 + extra)


def cost(flops, bytes_accessed, transcendentals=0):
    return pl.CostEstimate(
        flops=flops // 100,
        bytes_accessed=bytes_accessed // 100,
        transcendentals=transcendentals // 100,
    )


def shape(dims, dtype=BF16):
    return jax.ShapeDtypeStruct(tuple(dims), dtype)


def keep_in_hbm(array):
    return pltpu.with_memory_space_constraint(array, pltpu.HBM)


def start_copies(source, target, sems, base):
    rows = source.shape[0] // STREAMS
    copies = []
    for index in range(STREAMS):
        where = slice(index * rows, (index + 1) * rows)
        copy = pltpu.make_async_copy(source.at[where, :], target.at[where, :], sems.at[base + index])
        copy.start()
        copies.append(copy)
    return copies


def halves_of(width):
    tile = min(256, width)
    return [slice(i * tile, (i + 1) * tile) for i in range(width // tile)]


def pick_dilated(pattern, blocks, kept):
    positions = lax.broadcasted_iota(jnp.int32, (BLOCK, BLOCK), 0)
    for head in range(kept.shape[1]):
        row = pattern[head : head + 1, :]
        chosen = (positions == row).astype(F32).T[:DILATED_KEPT].astype(BF16)
        for index, block in enumerate(blocks):
            picked = dot(chosen, jnp.concatenate(block(head), axis=1)).astype(BF16)
            spot = slice(index * DILATED_KEPT, (index + 1) * DILATED_KEPT)
            kept[0, head, spot, :] = picked[:, :HEAD_SIZE]
            kept[1, head, spot, :] = picked[:, HEAD_SIZE:]


def head_of(ref, head, rows=slice(None)):
    return ref[rows, head * HEAD_SIZE : (head + 1) * HEAD_SIZE]


def first_kernel(rows_hbm, wk_hbm, wv_hbm, rows, wk, wv, keys, values, sems):
    whole = pltpu.make_async_copy(rows_hbm, rows, sems.at[0])
    whole.start()
    key_copies = start_copies(wk_hbm, wk, sems, 1)
    value_copies = start_copies(wv_hbm, wv, sems, 1 + STREAMS)
    whole.wait()
    for copies, weight, out in ((key_copies, wk, keys), (value_copies, wv, values)):
        for copy in copies:
            copy.wait()
        for part in halves_of(wk.shape[1]):
            out[:, part] = dot(rows[...], weight[:, part]).astype(BF16)


def first(rows, w_key, w_value):
    count, depth = rows.shape
    width = w_key.shape[1]
    return pl.pallas_call(
        first_kernel,
        in_specs=[IN_HBM] * 3,
        out_specs=[IN_VMEM] * 5,
        out_shape=[
            pltpu.VMEM(rows.shape, BF16),
            pltpu.VMEM(w_key.shape, BF16),
            pltpu.VMEM(w_value.shape, BF16),
            shape((count, width)),
            shape((count, width)),
        ],
        scratch_shapes=[pltpu.SemaphoreType.DMA((1 + 2 * STREAMS,))],
        compiler_params=params(),
        cost_estimate=cost(4 * count * depth * width, 4 * depth * width),
    )(keep_in_hbm(rows), keep_in_hbm(w_key), keep_in_hbm(w_value))


def second_kernel(rows, wk, wv, keys_0, values_0, pattern, keys, values, kept):
    for part in halves_of(wk.shape[1]):
        keys[:, part] = dot(rows[...], wk[:, part]).astype(BF16)
        values[:, part] = dot(rows[...], wv[:, part]).astype(BF16)
    blocks = [
        lambda head: (head_of(keys_0, head), head_of(values_0, head)),
        lambda head: (head_of(keys, head), head_of(values, head)),
    ]
    pick_dilated(pattern, blocks, kept)


def second(rows, wk, wv, keys_0, values_0, pattern):
    count, depth = rows.shape
    width = wk.shape[1]
    kept = (2, width // HEAD_SIZE, FAR_ROWS, HEAD_SIZE)
    return pl.pallas_call(
        second_kernel,
        in_specs=[IN_VMEM] * 6,
        out_specs=[IN_VMEM] * 3,
        out_shape=[shape((count, width))] * 2 + [shape(kept)],
        compiler_params=params(),
        cost_estimate=cost(4 * count * depth * width, 2 * count * depth),
    )(rows, wk, wv, keys_0, values_0, pattern)


def query_kernel(*refs):
    rows, (wq_hbm, w_hbm), outs, (wq, sems) = refs[:4], refs[4:6], refs[6:9], refs[9:]
    copies = start_copies(wq_hbm, wq, sems, 0)
    more = start_copies(w_hbm, outs[2], sems, STREAMS)
    for copy in copies:
        copy.wait()
    for pair, out in ((rows[2:], outs[1]), (rows[:2], outs[0])):
        both = jnp.concatenate([ref[...] for ref in pair], axis=0)
        for part in halves_of(wq.shape[1]):
            out[:, part] = dot(both, wq[:, part]).astype(BF16)
    for copy in more:
        copy.wait()


def query(rows, w_query, w_out):
    count, depth = rows[0].shape
    width = w_query.shape[1]
    return pl.pallas_call(
        query_kernel,
        in_specs=[IN_VMEM] * 4 + [IN_HBM] * 2,
        out_specs=[IN_VMEM] * 3,
        out_shape=[shape((2 * count, width))] * 2 + [pltpu.VMEM(w_out.shape, BF16)],
        scratch_shapes=[
            pltpu.VMEM(w_query.shape, BF16),
            pltpu.SemaphoreType.DMA((2 * STREAMS,)),
        ],
        compiler_params=params(),
        cost_estimate=cost(8 * count * depth * width, 4 * depth * width),
    )(*rows, keep_in_hbm(w_query), keep_in_hbm(w_out))


def again_kernel(source, out):
    out[...] = source[...]


def again(kept):
    return pl.pallas_call(
        again_kernel,
        in_specs=[IN_VMEM],
        out_specs=IN_VMEM,
        out_shape=shape(kept.shape),
        compiler_params=params(),
        cost_estimate=cost(0, 4 * kept.size),
    )(kept)


def across_kernel(rows, wk, wv, keys, values):
    for part in halves_of(wk.shape[1]):
        keys[:, part] = dot(rows[...], wk[:, part]).astype(BF16)
        values[:, part] = dot(rows[...], wv[:, part]).astype(BF16)


def keys_and_values(rows, wk, wv):
    count, depth = rows.shape
    width = wk.shape[1]
    return pl.pallas_call(
        across_kernel,
        in_specs=[IN_VMEM] * 3,
        out_specs=[IN_VMEM] * 2,
        out_shape=[shape((count, width))] * 2,
        compiler_params=params(),
        cost_estimate=cost(4 * count * depth * width, 2 * count * depth),
    )(rows, wk, wv)


def slide_of(place, slides, block):
    end, total = jnp.int32(0), jnp.zeros_like(block)
    for index in range(slides):
        end = end + place[index]
        total = total + (block >= end).astype(jnp.int32)
    return total


def mask_kernel(slides, subs, spans, few, place, asking, asked):
    span, sub = place[slides], place[slides + 1]
    slide = [slide_of(place, slides, span * subs + (sub ^ r)) for r in range(subs)]
    lane = lax.broadcasted_iota(jnp.int32, (BLOCK, HEAD_SIZE), 1)
    for r in range(subs):
        rows = slice(r * BLOCK, (r + 1) * BLOCK)
        apart = (lane <= slides) & (lane != slide[r])
        asking[rows, :] = jnp.where(apart, HIDDEN, 0.0).astype(BF16)
        asked[rows, :] = jnp.where(lane == slide[r], 1.0, 0.0).astype(BF16)
    count = min(spans, GROUP) * FAR_ROWS
    row = lax.broadcasted_iota(jnp.int32, (count, HEAD_SIZE), 0)
    lane = lax.broadcasted_iota(jnp.int32, (count, HEAD_SIZE), 1)
    upper = (row // DILATED_KEPT) % BLOCKS_HALF
    for half in range(subs // BLOCKS_HALF):
        place_0, place_1 = sub ^ (half * BLOCKS_HALF), sub ^ (half * BLOCKS_HALF + 1)
        for group in range(spans * FAR_ROWS // count):
            far = row // FAR_ROWS
            if few:
                order = [bit | y for y in (0, Y_BIT) for bit in (0, *Z_BITS)]
                place_of = jnp.zeros_like(far)
                for index, bits in enumerate(order):
                    place_of = jnp.where(far == index, bits, place_of)
                far = place_of ^ span
            else:
                far = far + group * GROUP
            theirs = slide_of(place, slides, far * subs + jnp.where(upper == 0, place_0, place_1))
            marked = (lane == theirs) | ((lane == slides) & (far == span))
            start = subs * BLOCK + (half * spans * FAR_ROWS + group * count)
            asked[start : start + count, :] = jnp.where(marked, 1.0, 0.0).astype(BF16)


def make_masks(place, slides, subs, spans, few):
    keys = subs * BLOCK + subs // BLOCKS_HALF * spans * FAR_ROWS
    return pl.pallas_call(
        functools.partial(mask_kernel, slides, subs, spans, few),
        in_specs=[IN_SMEM],
        out_specs=[IN_VMEM] * 2,
        out_shape=[shape((subs * BLOCK, HEAD_SIZE)), shape((keys, HEAD_SIZE))],
        compiler_params=params(),
        cost_estimate=cost(64 * keys * HEAD_SIZE, 2 * keys * HEAD_SIZE),
    )(place)


def scores_of(keys, queries):
    return dot_t(keys, queries)


def gather(values, weight):
    return lax.dot_general(
        values, weight.astype(BF16), (((0,), (0,)), ((), ())), preferred_element_type=F32
    )


def begin(queries, keys, values):
    scores = [scores_of(k, q) for k, q in zip(keys, queries)]
    peak = [jnp.max(each, axis=0, keepdims=True) for each in scores]
    weight = [jnp.exp2((each - top) * SCALE) for each, top in zip(scores, peak)]
    total = [jnp.sum(each, axis=0, keepdims=True) for each in weight]
    return peak, total, [gather(v, each) for v, each in zip(values, weight)]


def update(queries, keys, values, state):
    scores = [scores_of(k, q) for k, q in zip(keys, queries)]
    higher = [
        jnp.maximum(top, jnp.max(each, axis=0, keepdims=True))
        for top, each in zip(state[0], scores)
    ]
    shrink = [jnp.exp2((top - new) * SCALE) for top, new in zip(state[0], higher)]
    weight = [jnp.exp2((each - new) * SCALE) for each, new in zip(scores, higher)]
    total = [
        old * less + jnp.sum(each, axis=0, keepdims=True)
        for old, less, each in zip(state[1], shrink, weight)
    ]
    added = [gather(v, each) for v, each in zip(values, weight)]
    return higher, total, [old * less + new for old, less, new in zip(state[2], shrink, added)]


def attend_kernel(first_row, near, halves, few, finish, asking, asked_of, *refs):
    refs = list(refs)
    queries = refs.pop(0)
    if near:
        keys, values = refs[0:4], refs[4:8]
        del refs[:8]
    else:
        gathered_in, stats_in = refs[0:2]
        del refs[:2]
    far = []
    for half, size in halves:
        far.append((half, refs[:size]))
        del refs[:size]
    rows = queries.shape[0]
    span = asking.shape[0]
    half_count = (asked_of.shape[0] - span) // BLOCKS_HALF

    heads = queries.shape[1] // HEAD_SIZE
    group = 1 if not few else heads

    def some_heads(turn, _):
        those = [turn * group + i for i in range(group)]
        columns = [
            pl.ds(pl.multiple_of(head * HEAD_SIZE, HEAD_SIZE), HEAD_SIZE)
            if group < heads
            else slice(head * HEAD_SIZE, (head + 1) * HEAD_SIZE)
            for head in those
        ]
        row_marks = asking[first_row : first_row + rows, :]
        asked = [jnp.concatenate([queries[:, each], row_marks], axis=1) for each in columns]

        def marked(parts, where):
            return jnp.concatenate([jnp.concatenate(parts, axis=0), asked_of[where, :]], axis=1)

        def ready(head, each):
            keyed, valued = [], []
            if near:
                keyed.append(marked([ref[:, each] for ref in keys], slice(0, span)))
                valued += [ref[:, each] for ref in values]
            if few:
                for half, parts in far:
                    start = span + half * half_count
                    pieces = [(ref, i) for ref in parts for i in range(ref.shape[0])]
                    where = slice(start, start + half_count)
                    keyed.append(marked([ref[i, 0, head] for ref, i in pieces], where))
                    valued += [ref[i, 1, head] for ref, i in pieces]
            return jnp.concatenate(keyed, axis=0), jnp.concatenate(valued, axis=0)

        if near:
            state = begin(asked, *zip(*map(ready, those, columns)))
        else:
            state = (
                [stats_in[head, 0:1, :] for head in those],
                [stats_in[head, 1:2, :] for head in those],
                [gathered_in[head] for head in those],
            )
            if few:
                state = update(asked, *zip(*map(ready, those, columns)), state)
        if not few:
            for half, (part,) in far:
                start = span + half * half_count

                def step(number, state, start=start, part=part):
                    base = number * GROUP
                    width = GROUP * FAR_ROWS
                    where = pl.ds(pl.multiple_of(start + number * width, width), width)
                    found = [
                        [
                            marked([part[base + i, 0, head] for i in range(GROUP)], where)
                            for head in those
                        ],
                        [
                            jnp.concatenate([part[base + i, 1, head] for i in range(GROUP)], axis=0)
                            for head in those
                        ],
                    ]
                    return update(asked, *found, state)

                state = lax.fori_loop(0, part.shape[0] // GROUP, step, state)
        for head, each, peak, total, gathered in zip(those, columns, *state):
            if finish:
                keep, send = refs
                context = (gathered / total).T.astype(BF16)
                keep[:, each] = context[:BLOCK]
                send[:, each] = context[BLOCK:]
            else:
                gathered_out, stats_out = refs
                gathered_out[head] = gathered
                stats_out[head, 0:1, :] = peak
                stats_out[head, 1:2, :] = total
        return 0

    if group == heads:
        some_heads(0, 0)
    else:
        lax.fori_loop(0, heads // group, some_heads, 0)


def attend(masks, few, first_row, queries, halves, near=None, begun=None, finish=True):
    rows, width = queries.shape
    heads = width // HEAD_SIZE
    operands = [*masks, queries]
    operands += [*near[0], *near[1]] if near else list(begun)
    columns = masks[0].shape[0] if near else 0
    for _, parts in halves:
        operands += parts
    far_bytes = sum(2 * part.size for _, parts in halves for part in parts)
    columns += far_bytes // (4 * width)
    if finish:
        out_shape = [shape((BLOCK, width))] * 2
    else:
        out_shape = [shape((heads, HEAD_SIZE, rows), F32), shape((heads, 8, rows), F32)]
    return pl.pallas_call(
        functools.partial(
            attend_kernel,
            first_row,
            near is not None,
            [(half, len(parts)) for half, parts in halves],
            few,
            finish,
        ),
        in_specs=[IN_VMEM] * len(operands),
        out_specs=[IN_VMEM] * 2,
        out_shape=out_shape,
        compiler_params=params(far_bytes),
        cost_estimate=cost(
            4 * rows * columns * width, 4 * rows * width, heads * rows * columns
        ),
    )(*operands)


def mix_kernel(more, rows, weight, *refs):
    out = refs[-1]
    tile = min(512, out.shape[1])
    for index in range(out.shape[1] // tile):
        part = slice(index * tile, (index + 1) * tile)
        total = dot(rows[...], weight[:, part])
        if more:
            total = total + refs[0][:, part]
        out[:, part] = total.astype(out.dtype)


def mix(rows, weight, dtype, begun=None):
    count, depth = rows.shape
    width = weight.shape[1]
    operands = [rows, weight] + ([begun] if begun is not None else [])
    return pl.pallas_call(
        functools.partial(mix_kernel, begun is not None),
        in_specs=[IN_VMEM] * len(operands),
        out_specs=IN_VMEM,
        out_shape=shape((count, width), dtype),
        compiler_params=params(),
        cost_estimate=cost(2 * count * depth * width, 4 * count * width),
    )(*operands)


def add_kernel(own, arriving, out, held, sems):
    rows = held.shape[0] // PARTS
    copies = []
    for index in range(PARTS):
        where = slice(index * rows, (index + 1) * rows)
        held[where, :] = (own[where, :] + arriving[where, :].astype(F32)).astype(BF16)
        copy = pltpu.make_async_copy(held.at[where, :], out.at[where, :], sems.at[index])
        copy.start()
        copies.append(copy)
    for copy in copies:
        copy.wait()


def add(own, arriving):
    return pl.pallas_call(
        add_kernel,
        in_specs=[IN_VMEM] * 2,
        out_specs=IN_HBM,
        out_shape=shape(arriving.shape),
        scratch_shapes=[pltpu.VMEM(arriving.shape, BF16), pltpu.SemaphoreType.DMA((PARTS,))],
        compiler_params=params(),
        cost_estimate=cost(own.size, 8 * own.size),
    )(own, arriving)


def shards(seqs, subs, normed, w_query, w_key, w_value, w_out, pattern, slide_lengths):
    slides = slide_lengths.shape[0]
    axes = [lax.axis_index(name).astype(jnp.int32)[None] for name in ("seq", "sub")]
    few = seqs == GROUP

    def swap(array, bit, axis="sub"):
        count = subs if axis == "sub" else seqs
        return lax.ppermute(array, axis, [(i, i ^ bit) for i in range(count)])

    def after(array, *others):
        return lax.optimization_barrier((array, *others))[0]

    def first_round(kept):
        return [swap(kept, bit, "seq") for bit in Z_BITS]

    def second_round(pieces):
        column = jnp.stack(pieces)
        return [column, swap(column, Y_BIT, "seq")]

    across = swap(normed, 2)
    beside = swap(normed, 1)
    mine, wk, wv, keys_0, values_0 = first(normed, w_key, w_value)
    keys_1, values_1, kept_a = second(beside, wk, wv, keys_0, values_0, pattern)
    place = jnp.concatenate([after(slide_lengths, kept_a), *axes])
    masks = list(make_masks(place, slides, subs, seqs, few))
    wo_beside = swap(w_out, 1)
    if few:
        along_z = first_round(kept_a)
        *along_z, masks[0] = lax.optimization_barrier((*along_z, masks[0]))
        half_a = 0, second_round([kept_a, *along_z])
        across = after(across, masks[0], wo_beside)
    else:
        half_a = 0, [lax.all_gather(kept_a, "seq", axis=0)]
    wo_beside = pltpu.with_memory_space_constraint(wo_beside, pltpu.VMEM)
    beyond = swap(across, 1)
    if few:
        beyond = after(beyond, half_a[1][0])
    keys_2, values_2 = keys_and_values(across, wk, wv)
    keys_3, values_3, kept_b = second(after(beyond, keys_2), wk, wv, keys_2, values_2, pattern)
    sent_later = again(kept_b)
    near = [keys_0, keys_1, keys_2, keys_3], [values_0, values_1, values_2, values_3]
    call = functools.partial(attend, masks, few)
    if few:
        along_z = first_round(kept_b)
        along_y = swap(sent_later, Y_BIT, "seq")
        diagonal = swap(sent_later, Z_BITS[-1] | Y_BIT, "seq")
        *along_z, along_y, diagonal, half_a[1][1] = lax.optimization_barrier(
            (*along_z, along_y, diagonal, half_a[1][1])
        )
        column, other = second_round(along_z[:-1])
        nearest = along_z[-1][None]
        half_b = 1, [kept_b[None], column, nearest, along_y[None], other, diagonal[None]]
        mine = after(mine, column)
    else:
        half_b = 1, [lax.all_gather(kept_b, "seq", axis=0)]
    query_a, query_b, wo = query([mine, beside, across, beyond], w_query, w_out)
    begun = call(2 * BLOCK, query_b, [half_a], near=near, finish=False)
    keep_b, send_b = call(2 * BLOCK, query_b, [half_b], begun=begun)
    other_b = swap(send_b, 1)
    leaving = mix(other_b, wo_beside, BF16, mix(keep_b, wo, F32))
    arriving = swap(leaving, 2)
    query_a = after(query_a, leaving)
    keep_a, send_a = call(0, query_a, [half_a, half_b], near=near)
    other_a = swap(send_a, 1)
    own = mix(other_a, wo_beside, F32, mix(keep_a, wo, F32))
    return add(own, arriving)


def solution(mesh):
    placed = (
        P(("seq", "sub"), None),
        P(None, "sub"),
        P(None, "sub"),
        P(None, "sub"),
        P("sub", None),
        P("sub", None),
        P(),
    )
    return jax.shard_map(
        functools.partial(shards, mesh.shape["seq"], mesh.shape["sub"]),
        mesh=mesh,
        in_specs=placed,
        out_specs=P(("seq", "sub"), None),
        check_vma=False,
    )
```
